32 devices in a mesh: dom: 8 (over y, x, core), pair: 4 (over z).
Axes of the slice: x: 2, y: 2, z: 4, core: 2. Of those that a mesh axis runs over, the one named last changes fastest.
Arguments:
- occupied: bfloat16 [12, 32, 256, 128], P(None, 'dom'), may hold values from -6 to 6
- virtual: bfloat16 [12, 32, 256, 128], P(None, 'dom'), may hold values from -6 to 6
- pair_ids: int32 [16, 2], P('pair'), may hold values from 0 to 11
Outputs:
- potentials: bfloat16 [16, 32, 256, 128], P('pair', 'dom')
- panel: float32 [16, 16], P('dom', 'pair')
The draws below stay inside these ranges and needn't reach their ends.
Inputs may be any that keep to these rules, and one draw needn't show every extreme that they name: `pair_ids`: each row holds an occupied orbital's index and a virtual orbital's index.
All inputs are finite; a program needn't handle non-finite values.
Results may differ from the reference program's by a relative error of at most 0.001.
Values may be sent and summed in bfloat16 or wider, within the bound.
No kernel may reach another device: no remote copies, remote signals or barrier semaphores. Data moves between devices by JAX's collectives and lax.ppermute only.
A program may use at most 128 MiB of HBM per device.

```python
import math
import jax
import jax.numpy as jnp
from jax import lax

NY = 256
NZ = 128
PAIR_DEV = 4
ORBS = 12
NX = 32
NPAIR = 16
CELLS = 1048576
N_PAIR = 4


def orbital_field(key, count):
    keys = jax.random.split(key, 6)
    xs = jnp.arange(NX, dtype=jnp.float32)[None, :, None, None]
    ys = jnp.arange(NY, dtype=jnp.float32)[None, None, :, None]
    zs = jnp.arange(NZ, dtype=jnp.float32)[None, None, None, :]
    waves = jax.random.uniform(keys[0], (count, 3), minval=0.15, maxval=0.6)
    turns = jnp.where(jax.random.bernoulli(keys[1], 0.5, (count, 3)), 1.0, -1.0)
    rates = waves * turns
    phase = jax.random.uniform(keys[2], (count,), minval=-math.pi, maxval=math.pi)
    angle = rates[:, 0, None, None, None] * xs + rates[:, 1, None, None, None] * ys
    angle = angle + rates[:, 2, None, None, None] * zs + phase[:, None, None, None]
    amplitude = jax.random.uniform(keys[3], (count,), minval=0.6, maxval=1.4)
    noise = 0.7 * jax.random.truncated_normal(keys[5], -4.0, 4.0, (count, NX, NY, NZ))
    field = amplitude[:, None, None, None] * jnp.cos(angle) + noise
    return field.astype(jnp.float32).astype(jnp.bfloat16)


def draw_occupied(key, part):
    return orbital_field(jax.random.fold_in(key, 11), ORBS)


def draw_virtual(key, part):
    return orbital_field(jax.random.fold_in(key, 23), ORBS)


def touch_ends(array, own_key, smallest, largest):
    shape = array.shape
    index_at = [jax.random.randint(jax.random.fold_in(own_key, axis), (), 0, shape[axis]) for axis in range(len(shape))]
    array = array.at[tuple(index_at)].set(smallest)
    longest = shape.index(max(shape))
    index_at[longest] = (index_at[longest] + 1) % shape[longest]
    return array.at[tuple(index_at)].set(largest)


def setup_inputs(seed: int = 0) -> dict:
    arg_keys = jax.random.split(jax.random.key(seed), 4)
    return {
        "occupied": draw_occupied(jax.random.fold_in(arg_keys[3], 71), 0),
        "virtual": draw_virtual(jax.random.fold_in(arg_keys[3], 71), 0),
        "pair_ids": touch_ends(jax.random.randint(arg_keys[2], (NPAIR, 2), 0, ORBS), jax.random.fold_in(arg_keys[2], 1), 0, ORBS - 1).astype(jnp.int32),
    }


relax_step = 0.8 / 6.0
highest = lax.Precision.HIGHEST

def operate(field):
    padded = jnp.pad(field, ((0, 0), (1, 1), (1, 1), (1, 1)))
    beside = padded[:, 2:, 1:-1, 1:-1] + padded[:, :-2, 1:-1, 1:-1]
    beside = beside + padded[:, 1:-1, 2:, 1:-1] + padded[:, 1:-1, :-2, 1:-1]
    beside = beside + padded[:, 1:-1, 1:-1, 2:] + padded[:, 1:-1, 1:-1, :-2]
    return 6.0 * field - beside

def smooth(field, source):
    return field + relax_step * (source - operate(field))

def restrict(field):
    count, sx, sy, sz = field.shape
    blocks = field.reshape(count, sx // 2, 2, sy // 2, 2, sz // 2, 2)
    return 0.5 * lax.optimization_barrier(jnp.sum(blocks, axis=(2, 4, 6)))

def prolong(field):
    count, sx, sy, sz = field.shape
    spread = jnp.broadcast_to(field[:, :, None, :, None, :, None], (count, sx, 2, sy, 2, sz, 2))
    return spread.reshape(count, 2 * sx, 2 * sy, 2 * sz)

def sine_table(length):
    steps = jnp.arange(length, dtype=jnp.float32) + 1.0
    return math.sqrt(2.0 / (length + 1)) * jnp.sin(math.pi * steps[:, None] * steps[None, :] / (length + 1))

def mode_diagonal(length_y, length_z):
    lam_y = 2.0 - 2.0 * jnp.cos(math.pi * (jnp.arange(length_y, dtype=jnp.float32) + 1.0) / (length_y + 1))
    lam_z = 2.0 - 2.0 * jnp.cos(math.pi * (jnp.arange(length_z, dtype=jnp.float32) + 1.0) / (length_z + 1))
    return (2.0 + lam_y[:, None] + lam_z[None, :]).reshape(length_y * length_z)

def solve_lines(right_side, diagonal):
    systems = jnp.transpose(right_side, (2, 1, 0))
    count = systems.shape[1]
    main = jnp.broadcast_to(diagonal[:, None], systems.shape[:2])
    position = jnp.arange(count, dtype=jnp.int32)
    lower = jnp.broadcast_to(jnp.where(position == 0, 0.0, -1.0).astype(jnp.float32), main.shape)
    upper = jnp.broadcast_to(jnp.where(position == count - 1, 0.0, -1.0).astype(jnp.float32), main.shape)
    solved = lax.linalg.tridiagonal_solve(lower, main, upper, systems)
    return jnp.transpose(solved, (2, 1, 0))

def coarse_solve(source):
    count, sx, sy, sz = source.shape
    table_y = sine_table(sy)
    table_z = sine_table(sz)
    spectral = jnp.einsum('pxyz,ky,lz->pxkl', source, table_y, table_z, precision=highest)
    solved = solve_lines(spectral.reshape(count, sx, sy * sz), mode_diagonal(sy, sz))
    solved = solved.reshape(count, sx, sy, sz)
    return jnp.einsum('pxkl,ky,lz->pxyz', solved, table_y, table_z, precision=highest)

def vcycle(source):
    fine = smooth(relax_step * source, source)
    middle_source = restrict(source - operate(fine))
    middle = smooth(relax_step * middle_source, middle_source)
    coarse_source = restrict(middle_source - operate(middle))
    coarse = coarse_solve(coarse_source)
    middle = smooth(smooth(middle + prolong(coarse), middle_source), middle_source)
    fine = smooth(smooth(fine + prolong(middle), source), source)
    return fine

def reference(occupied, virtual, pair_ids):
    pair_groups = pair_ids.reshape(N_PAIR, PAIR_DEV, 2)

    def density(pair_rows):
        left = jnp.take(occupied, pair_rows[:, 0], axis=0).astype(jnp.float32)
        right = jnp.take(virtual, pair_rows[:, 1], axis=0).astype(jnp.float32)
        return left * right
    potentials = lax.map(lambda pair_rows: vcycle(density(pair_rows)).astype(jnp.bfloat16), pair_groups)
    potentials = potentials.reshape(NPAIR, NX, NY, NZ)
    flat = potentials.reshape(NPAIR, NX * NY * NZ)

    def panel_rows(pair_rows):
        rho_half = density(pair_rows).astype(jnp.bfloat16).reshape(PAIR_DEV, NX * NY * NZ)
        return lax.dot_general(rho_half.astype(jnp.float32), flat.astype(jnp.float32), (((1,), (1,)), ((), ())), preferred_element_type=jnp.float32)
    panel = lax.map(panel_rows, pair_groups).reshape(NPAIR, NPAIR) / float(CELLS)
    return (potentials, panel)
```

```python
import functools
import math

import jax
import jax.numpy as jnp
import numpy as np
from jax import lax
from jax.experimental import pallas as pl
from jax.experimental.pallas import tpu as pltpu
from jax.sharding import PartitionSpec as P

W = 0.8 / 6.0
C = 0.2
PAD = 8
F32 = jnp.float32
BF16 = jnp.bfloat16


def dot(a, b, contract=((1,), (0,)), precision=None):
    return lax.dot_general(a, b, (contract, ((), ())), precision=precision, preferred_element_type=F32)


def high_low(x):
    high = x.astype(BF16)
    return high, (x - high.astype(F32)).astype(BF16)


def zero_rims(ref):
    zeros = jnp.zeros((ref.shape[0], PAD, ref.shape[2]), F32)
    ref[:, :PAD] = zeros
    ref[:, ref.shape[1] - PAD :] = zeros


def read(ref, layer, row, rows):
    return ref[layer, PAD + row : PAD + row + rows, :]


def around(ref, layer, row, rows, centre, blocks=1):
    lane = lax.broadcasted_iota(jnp.int32, centre.shape, 1)
    width = centre.shape[1] // blocks
    first = lane % width == 0 if blocks > 1 else lane == 0
    last = lane % width == width - 1 if blocks > 1 else lane == width - 1
    total = read(ref, layer, row - 1, rows) + read(ref, layer, row + 1, rows)
    total = total + jnp.where(first, 0.0, pltpu.roll(centre, 1, 1))
    return total + jnp.where(last, 0.0, pltpu.roll(centre, centre.shape[1] - 1, 1))


def source_kernel(ids, place, occ, vir, fold, shares, first, second, v0_out, field, once, sums):
    slab, rows_y, _ = occ.shape[1:]
    step = 64
    in_left = jnp.where(place[0] == 0, 0.0, 1.0)
    in_right = jnp.where(place[1] == 0, 0.0, 1.0)
    even = place[2] == 0
    zero_rims(field)
    zero_rims(once)
    for layer in range(slab):
        field[layer, PAD : PAD + rows_y] = occ[0, layer].astype(F32) * vir[0, layer].astype(F32)

    def pack_out(edge, index, row, value):
        rows = slice(row, row + step)
        value = value.astype(BF16)

        @pl.when(even == (edge == 1))
        def _():
            first[0, index, rows] = value

        @pl.when(even != (edge == 1))
        def _():
            second[0, index, rows] = value

    for row in range(0, rows_y, step):
        for layer in range(slab):
            centre = read(field, layer, row, step)
            total = around(field, layer, row, step, centre)
            if layer > 0:
                total = total + read(field, layer - 1, row, step)
            if layer < slab - 1:
                total = total + read(field, layer + 1, row, step)
            value = C * centre + W * total
            once[layer + 1, PAD + row : PAD + row + step] = value
            v0 = W * (centre + value)
            v0_out[0, layer, row : row + step] = v0
            if layer == 0:
                once[0, PAD + row : PAD + row + step] = (W * in_left) * centre
                pack_out(0, 0, row, centre)
                pack_out(0, 1, row, v0)
            if layer == 1:
                pack_out(0, 2, row, v0)
            if layer == slab - 2:
                pack_out(1, 2, row, v0)
            if layer == slab - 1:
                once[slab + 1, PAD + row : PAD + row + step] = (W * in_right) * centre
                pack_out(1, 0, row, centre)
                pack_out(1, 1, row, v0)

    def twice(layer, row):
        if layer == -2:
            return W * read(once, 0, row, step)
        if layer == slab + 1:
            return W * read(once, slab + 1, row, step)
        at = layer + 1
        centre = read(once, at, row, step)
        total = around(once, at, row, step, centre)
        if at > 0:
            total = total + read(once, at - 1, row, step)
        if at < slab + 1:
            total = total + read(once, at + 1, row, step)
        return C * centre + W * total

    for row in range(0, rows_y, step):
        for coarse in range(slab // 2 + 2):
            pair_sum = twice(2 * coarse - 2, row) + twice(2 * coarse - 1, row)
            sums[coarse, row : row + step] = pair_sum

    def folded(coarse):
        half = rows_y // 2
        return sums[coarse, pl.ds(0, half, stride=2), :] + sums[coarse, pl.ds(1, half, stride=2), :]

    def together(left, right):
        both = jnp.concatenate([folded(left), folded(right)], axis=1)
        high, low = high_low(both)
        return dot(high, fold[...]) + dot(low, fold[...])

    own_high, own_low = high_low(together(1, 2))
    edge = together(3, 0).astype(BF16)
    parts, part_rows = shares.shape[1], shares.shape[3]
    for part in range(parts):
        rows = slice(part * part_rows, (part + 1) * part_rows)
        shares[0, part, 0] = own_high[rows]
        shares[0, part, 1] = own_low[rows]
        shares[0, part, 2] = edge[rows]


def middle_kernel(place, *refs):
    parts = (len(refs) - 10)
    received = refs[:parts]
    modes, table_y, inverse, back, out, source, field_a, field_b, smooth, edge = refs[parts:]
    slabs, _, part_rows, lanes = received[0].shape
    rows_y = parts * part_rows
    own_part = place[3]
    left = lax.broadcasted_iota(jnp.int32, (part_rows, lanes), 1) < lanes // 2
    for ref in (source, field_a, field_b):
        zero_rims(ref)
    for turn in range(parts):
        at = own_part + turn
        at = jnp.where(at >= parts, at - parts, at) * part_rows
        at = pl.multiple_of(at, part_rows)
        ref = received[turn]
        for d in range(slabs):
            value = ref[d, 0].astype(F32) + ref[d, 1].astype(F32)
            before = ref[d - 1, 2].astype(F32) if d > 0 else jnp.zeros_like(value)
            after = ref[d + 1, 2].astype(F32) if d < slabs - 1 else jnp.zeros_like(value)
            source[d, pl.ds(PAD + at, part_rows)] = value + jnp.where(left, before, after)

    half = lanes // 2
    left = lax.broadcasted_iota(jnp.int32, (rows_y, lanes), 1) < half

    def swapped(ref, d):
        return pltpu.roll(read(ref, d, 0, rows_y), half, 1)

    def apply(ref, each):
        zeros = jnp.zeros((rows_y, lanes), F32)
        before, here = zeros, swapped(ref, 0)
        for d in range(slabs):
            after = swapped(ref, d + 1) if d < slabs - 1 else zeros
            centre = read(ref, d, 0, rows_y)
            total = around(ref, d, 0, rows_y, centre, 2) + here + jnp.where(left, before, after)
            each(d, C * centre + W * total)
            before, here = here, after

    def write(ref, d, value):
        ref[d, PAD : PAD + rows_y] = value

    apply(source, lambda d, value: write(field_a, d, value))

    def to_coarse(d, value):
        smooth[d] = W * (read(source, d, 0, rows_y) + read(field_a, d, 0, rows_y))
        write(field_b, d, value)

    apply(field_a, to_coarse)
    highest = lax.Precision.HIGHEST
    pieces = []
    for d in range(slabs):
        even_rows = field_b[d, pl.ds(PAD, rows_y // 2, stride=2), :]
        odd_rows = field_b[d, pl.ds(PAD + 1, rows_y // 2, stride=2), :]
        pieces.append(even_rows + odd_rows)
    spectral = dot(jnp.concatenate(pieces, axis=1), modes[...], precision=highest)
    spectral = dot(table_y[...], spectral, precision=highest) * inverse[...]
    spread = dot(dot(table_y[...], spectral, precision=highest), back[...], precision=highest)
    for d in range(slabs):
        value = spread[:, d * lanes : (d + 1) * lanes]
        field_b[d, pl.ds(PAD, rows_y // 2, stride=2), :] = value
        field_b[d, pl.ds(PAD + 1, rows_y // 2, stride=2), :] = value
    for d in range(slabs):
        write(field_a, d, smooth[d] + read(field_b, d, 0, rows_y))

    def add_source(ref):
        return lambda d, value: write(ref, d, value + W * read(source, d, 0, rows_y))

    apply(field_a, add_source(field_b))
    apply(field_b, add_source(field_a))
    zeros = jnp.zeros((rows_y, lanes), F32)
    before, here = zeros, swapped(field_a, 0)
    for d in range(slabs):
        after = swapped(field_a, d + 1) if d < slabs - 1 else zeros
        edge[d] = jnp.where(left, before, after) - read(field_a, d, 0, rows_y)
        before, here = here, after
    at = pl.multiple_of(own_part * part_rows, part_rows)
    for d in range(slabs):
        high, low = high_low(field_a[d, pl.ds(PAD + at, part_rows)])
        out[d, 0] = high
        out[d, 1] = low
        out[d, 2] = edge[d, pl.ds(at, part_rows)].astype(BF16)


def final_kernel(
    own_ids, ids, place, occ, vir, v0, coarse, first, second, spread, all_occ, all_vir,
    out, panel, wide, start, swept, kept, occ_copy, vir_copy, sems,
):
    slab, rows_y, lanes = occ.shape[1:]
    pair, pairs = pl.program_id(0), kept.shape[1]
    step = 64
    in_left = jnp.where(place[0] == 0, 0.0, 1.0)
    in_right = jnp.where(place[1] == 0, 0.0, 1.0)
    even = place[2] == 0
    copies = [
        pltpu.make_async_copy(all_occ, occ_copy, sems.at[0]),
        pltpu.make_async_copy(all_vir, vir_copy, sems.at[1]),
    ]

    @pl.when(pair == 0)
    def _():
        for copy in copies:
            copy.start()

    zero_rims(start)
    zero_rims(swept)
    parts, part_rows = coarse.shape[1], coarse.shape[3]
    for part in range(parts):
        table = spread[...]
        own = dot(coarse[0, part, 0], table) + dot(coarse[0, part, 1], table)
        beyond = own + dot(coarse[0, part, 2], table)
        for at, value in enumerate((beyond[:, :lanes], own[:, :lanes], own[:, lanes:], beyond[:, lanes:])):
            rows = 2 * part * part_rows
            wide[at, pl.ds(rows, part_rows, stride=2), :] = value
            wide[at, pl.ds(rows + 1, part_rows, stride=2), :] = value

    def halo(edge, index, row):
        rows = slice(row, row + step)
        one, two = first[0, index, rows].astype(F32), second[0, index, rows].astype(F32)
        return jnp.where(even == (edge == 1), one, two)

    def density(layer, row):
        rows = slice(row, row + step)
        return occ[0, layer, rows].astype(F32) * vir[0, layer, rows].astype(F32)

    def put(ref, layer, row, value):
        ref[layer, PAD + row : PAD + row + step] = value

    for row in range(0, rows_y, step):
        rows = slice(row, row + step)
        for layer in range(slab):
            value = v0[0, layer, rows] + wide[1 + layer // 2, rows]
            if layer == 0:
                value = value + (W * W) * halo(0, 0, row)
            if layer == slab - 1:
                value = value + (W * W) * halo(1, 0, row)
            put(start, layer + 2, row, value)
        near = halo(0, 1, row) + (W * W) * density(0, row) + wide[0, rows]
        put(start, 1, row, in_left * near)
        put(start, 0, row, in_left * (halo(0, 2, row) + wide[0, rows]))
        near = halo(1, 1, row) + (W * W) * density(slab - 1, row) + wide[3, rows]
        put(start, slab + 2, row, in_right * near)
        put(start, slab + 3, row, in_right * (halo(1, 2, row) + wide[3, rows]))

    def sweep(ref, at, row, source):
        centre = read(ref, at, row, step)
        total = around(ref, at, row, step, centre)
        total = total + read(ref, at - 1, row, step) + read(ref, at + 1, row, step) + source
        return C * centre + W * total

    for row in range(0, rows_y, step):
        put(swept, 0, row, in_left * sweep(start, 1, row, halo(0, 0, row)))
        for layer in range(slab):
            put(swept, layer + 1, row, sweep(start, layer + 2, row, density(layer, row)))
        put(swept, slab + 1, row, in_right * sweep(start, slab + 2, row, halo(1, 0, row)))
    for row in range(0, rows_y, step):
        rows = slice(row, row + step)
        for layer in range(slab):
            value = sweep(swept, layer + 1, row, density(layer, row)).astype(BF16)
            out[0, layer, rows] = value
            kept[layer, pair, rows] = value

    @pl.when(pair == pairs - 1)
    def _():
        for copy in copies:
            copy.wait()
        lane = lax.broadcasted_iota(jnp.int32, (lanes, lanes), 0)
        diagonal = lane == lax.broadcasted_iota(jnp.int32, (lanes, lanes), 1)
        count = ids.shape[0]
        fields = [jnp.concatenate([kept[layer, q] for q in range(pairs)], axis=1) for layer in range(slab)]
        for p in range(count):
            i, a = ids[p, 0], ids[p, 1]
            row = place[4] + p
            row = jnp.where(row >= count, row - count, row)
            product = jnp.zeros((pairs * lanes, lanes), F32)
            for layer in range(slab):
                rho = (occ_copy[i, layer].astype(F32) * vir_copy[a, layer].astype(F32)).astype(BF16)
                product = product + dot(fields[layer], rho, ((0,), (0,)))
            for q in range(pairs):
                block = jnp.where(diagonal, product[q * lanes : (q + 1) * lanes], 0.0)
                panel[row, q : q + 1, :] = jnp.sum(block, axis=0, keepdims=True)


def sine_table(length):
    steps = np.arange(length, dtype=np.float64) + 1.0
    return math.sqrt(2.0 / (length + 1)) * np.sin(np.pi * steps[:, None] * steps[None, :] / (length + 1))


def eigenvalues(length):
    return 2.0 - 2.0 * np.cos(np.pi * (np.arange(length, dtype=np.float64) + 1.0) / (length + 1))


def coarse_tables(size_x, size_y, size_z):
    sine_x, sine_z = sine_table(size_x), sine_table(size_z)
    back = np.einsum("dk,zl->dzkl", sine_x, np.repeat(sine_z, 2, axis=0))
    back = np.repeat(back[:, None], 2, axis=1).reshape(size_x * 4 * size_z, size_x * size_z)
    total = eigenvalues(size_y)[:, None, None] + eigenvalues(size_x)[None, :, None] + eigenvalues(size_z)[None, None, :]
    inverse = (1.0 / total).reshape(size_y, size_x * size_z)
    as_f32 = lambda x: jnp.asarray(np.ascontiguousarray(x), F32)
    return as_f32(0.5 * back), as_f32(sine_table(size_y)), as_f32(inverse), as_f32(back.T)


def shards(occupied, virtual, pair_ids):
    _, slab, rows_y, lanes = occupied.shape
    pairs = pair_ids.shape[0]
    slabs = lax.axis_size("dom")
    me = lax.axis_index("dom")
    parts = slabs // pairs
    half_y = rows_y // 2
    part_rows = half_y // parts
    first_pair = lax.axis_index("pair") * pairs
    place = jnp.stack([me, slabs - 1 - me, me % 2, me % parts, first_pair]).astype(jnp.int32)
    fold = np.zeros((2 * lanes, lanes), np.float32)
    fold[np.arange(2 * lanes), np.arange(2 * lanes) // 2] = 0.5
    spread = (2.0 * fold).T
    by_pair = lambda *tail: (lambda p, *_: (p,) + tail)
    row_of = lambda column: (lambda p, ids, *_: (ids[p, column], 0, 0, 0))
    orbital = (1, slab, rows_y, lanes)

    shares, first, second, v0 = pl.pallas_call(
        source_kernel,
        grid_spec=pltpu.PrefetchScalarGridSpec(
            num_scalar_prefetch=2,
            grid=(pairs,),
            in_specs=[
                pl.BlockSpec(orbital, row_of(0)),
                pl.BlockSpec(orbital, row_of(1)),
                pl.BlockSpec((2 * lanes, lanes), lambda p, *_: (0, 0)),
            ],
            out_specs=[
                pl.BlockSpec((1, parts, 3, part_rows, lanes), by_pair(0, 0, 0, 0)),
                pl.BlockSpec((1, 3, rows_y, lanes), by_pair(0, 0, 0)),
                pl.BlockSpec((1, 3, rows_y, lanes), by_pair(0, 0, 0)),
                pl.BlockSpec(orbital, by_pair(0, 0, 0)),
            ],
            scratch_shapes=[
                pltpu.VMEM((slab, rows_y + 2 * PAD, lanes), F32),
                pltpu.VMEM((slab + 2, rows_y + 2 * PAD, lanes), F32),
                pltpu.VMEM((slab // 2 + 2, rows_y, lanes), F32),
            ],
        ),
        out_shape=[
            jax.ShapeDtypeStruct((pairs, parts, 3, part_rows, lanes), BF16),
            jax.ShapeDtypeStruct((pairs, 3, rows_y, lanes), BF16),
            jax.ShapeDtypeStruct((pairs, 3, rows_y, lanes), BF16),
            jax.ShapeDtypeStruct((pairs, slab, rows_y, lanes), F32),
        ],
        compiler_params=pltpu.CompilerParams(vmem_limit_bytes=60 * 1024 * 1024),
        name="source",
    )(pair_ids, place, occupied, virtual, jnp.asarray(fold, BF16))

    inside = [(i, i ^ 1) for i in range(slabs)]
    across = [(i, i + 1) for i in range(1, slabs - 1, 2)]
    across = across + [(j, i) for i, j in across]
    first_halo = lax.ppermute(first, "dom", inside)
    second_halo = lax.ppermute(second, "dom", across)

    received = lax.all_to_all(shares.reshape(slabs, 3, part_rows, lanes), "dom", 0, 0)
    views = [received]
    for turn in range(1, parts):
        perm = [(g * parts + (h + turn) % parts, g * parts + h) for g in range(slabs // parts) for h in range(parts)]
        views.append(lax.ppermute(received, "dom", perm))
    tables = coarse_tables(slabs, half_y // 2, lanes // 4)
    vmem = pl.BlockSpec(memory_space=pltpu.VMEM)
    padded = (slabs, half_y + 2 * PAD, lanes)
    smoothed = pl.pallas_call(
        middle_kernel,
        in_specs=[pl.BlockSpec(memory_space=pltpu.SMEM)] + [vmem] * (parts + 4),
        out_specs=vmem,
        out_shape=jax.ShapeDtypeStruct((slabs, 3, part_rows, lanes), BF16),
        scratch_shapes=[
            pltpu.VMEM(padded, F32),
            pltpu.VMEM(padded, F32),
            pltpu.VMEM(padded, F32),
            pltpu.VMEM((slabs, half_y, lanes), F32),
            pltpu.VMEM((slabs, half_y, lanes), F32),
        ],
        compiler_params=pltpu.CompilerParams(vmem_limit_bytes=50 * 1024 * 1024),
        name="middle",
    )(place, *views, *tables)
    groups = lax.axis_size("pair")
    ids, smoothed = lax.optimization_barrier((pair_ids, smoothed))
    turns = [[((g + turn) % groups, g) for g in range(groups)] for turn in range(1, groups)]
    all_ids = jnp.concatenate([ids] + [lax.ppermute(ids, "pair", perm) for perm in turns], axis=0)
    returned = lax.all_to_all(smoothed, "dom", 0, 0).reshape(pairs, parts, 3, part_rows, lanes)

    count = all_ids.shape[0]
    potentials, panel = pl.pallas_call(
        final_kernel,
        grid_spec=pltpu.PrefetchScalarGridSpec(
            num_scalar_prefetch=3,
            grid=(pairs,),
            in_specs=[
                pl.BlockSpec(orbital, row_of(0)),
                pl.BlockSpec(orbital, row_of(1)),
                pl.BlockSpec(orbital, by_pair(0, 0, 0)),
                pl.BlockSpec((1, parts, 3, part_rows, lanes), by_pair(0, 0, 0, 0)),
                pl.BlockSpec((1, 3, rows_y, lanes), by_pair(0, 0, 0)),
                pl.BlockSpec((1, 3, rows_y, lanes), by_pair(0, 0, 0)),
                pl.BlockSpec((lanes, 2 * lanes), lambda p, *_: (0, 0)),
                pl.BlockSpec(memory_space=pl.ANY),
                pl.BlockSpec(memory_space=pl.ANY),
            ],
            out_specs=[
                pl.BlockSpec(orbital, by_pair(0, 0, 0)),
                pl.BlockSpec((count, pairs, lanes), lambda p, *_: (0, 0, 0)),
            ],
            scratch_shapes=[
                pltpu.VMEM((4, rows_y, lanes), F32),
                pltpu.VMEM((slab + 4, rows_y + 2 * PAD, lanes), F32),
                pltpu.VMEM((slab + 2, rows_y + 2 * PAD, lanes), F32),
                pltpu.VMEM((slab, pairs, rows_y, lanes), BF16),
                pltpu.VMEM(occupied.shape, BF16),
                pltpu.VMEM(virtual.shape, BF16),
                pltpu.SemaphoreType.DMA((2,)),
            ],
        ),
        out_shape=[
            jax.ShapeDtypeStruct((pairs, slab, rows_y, lanes), BF16),
            jax.ShapeDtypeStruct((count, pairs, lanes), F32),
        ],
        compiler_params=pltpu.CompilerParams(vmem_limit_bytes=60 * 1024 * 1024),
        name="final",
    )(
        pair_ids, all_ids, place, occupied, virtual, v0, returned, first_halo, second_halo,
        jnp.asarray(spread, BF16), occupied, virtual,
    )
    sums = jnp.sum(panel, axis=2).reshape(slabs, count // slabs, pairs)
    blocks = lax.all_to_all(sums, "dom", 0, 0)
    return potentials, jnp.sum(blocks, axis=0) / float(slab * rows_y * lanes * slabs)


def solution(mesh):
    placed = (P(None, "dom", None, None), P(None, "dom", None, None), P("pair", None))
    return jax.shard_map(
        shards,
        mesh=mesh,
        in_specs=placed,
        out_specs=(P("pair", "dom", None, None), P("dom", "pair")),
        check_vma=False,
    )
```

```python
import math

import jax
import jax.numpy as jnp
import numpy as np
from jax import lax
from jax.experimental import pallas as pl
from jax.experimental.pallas import tpu as pltpu
from jax.sharding import PartitionSpec as P

W = 0.8 / 6.0
CENTRE = 1.5
PAD = 8
STEP = 64
F32 = jnp.float32
BF16 = jnp.bfloat16
MIB = 1024 * 1024
HIGHEST = lax.Precision.HIGHEST


def dot(a, b, contract=((1,), (0,)), precision=None):
    return lax.dot_general(a, b, (contract, ((), ())), precision=precision, preferred_element_type=F32)


def high_low(x):
    high = x.astype(BF16)
    return high, (x - high.astype(F32)).astype(BF16)


def dot_split(a, table, contract=((1,), (0,))):
    high, low = high_low(a)
    return dot(high, table[0], contract) + (dot(low, table[0], contract) + dot(high, table[1], contract))


def zero_rims(ref):
    zeros = jnp.zeros((ref.shape[0], PAD, ref.shape[2]), F32)
    ref[:, :PAD] = zeros
    ref[:, ref.shape[1] - PAD :] = zeros


def read(ref, layer, row, rows=STEP):
    return ref[layer, PAD + row : PAD + row + rows, :]


def put(ref, layer, row, value):
    ref[layer, PAD + row : PAD + row + value.shape[0]] = value


def across(centre, blocks=1):
    lane = lax.broadcasted_iota(jnp.int32, centre.shape, 1)
    width = centre.shape[1] // blocks
    first = lane % width == 0 if blocks > 1 else lane == 0
    last = lane % width == width - 1 if blocks > 1 else lane == width - 1
    lower = jnp.where(first, 0.0, pltpu.roll(centre, 1, 1))
    upper = jnp.where(last, 0.0, pltpu.roll(centre, centre.shape[1] - 1, 1))
    return CENTRE * centre + lower + upper


def across_by_matrix(centre, band):
    high, low = high_low(centre)
    return dot(jnp.concatenate([high, low], axis=1), band)


def beside(ref, layer, row, rows=STEP):
    return read(ref, layer, row - 1, rows) + read(ref, layer, row + 1, rows)


def stencil(ref, layer, row, band):
    centre = read(ref, layer, row)
    along_z = across(centre) if layer % 2 else across_by_matrix(centre, band)
    return along_z + beside(ref, layer, row)


def fill_band(ref):
    lanes = ref.shape[1]
    line = lax.rem(lax.broadcasted_iota(jnp.int32, ref.shape, 0), lanes)
    apart = jnp.abs(line - lax.broadcasted_iota(jnp.int32, ref.shape, 1))
    ref[...] = jnp.where(apart == 0, CENTRE, jnp.where(apart == 1, 1.0, 0.0)).astype(BF16)


def fill_children(ref, value, axis):
    child = lax.broadcasted_iota(jnp.int32, ref.shape, axis)
    parent = lax.broadcasted_iota(jnp.int32, ref.shape, 1 - axis)
    ref[...] = jnp.where(child // 2 == parent, value, 0.0).astype(BF16)


def sides(axis="dom"):
    me, count = lax.axis_index(axis), lax.axis_size(axis)
    below = jnp.where(me == 0, 0.0, 1.0).astype(F32)
    above = jnp.where(me == count - 1, 0.0, 1.0).astype(F32)
    return below, above, lax.rem(me, 2) == 0


def source_kernel(
    ids_hbm, occ, vir, shares, first, second, v0_out, ids_out,
    ids, occ_rows, vir_rows, band, fold, own, once, v0s, sums, packed, share, ids_tile, ids_sems, in_sems, out_sems,
):
    pairs, slab, rows_y, lanes = occ_rows.shape
    parts, part_rows = share.shape[1], share.shape[3]
    in_left, in_right, even = sides()
    upper = jnp.where(even, 1, 0)

    copy = pltpu.make_async_copy(ids_hbm, ids, ids_sems.at[0])
    copy.start()
    copy.wait()

    def inputs(p):
        return (
            pltpu.make_async_copy(occ.at[ids[0, p]], occ_rows.at[p], in_sems.at[0, p]),
            pltpu.make_async_copy(vir.at[ids[1, p]], vir_rows.at[p], in_sems.at[1, p]),
        )

    def outputs(p):
        return (
            pltpu.make_async_copy(share.at[p], shares.at[p], out_sems.at[0, p]),
            pltpu.make_async_copy(packed.at[p, upper], first.at[p], out_sems.at[1, p]),
            pltpu.make_async_copy(packed.at[p, 1 - upper], second.at[p], out_sems.at[2, p]),
            pltpu.make_async_copy(v0s.at[p], v0_out.at[p], out_sems.at[3, p]),
        )

    for p in range(pairs):
        for copy in inputs(p):
            copy.start()
    line = lax.broadcasted_iota(jnp.int32, ids_tile.shape, 0)
    lane = lax.broadcasted_iota(jnp.int32, ids_tile.shape, 1)
    tile = jnp.zeros(ids_tile.shape, F32)
    for p in range(pairs):
        for j in range(2):
            tile = jnp.where((line == j) & (lane == p), ids[j, p].astype(F32), tile)
    ids_tile[...] = tile.astype(BF16)
    ids_copy = pltpu.make_async_copy(ids_tile, ids_out, ids_sems.at[1])
    ids_copy.start()
    fill_band(band)
    fill_children(fold, 0.5, 0)
    zero_rims(own)
    zero_rims(once)

    def one_pair(p, carry):
        for copy in inputs(p):
            copy.wait()
        for layer in range(slab):
            own[layer, PAD : PAD + rows_y] = occ_rows[p, layer].astype(F32) * vir_rows[p, layer].astype(F32)

        for row in range(0, rows_y, STEP):
            rows = slice(row, row + STEP)
            for layer in range(slab):
                centre = read(own, layer, row)
                total = stencil(own, layer, row, band[...])
                if layer > 0:
                    total = total + read(own, layer - 1, row)
                if layer < slab - 1:
                    total = total + read(own, layer + 1, row)
                value = W * total
                put(once, layer + 1, row, value)
                v0 = W * (centre + value)
                v0s[p, layer, rows] = v0
                if layer == 0:
                    put(once, 0, row, (W * in_left) * centre)
                    packed[p, 0, 0, rows] = centre.astype(BF16)
                    packed[p, 0, 1, rows] = v0.astype(BF16)
                if layer == 1:
                    packed[p, 0, 2, rows] = v0.astype(BF16)
                if layer == slab - 2:
                    packed[p, 1, 2, rows] = v0.astype(BF16)
                if layer == slab - 1:
                    put(once, slab + 1, row, (W * in_right) * centre)
                    packed[p, 1, 0, rows] = centre.astype(BF16)
                    packed[p, 1, 1, rows] = v0.astype(BF16)

        def twice(layer, row):
            if layer == -2:
                return read(once, 0, row)
            if layer == slab + 1:
                return read(once, slab + 1, row)
            at = layer + 1
            total = stencil(once, at, row, band[...])
            if at > 0:
                total = total + read(once, at - 1, row)
            if at < slab + 1:
                total = total + read(once, at + 1, row)
            return total

        for row in range(0, rows_y, STEP):
            for coarse in range(slab // 2 + 2):
                pair_sum = twice(2 * coarse - 2, row) + twice(2 * coarse - 1, row)
                sums[coarse, row : row + STEP] = W * pair_sum

        half = rows_y // 2

        def folded(coarse):
            return sums[coarse, pl.ds(0, half, stride=2), :] + sums[coarse, pl.ds(1, half, stride=2), :]

        def together(left, right):
            both = jnp.concatenate([folded(left), folded(right)], axis=1)
            high, low = high_low(both)
            return dot(high, fold[...]) + dot(low, fold[...])

        outer = together(3, 0)
        edge = outer.astype(BF16)
        lane = lax.broadcasted_iota(jnp.int32, outer.shape, 1)
        rest = pltpu.roll(outer - edge.astype(F32), lanes // 2, 1) * jnp.where(lane < lanes // 2, in_left, in_right)
        own_high, own_low = high_low(together(1, 2) + rest)
        for part in range(parts):
            rows = slice(part * part_rows, (part + 1) * part_rows)
            share[p, part, 0] = own_high[rows]
            share[p, part, 1] = own_low[rows]
            share[p, part, 2] = edge[rows]
        for copy in outputs(p):
            copy.start()
        return carry

    lax.fori_loop(0, pairs, one_pair, 0)
    ids_copy.wait()
    for p in range(pairs):
        for copy in outputs(p):
            copy.wait()


def middle_kernel(*refs):
    parts = len(refs) - 10
    received = refs[:parts]
    modes, table_y, inverse, ids_tile, out = refs[parts : parts + 5]
    source, field_a, field_b, smooth, edge = refs[parts + 5 :]
    slabs, _, part_rows, lanes = received[0].shape
    rows_y = parts * part_rows
    own_part = lax.rem(lax.axis_index("dom"), parts)
    left = lax.broadcasted_iota(jnp.int32, (part_rows, lanes), 1) < lanes // 2
    for ref in (source, field_a, field_b):
        zero_rims(ref)
    for turn in range(parts):
        at = own_part + turn
        at = jnp.where(at >= parts, at - parts, at) * part_rows
        at = pl.multiple_of(at, part_rows)
        ref = received[turn]
        for d in range(slabs):
            value = ref[d, 0].astype(F32) + ref[d, 1].astype(F32)
            before = ref[d - 1, 2].astype(F32) if d > 0 else jnp.zeros_like(value)
            after = ref[d + 1, 2].astype(F32) if d < slabs - 1 else jnp.zeros_like(value)
            source[d, pl.ds(PAD + at, part_rows)] = value + jnp.where(left, before, after)

    half = lanes // 2
    left = lax.broadcasted_iota(jnp.int32, (rows_y, lanes), 1) < half

    def swapped(ref, d):
        return pltpu.roll(read(ref, d, 0, rows_y), half, 1)

    def apply(ref, each):
        zeros = jnp.zeros((rows_y, lanes), F32)
        before, here = zeros, swapped(ref, 0)
        for d in range(slabs):
            after = swapped(ref, d + 1) if d < slabs - 1 else zeros
            total = across(read(ref, d, 0, rows_y), 2) + beside(ref, d, 0, rows_y)
            each(d, total + here + jnp.where(left, before, after))
            before, here = here, after

    apply(source, lambda d, total: put(field_a, d, 0, W * total))

    def to_coarse(d, total):
        smooth[d] = W * (read(source, d, 0, rows_y) + read(field_a, d, 0, rows_y))
        put(field_b, d, 0, W * total)

    apply(field_a, to_coarse)
    pieces = []
    for d in range(slabs):
        even_rows = field_b[d, pl.ds(PAD, rows_y // 2, stride=2), :]
        odd_rows = field_b[d, pl.ds(PAD + 1, rows_y // 2, stride=2), :]
        pieces.append(even_rows + odd_rows)
    spectral = dot_split(jnp.concatenate(pieces, axis=1), modes)
    spectral = dot(table_y[...], spectral, precision=HIGHEST) * inverse[...]
    spread = dot_split(dot(table_y[...], spectral, precision=HIGHEST), modes, ((1,), (1,)))
    for d in range(slabs):
        value = spread[:, d * lanes : (d + 1) * lanes]
        field_b[d, pl.ds(PAD, rows_y // 2, stride=2), :] = value
        field_b[d, pl.ds(PAD + 1, rows_y // 2, stride=2), :] = value
    for d in range(slabs):
        put(field_a, d, 0, smooth[d] + read(field_b, d, 0, rows_y))

    def add_source(ref):
        return lambda d, total: put(ref, d, 0, W * (total + read(source, d, 0, rows_y)))

    apply(field_a, add_source(field_b))
    apply(field_b, add_source(field_a))
    zeros = jnp.zeros((rows_y, lanes), F32)
    before, here = zeros, swapped(field_a, 0)
    for d in range(slabs):
        after = swapped(field_a, d + 1) if d < slabs - 1 else zeros
        edge[d] = jnp.where(left, before, after) - read(field_a, d, 0, rows_y)
        before, here = here, after
    at = pl.multiple_of(own_part * part_rows, part_rows)
    for d in range(slabs):
        high, low = high_low(field_a[d, pl.ds(PAD + at, part_rows)])
        out[d, :part_rows] = high
        out[d, part_rows : 2 * part_rows] = low
        out[d, 2 * part_rows : 3 * part_rows] = edge[d, pl.ds(at, part_rows)].astype(BF16)
        out[d, 3 * part_rows :] = ids_tile[...]


def final_kernel(
    ids_hbm, all_occ, all_vir, v0_hbm, coarse, first, second, out, panel,
    ids, occ_rows, vir_rows, v0, band, spread, identity, own_field, wide, start, swept, kept,
    occ, vir, late_vector, late_ids, turned, sums, ids_sem, in_sems, out_sems, late_sems,
):
    pairs, slab, rows_y, lanes = kept.shape
    groups = late_vector.shape[0]
    parts, part_rows = coarse.shape[0] // pairs, (coarse.shape[1] - 16) // 3
    in_left, in_right, even = sides()

    ids_copy = pltpu.make_async_copy(ids_hbm, ids, ids_sem)
    ids_copy.start()

    def inputs(p):
        return [pltpu.make_async_copy(v0_hbm.at[p], v0.at[p], in_sems.at[0, p])]

    def own_rows(p):
        return [
            pltpu.make_async_copy(all_occ.at[ids[0, p]], occ_rows.at[p], in_sems.at[1, p]),
            pltpu.make_async_copy(all_vir.at[ids[1, p]], vir_rows.at[p], in_sems.at[2, p]),
        ]

    def output(p):
        return pltpu.make_async_copy(kept.at[p], out.at[p], out_sems.at[p])

    for copy in inputs(0):
        copy.start()
    ids_copy.wait()
    for copy in own_rows(0):
        copy.start()
    for p in range(1, pairs):
        for copy in inputs(p) + own_rows(p):
            copy.start()
    late = [pltpu.make_async_copy(all_occ, occ, late_sems.at[0]), pltpu.make_async_copy(all_vir, vir, late_sems.at[1])]
    for copy in late:
        copy.start()
    fill_band(band)
    fill_children(spread, 1.0, 1)
    line = lax.broadcasted_iota(jnp.int32, identity.shape, 0)
    identity[...] = jnp.where(line == lax.broadcasted_iota(jnp.int32, identity.shape, 1), 1.0, 0.0).astype(BF16)
    zero_rims(start)
    zero_rims(swept)

    def one_pair(p, carry):
        for copy in inputs(p) + own_rows(p):
            copy.wait()
        for layer in range(slab):
            own_field[layer] = occ_rows[p, layer].astype(F32) * vir_rows[p, layer].astype(F32)
        for part in range(parts):
            table = spread[...]
            at = p * parts + part
            own = dot(coarse[at, :part_rows], table) + dot(coarse[at, part_rows : 2 * part_rows], table)
            beyond = own + dot(coarse[at, 2 * part_rows : 3 * part_rows], table)
            for at, value in enumerate((beyond[:, :lanes], own[:, :lanes], own[:, lanes:], beyond[:, lanes:])):
                rows = 2 * part * part_rows
                wide[at, pl.ds(rows, part_rows, stride=2), :] = value
                wide[at, pl.ds(rows + 1, part_rows, stride=2), :] = value

        def halo(edge, index, row):
            rows = slice(row, row + STEP)
            one, two = first[p, index, rows].astype(F32), second[p, index, rows].astype(F32)
            return jnp.where(even == (edge == 1), one, two)

        for row in range(0, rows_y, STEP):
            rows = slice(row, row + STEP)
            for layer in range(slab):
                value = v0[p, layer, rows] + wide[1 + layer // 2, rows]
                if layer == 0:
                    value = value + (W * W) * halo(0, 0, row)
                if layer == slab - 1:
                    value = value + (W * W) * halo(1, 0, row)
                put(start, layer + 2, row, value)
            near = halo(0, 1, row) + (W * W) * own_field[0, rows] + wide[0, rows]
            put(start, 1, row, in_left * near)
            put(start, 0, row, in_left * (halo(0, 2, row) + wide[0, rows]))
            near = halo(1, 1, row) + (W * W) * own_field[slab - 1, rows] + wide[3, rows]
            put(start, slab + 2, row, in_right * near)
            put(start, slab + 3, row, in_right * (halo(1, 2, row) + wide[3, rows]))

        def sweep(ref, at, row, source):
            total = stencil(ref, at, row, band[...])
            return W * (total + read(ref, at - 1, row) + read(ref, at + 1, row) + source)

        for row in range(0, rows_y, STEP):
            rows = slice(row, row + STEP)
            put(swept, 0, row, in_left * sweep(start, 1, row, halo(0, 0, row)))
            for layer in range(slab):
                put(swept, layer + 1, row, sweep(start, layer + 2, row, own_field[layer, rows]))
            put(swept, slab + 1, row, in_right * sweep(start, slab + 2, row, halo(1, 0, row)))
        for row in range(0, rows_y, STEP):
            rows = slice(row, row + STEP)
            for layer in range(slab):
                value = sweep(swept, layer + 1, row, own_field[layer, rows]).astype(BF16)
                kept[p, layer, rows] = value
        output(p).start()
        return carry

    lax.fori_loop(0, pairs, one_pair, 0)

    for copy in late:
        copy.wait()
    for turn in range(groups):
        late_vector[turn] = coarse[turn, 3 * part_rows :].astype(F32).astype(jnp.int32)
    copy = pltpu.make_async_copy(late_vector, late_ids, ids_sem)
    copy.start()
    half = lanes // 2
    for q in range(pairs):
        for layer in range(slab):
            value = dot(identity[...], kept[q, layer], ((1,), (1,))).astype(BF16)
            column = 2 * layer * rows_y
            turned[q * half : (q + 1) * half, column : column + rows_y] = value[:half]
            turned[q * half : (q + 1) * half, column + rows_y : column + 2 * rows_y] = value[half:]
    copy.wait()
    count = groups * pairs
    first_row = lax.axis_index("pair") * pairs
    left = lax.broadcasted_iota(jnp.int32, (rows_y, lanes), 1) < half
    diagonal = lax.broadcasted_iota(jnp.int32, (half, 2 * lanes), 0) == lax.rem(
        lax.broadcasted_iota(jnp.int32, (half, 2 * lanes), 1), half
    )

    def density16(p, layer):
        turn, k = p // pairs, lax.rem(p, pairs)
        i, a = late_ids[turn, 0, k], late_ids[turn, 1, k]
        return (occ[i, layer].astype(F32) * vir[a, layer].astype(F32)).astype(BF16)

    def four_rows(turn, carry):
        p = 4 * turn
        pieces = []
        for layer in range(slab):
            upper_row, lower_row = [], []
            for j in (0, 2):
                one, two = density16(p + j, layer), density16(p + j + 1, layer)
                upper_row.append(jnp.where(left, one, pltpu.roll(two, half, 1)))
                lower_row.append(jnp.where(left, pltpu.roll(one, half, 1), two))
            pieces += [jnp.concatenate(upper_row, axis=1), jnp.concatenate(lower_row, axis=1)]
        product = dot(turned[...], jnp.concatenate(pieces, axis=0))
        row = first_row + p
        row = jnp.where(row >= count, row - count, row) // 2
        for q in range(pairs):
            block = jnp.where(diagonal, product[q * half : (q + 1) * half], 0.0)
            block = jnp.sum(block, axis=0, keepdims=True)
            sums[row, q : q + 1] = block[:, :lanes]
            sums[row + 1, q : q + 1] = block[:, lanes:]
        return carry

    lax.fori_loop(0, count // 4, four_rows, 0)
    scale = 1.0 / float(slab * rows_y * lanes * lax.axis_size("dom"))
    total = scale * sums[...]
    left = lax.broadcasted_iota(jnp.int32, total.shape, 2) < half
    panel[0] = jnp.sum(jnp.where(left, total, 0.0), axis=2)
    panel[1] = jnp.sum(jnp.where(left, 0.0, total), axis=2)
    for p in range(pairs):
        output(p).wait()


def sine_table(length):
    steps = np.arange(length, dtype=np.float64) + 1.0
    return math.sqrt(2.0 / (length + 1)) * np.sin(np.pi * steps[:, None] * steps[None, :] / (length + 1))


def eigenvalues(length):
    return 2.0 - 2.0 * np.cos(np.pi * (np.arange(length, dtype=np.float64) + 1.0) / (length + 1))


def coarse_tables(size_x, size_y, size_z):
    sine_x, sine_z = sine_table(size_x), sine_table(size_z)
    modes = np.einsum("dk,zl->dzkl", sine_x, np.repeat(sine_z, 2, axis=0))
    modes = np.repeat(modes[:, None], 2, axis=1).reshape(size_x * 4 * size_z, size_x * size_z)
    high = modes.astype(BF16)
    low = (modes - high.astype(np.float64)).astype(BF16)
    total = eigenvalues(size_y)[:, None, None] + eigenvalues(size_x)[None, :, None] + eigenvalues(size_z)[None, None, :]
    inverse = (0.5 / total).reshape(size_y, size_x * size_z)
    return jnp.asarray(np.stack([high, low])), jnp.asarray(sine_table(size_y), F32), jnp.asarray(inverse, F32)


def shards(occupied, virtual, pair_ids):
    orbitals, slab, rows_y, lanes = occupied.shape
    pairs = pair_ids.shape[0]
    slabs = lax.axis_size("dom")
    parts = slabs // pairs
    half_y = rows_y // 2
    part_rows = half_y // parts
    padded_y = rows_y + 2 * PAD
    ids = pair_ids.T

    hbm, vmem = pl.BlockSpec(memory_space=pltpu.HBM), pl.BlockSpec(memory_space=pltpu.VMEM)
    anywhere = pl.BlockSpec(memory_space=pl.ANY)
    in_hbm = lambda x: pltpu.with_memory_space_constraint(x, pltpu.HBM)
    halo = (pairs, 3, rows_y, lanes)
    own = (pairs, slab, rows_y, lanes)
    share = (pairs, parts, 3, part_rows, lanes)
    tile = (16, lanes)
    shares, first, second, v0, ids_tile = pl.pallas_call(
        source_kernel,
        in_specs=[hbm, hbm, hbm],
        out_specs=[hbm] * 5,
        out_shape=[
            pltpu.HBM(share, BF16),
            pltpu.HBM(halo, BF16),
            pltpu.HBM(halo, BF16),
            pltpu.HBM(own, F32),
            pltpu.HBM(tile, BF16),
        ],
        scratch_shapes=[
            pltpu.SMEM(ids.shape, jnp.int32),
            pltpu.VMEM(own, BF16),
            pltpu.VMEM(own, BF16),
            pltpu.VMEM((2 * lanes, lanes), BF16),
            pltpu.VMEM((2 * lanes, lanes), BF16),
            pltpu.VMEM((slab, padded_y, lanes), F32),
            pltpu.VMEM((slab + 2, padded_y, lanes), F32),
            pltpu.VMEM(own, F32),
            pltpu.VMEM((slab // 2 + 2, rows_y, lanes), F32),
            pltpu.VMEM((pairs, 2, 3, rows_y, lanes), BF16),
            pltpu.VMEM(share, BF16),
            pltpu.VMEM(tile, BF16),
            pltpu.SemaphoreType.DMA((2,)),
            pltpu.SemaphoreType.DMA((2, pairs)),
            pltpu.SemaphoreType.DMA((4, pairs)),
        ],
        compiler_params=pltpu.CompilerParams(vmem_limit_bytes=32 * MIB),
        name="source",
    )(in_hbm(ids), in_hbm(occupied), in_hbm(virtual))

    inside = [(i, i ^ 1) for i in range(slabs)]
    outside = [(i, i + 1) for i in range(1, slabs - 1, 2)]
    outside = outside + [(j, i) for i, j in outside]
    first_halo = lax.ppermute(first, "dom", inside)
    second_halo = lax.ppermute(second, "dom", outside)
    groups = lax.axis_size("pair")
    perm = [(d * groups + (g + d) % groups, d * groups + g) for d in range(slabs) for g in range(groups)]
    ids_tile = lax.ppermute(ids_tile, ("dom", "pair"), perm)

    received = lax.all_to_all(shares.reshape(slabs, 3, part_rows, lanes), "dom", 0, 0)
    views = [received]
    for turn in range(1, parts):
        perm = [(g * parts + (h + turn) % parts, g * parts + h) for g in range(slabs // parts) for h in range(parts)]
        views.append(lax.ppermute(received, "dom", perm))
    tables = coarse_tables(slabs, half_y // 2, lanes // 4)
    padded = pltpu.VMEM((slabs, half_y + 2 * PAD, lanes), F32)
    plain = pltpu.VMEM((slabs, half_y, lanes), F32)
    smoothed = pl.pallas_call(
        middle_kernel,
        in_specs=[vmem] * (parts + 4),
        out_specs=vmem,
        out_shape=jax.ShapeDtypeStruct((slabs, 3 * part_rows + 16, lanes), BF16),
        scratch_shapes=[padded, padded, padded, plain, plain],
        compiler_params=pltpu.CompilerParams(vmem_limit_bytes=32 * MIB),
        name="middle",
    )(*views, *tables, ids_tile)
    returned = lax.all_to_all(smoothed, "dom", 0, 0)

    count = groups * pairs
    potentials, panel = pl.pallas_call(
        final_kernel,
        in_specs=[hbm] * 4 + [vmem] * 3,
        out_specs=[hbm, vmem],
        out_shape=[pltpu.HBM(own, BF16), jax.ShapeDtypeStruct((2, count // 2, pairs), F32)],
        scratch_shapes=[
            pltpu.SMEM(ids.shape, jnp.int32),
            pltpu.VMEM(own, BF16),
            pltpu.VMEM(own, BF16),
            pltpu.VMEM(own, F32),
            pltpu.VMEM((2 * lanes, lanes), BF16),
            pltpu.VMEM((lanes, 2 * lanes), BF16),
            pltpu.VMEM((lanes, lanes), BF16),
            pltpu.VMEM((slab, rows_y, lanes), F32),
            pltpu.VMEM((4, rows_y, lanes), F32),
            pltpu.VMEM((slab + 4, padded_y, lanes), F32),
            pltpu.VMEM((slab + 2, padded_y, lanes), F32),
            pltpu.VMEM(own, BF16),
            pltpu.VMEM(occupied.shape, BF16),
            pltpu.VMEM(virtual.shape, BF16),
            pltpu.VMEM((groups,) + tile, jnp.int32),
            pltpu.SMEM((groups,) + tile, jnp.int32),
            pltpu.VMEM((pairs * lanes // 2, 2 * slab * rows_y), BF16),
            pltpu.VMEM((count // 2, pairs, lanes), F32),
            pltpu.SemaphoreType.DMA,
            pltpu.SemaphoreType.DMA((3, pairs)),
            pltpu.SemaphoreType.DMA((pairs,)),
            pltpu.SemaphoreType.DMA((2,)),
        ],
        compiler_params=pltpu.CompilerParams(vmem_limit_bytes=24 * MIB),
        name="final",
    )(in_hbm(ids), in_hbm(occupied), in_hbm(virtual), in_hbm(v0), returned, first_halo, second_halo)
    panel = jnp.swapaxes(panel, 0, 1).reshape(slabs, count // slabs, pairs)
    return potentials, jnp.sum(lax.all_to_all(panel, "dom", 0, 0), axis=0)


def solution(mesh):
    placed = (P(None, "dom", None, None), P(None, "dom", None, None), P("pair", None))
    return jax.shard_map(
        shards,
        mesh=mesh,
        in_specs=placed,
        out_specs=(P("pair", "dom", None, None), P("dom", "pair")),
        check_vma=False,
    )
```

```python
import math

import jax
import jax.numpy as jnp
import numpy as np
from jax import lax
from jax.experimental import pallas as pl
from jax.experimental.pallas import tpu as pltpu
from jax.sharding import PartitionSpec as P

W = 0.8 / 6.0
CENTRE = 1.5
PAD = 8
STEP = 64
F32 = jnp.float32
BF16 = jnp.bfloat16
MIB = 1024 * 1024
HIGHEST = lax.Precision.HIGHEST


def dot(a, b, contract=((1,), (0,)), precision=None):
    return lax.dot_general(a, b, (contract, ((), ())), precision=precision, preferred_element_type=F32)


def high_low(x):
    high = x.astype(BF16)
    return high, (x - high.astype(F32)).astype(BF16)


def dot_split(a, table, contract=((1,), (0,))):
    high, low = high_low(a)
    return dot(high, table[0], contract) + (dot(low, table[0], contract) + dot(high, table[1], contract))


def zero_rims(ref):
    zeros = jnp.zeros((ref.shape[0], PAD, ref.shape[2]), F32)
    ref[:, :PAD] = zeros
    ref[:, ref.shape[1] - PAD :] = zeros


def read(ref, layer, row, rows=STEP):
    return ref[layer, PAD + row : PAD + row + rows, :]


def put(ref, layer, row, value):
    ref[layer, PAD + row : PAD + row + value.shape[0]] = value


def across(centre, blocks=1):
    lane = lax.broadcasted_iota(jnp.int32, centre.shape, 1)
    width = centre.shape[1] // blocks
    first = lane % width == 0 if blocks > 1 else lane == 0
    last = lane % width == width - 1 if blocks > 1 else lane == width - 1
    lower = jnp.where(first, 0.0, pltpu.roll(centre, 1, 1))
    upper = jnp.where(last, 0.0, pltpu.roll(centre, centre.shape[1] - 1, 1))
    return CENTRE * centre + lower + upper


def across_by_matrix(centre, band):
    high, low = high_low(centre)
    return dot(jnp.concatenate([high, low], axis=1), band)


def beside(ref, layer, row, rows=STEP):
    return read(ref, layer, row - 1, rows) + read(ref, layer, row + 1, rows)


def stencil(ref, layer, row, band):
    centre = read(ref, layer, row)
    along_z = across(centre) if layer % 2 else across_by_matrix(centre, band)
    return along_z + beside(ref, layer, row)


def fill_band(ref):
    lanes = ref.shape[1]
    line = lax.rem(lax.broadcasted_iota(jnp.int32, ref.shape, 0), lanes)
    apart = jnp.abs(line - lax.broadcasted_iota(jnp.int32, ref.shape, 1))
    ref[...] = jnp.where(apart == 0, CENTRE, jnp.where(apart == 1, 1.0, 0.0)).astype(BF16)


def fill_children(ref, value, axis):
    child = lax.broadcasted_iota(jnp.int32, ref.shape, axis)
    parent = lax.broadcasted_iota(jnp.int32, ref.shape, 1 - axis)
    ref[...] = jnp.where(child // 2 == parent, value, 0.0).astype(BF16)


def sides(axis="dom"):
    me, count = lax.axis_index(axis), lax.axis_size(axis)
    below = jnp.where(me == 0, 0.0, 1.0).astype(F32)
    above = jnp.where(me == count - 1, 0.0, 1.0).astype(F32)
    return below, above, lax.rem(me, 2) == 0


def source_kernel(
    ids_hbm, occ, vir, shares, first, second, v0_out, ids_out,
    ids, occ_rows, vir_rows, band, fold, own, once, v0s, sums, packed, share, ids_tile, ids_sems, in_sems, out_sems,
):
    pairs, slab, rows_y, lanes = occ_rows.shape
    parts, part_rows = share.shape[1], share.shape[3]
    in_left, in_right, even = sides()
    upper = jnp.where(even, 1, 0)

    copy = pltpu.make_async_copy(ids_hbm, ids, ids_sems.at[0])
    copy.start()
    zero_rims(own)
    zero_rims(once)
    fill_band(band)
    copy.wait()

    def inputs(p):
        return (
            pltpu.make_async_copy(occ.at[ids[0, p]], occ_rows.at[p], in_sems.at[0, p]),
            pltpu.make_async_copy(vir.at[ids[1, p]], vir_rows.at[p], in_sems.at[1, p]),
        )

    def last_output(p):
        return pltpu.make_async_copy(share.at[p], shares.at[p], out_sems.at[0, p])

    def outputs(p):
        return (
            pltpu.make_async_copy(packed.at[p, upper], first.at[p], out_sems.at[1, p]),
            pltpu.make_async_copy(packed.at[p, 1 - upper], second.at[p], out_sems.at[2, p]),
            pltpu.make_async_copy(v0s.at[p], v0_out.at[p], out_sems.at[3, p]),
        )

    for p in range(pairs):
        for copy in inputs(p):
            copy.start()
    line = lax.broadcasted_iota(jnp.int32, ids_tile.shape, 0)
    lane = lax.broadcasted_iota(jnp.int32, ids_tile.shape, 1)
    tile = jnp.zeros(ids_tile.shape, F32)
    for p in range(pairs):
        for j in range(2):
            tile = jnp.where((line == j) & (lane == p), ids[j, p].astype(F32), tile)
    ids_tile[...] = tile.astype(BF16)
    ids_copy = pltpu.make_async_copy(ids_tile, ids_out, ids_sems.at[1])
    ids_copy.start()
    fill_children(fold, 0.5, 0)

    def one_pair(p, carry):
        for copy in inputs(p):
            copy.wait()
        for layer in range(slab):
            own[layer, PAD : PAD + rows_y] = occ_rows[p, layer].astype(F32) * vir_rows[p, layer].astype(F32)

        for row in range(0, rows_y, STEP):
            rows = slice(row, row + STEP)
            for layer in range(slab):
                centre = read(own, layer, row)
                total = stencil(own, layer, row, band[...])
                if layer > 0:
                    total = total + read(own, layer - 1, row)
                if layer < slab - 1:
                    total = total + read(own, layer + 1, row)
                value = W * total
                put(once, layer + 1, row, value)
                v0 = W * (centre + value)
                v0s[p, layer, rows] = v0
                if layer == 0:
                    put(once, 0, row, (W * in_left) * centre)
                    packed[p, 0, 0, rows] = (W * W * centre).astype(BF16)
                    packed[p, 0, 1, rows] = v0.astype(BF16)
                if layer == 1:
                    packed[p, 0, 2, rows] = v0.astype(BF16)
                if layer == slab - 2:
                    packed[p, 1, 2, rows] = v0.astype(BF16)
                if layer == slab - 1:
                    put(once, slab + 1, row, (W * in_right) * centre)
                    packed[p, 1, 0, rows] = (W * W * centre).astype(BF16)
                    packed[p, 1, 1, rows] = v0.astype(BF16)

        for copy in outputs(p):
            copy.start()

        def twice(layer, row):
            if layer == -2:
                return read(once, 0, row)
            if layer == slab + 1:
                return read(once, slab + 1, row)
            at = layer + 1
            total = stencil(once, at, row, band[...])
            if at > 0:
                total = total + read(once, at - 1, row)
            if at < slab + 1:
                total = total + read(once, at + 1, row)
            return total

        for row in range(0, rows_y, STEP):
            for coarse in range(slab // 2 + 2):
                pair_sum = twice(2 * coarse - 2, row) + twice(2 * coarse - 1, row)
                sums[coarse, row : row + STEP] = W * pair_sum

        half = rows_y // 2

        def folded(coarse):
            return sums[coarse, pl.ds(0, half, stride=2), :] + sums[coarse, pl.ds(1, half, stride=2), :]

        def together(left, right):
            both = jnp.concatenate([folded(left), folded(right)], axis=1)
            high, low = high_low(both)
            return dot(high, fold[...]) + dot(low, fold[...])

        outer = together(3, 0)
        edge = outer.astype(BF16)
        lane = lax.broadcasted_iota(jnp.int32, outer.shape, 1)
        rest = pltpu.roll(outer - edge.astype(F32), lanes // 2, 1) * jnp.where(lane < lanes // 2, in_left, in_right)
        own_high, own_low = high_low(together(1, 2) + rest)
        for part in range(parts):
            rows = slice(part * part_rows, (part + 1) * part_rows)
            share[p, part, 0] = own_high[rows]
            share[p, part, 1] = own_low[rows]
            share[p, part, 2] = edge[rows]
        last_output(p).start()
        return carry

    lax.fori_loop(0, pairs, one_pair, 0)
    ids_copy.wait()
    for p in range(pairs):
        for copy in (*outputs(p), last_output(p)):
            copy.wait()


def middle_kernel(*refs):
    parts = len(refs) - 10
    received = refs[:parts]
    modes, table_y, inverse, ids_tile, out = refs[parts : parts + 5]
    source, field_a, field_b, smooth, edge = refs[parts + 5 :]
    slabs, _, part_rows, lanes = received[0].shape
    rows_y = parts * part_rows
    own_part = lax.rem(lax.axis_index("dom"), parts)
    left = lax.broadcasted_iota(jnp.int32, (part_rows, lanes), 1) < lanes // 2
    for ref in (source, field_a, field_b):
        zero_rims(ref)
    for turn in range(parts):
        at = own_part + turn
        at = jnp.where(at >= parts, at - parts, at) * part_rows
        at = pl.multiple_of(at, part_rows)
        ref = received[turn]
        for d in range(slabs):
            value = ref[d, 0].astype(F32) + ref[d, 1].astype(F32)
            before = ref[d - 1, 2].astype(F32) if d > 0 else jnp.zeros_like(value)
            after = ref[d + 1, 2].astype(F32) if d < slabs - 1 else jnp.zeros_like(value)
            source[d, pl.ds(PAD + at, part_rows)] = value + jnp.where(left, before, after)

    half = lanes // 2
    left = lax.broadcasted_iota(jnp.int32, (rows_y, lanes), 1) < half

    def swapped(ref, d):
        return pltpu.roll(read(ref, d, 0, rows_y), half, 1)

    def apply(ref, each):
        zeros = jnp.zeros((rows_y, lanes), F32)
        before, here = zeros, swapped(ref, 0)
        for d in range(slabs):
            after = swapped(ref, d + 1) if d < slabs - 1 else zeros
            total = across(read(ref, d, 0, rows_y), 2) + beside(ref, d, 0, rows_y)
            each(d, total + here + jnp.where(left, before, after))
            before, here = here, after

    apply(source, lambda d, total: put(field_a, d, 0, W * total))

    def to_coarse(d, total):
        smooth[d] = W * (read(source, d, 0, rows_y) + read(field_a, d, 0, rows_y))
        put(field_b, d, 0, W * total)

    apply(field_a, to_coarse)
    pieces = []
    for d in range(slabs):
        even_rows = field_b[d, pl.ds(PAD, rows_y // 2, stride=2), :]
        odd_rows = field_b[d, pl.ds(PAD + 1, rows_y // 2, stride=2), :]
        pieces.append(even_rows + odd_rows)
    spectral = dot_split(jnp.concatenate(pieces, axis=1), modes)
    spectral = dot(table_y[...], spectral, precision=HIGHEST) * inverse[...]
    spread = dot_split(dot(table_y[...], spectral, precision=HIGHEST), modes, ((1,), (1,)))
    for d in range(slabs):
        value = spread[:, d * lanes : (d + 1) * lanes]
        field_b[d, pl.ds(PAD, rows_y // 2, stride=2), :] = value
        field_b[d, pl.ds(PAD + 1, rows_y // 2, stride=2), :] = value
    for d in range(slabs):
        put(field_a, d, 0, smooth[d] + read(field_b, d, 0, rows_y))

    apply(field_a, lambda d, total: put(field_b, d, 0, W * total))
    apply(field_b, lambda d, total: put(field_a, d, 0, W * total + smooth[d]))
    zeros = jnp.zeros((rows_y, lanes), F32)
    before, here = zeros, swapped(field_a, 0)
    for d in range(slabs):
        after = swapped(field_a, d + 1) if d < slabs - 1 else zeros
        edge[d] = jnp.where(left, before, after) - read(field_a, d, 0, rows_y)
        before, here = here, after
    at = pl.multiple_of(own_part * part_rows, part_rows)
    for d in range(slabs):
        high, low = high_low(field_a[d, pl.ds(PAD + at, part_rows)])
        out[d, :part_rows] = high
        out[d, part_rows : 2 * part_rows] = low
        out[d, 2 * part_rows : 3 * part_rows] = edge[d, pl.ds(at, part_rows)].astype(BF16)
        out[d, 3 * part_rows :] = ids_tile[...]


def final_kernel(
    all_occ, all_vir, v0_hbm, first_sent, second_sent, coarse, first, second, out, panel,
    v0, edges, band, spread, identity, wide, start, swept, kept,
    occ, vir, late_vector, late_ids, turned, sums, ids_sem, in_sems, out_sems, late_sems,
):
    pairs, slab, rows_y, lanes = kept.shape
    groups = late_vector.shape[0]
    parts, part_rows = coarse.shape[0] // pairs, (coarse.shape[1] - 16) // 3
    in_left, in_right, even = sides()
    upper = jnp.where(even, 1, 0)

    def inputs(p):
        return (
            pltpu.make_async_copy(v0_hbm.at[p], v0.at[p], in_sems.at[0, p]),
            pltpu.make_async_copy(first_sent.at[p, 0], edges.at[p, upper], in_sems.at[1, p]),
            pltpu.make_async_copy(second_sent.at[p, 0], edges.at[p, 1 - upper], in_sems.at[2, p]),
        )

    def output(p):
        return pltpu.make_async_copy(kept.at[p], out.at[p], out_sems.at[p])

    for p in range(pairs):
        for copy in inputs(p):
            copy.start()
    late = [pltpu.make_async_copy(all_occ, occ, late_sems.at[0]), pltpu.make_async_copy(all_vir, vir, late_sems.at[1])]
    for turn in range(groups):
        late_vector[turn] = coarse[turn, 3 * part_rows :].astype(F32).astype(jnp.int32)
    ids_copy = pltpu.make_async_copy(late_vector, late_ids, ids_sem)
    ids_copy.start()
    fill_band(band)
    fill_children(spread, 1.0, 1)
    line = lax.broadcasted_iota(jnp.int32, identity.shape, 0)
    identity[...] = jnp.where(line == lax.broadcasted_iota(jnp.int32, identity.shape, 1), 1.0, 0.0).astype(BF16)
    zero_rims(start)
    zero_rims(swept)

    def spread_out(p, carry):
        for part in range(parts):
            table = spread[...]
            at = p * parts + part
            own = dot(coarse[at, :part_rows], table) + dot(coarse[at, part_rows : 2 * part_rows], table)
            beyond = own + dot(coarse[at, 2 * part_rows : 3 * part_rows], table)
            for at, value in enumerate((beyond[:, :lanes], own[:, :lanes], own[:, lanes:], beyond[:, lanes:])):
                rows = 2 * part * part_rows
                wide[p, at, pl.ds(rows, part_rows, stride=2), :] = value
                wide[p, at, pl.ds(rows + 1, part_rows, stride=2), :] = value
        return carry

    lax.fori_loop(0, pairs, spread_out, 0)

    def one_pair(p, carry):
        for copy in inputs(p):
            copy.wait()

        @pl.when(p == 0)
        def _():
            for copy in late:
                copy.start()

        def halo(edge, index, row):
            rows = slice(row, row + STEP)
            one, two = first[p, index, rows].astype(F32), second[p, index, rows].astype(F32)
            return jnp.where(even == (edge == 1), one, two)

        for row in range(0, rows_y, STEP):
            rows = slice(row, row + STEP)
            for layer in range(slab):
                value = v0[p, layer, rows]
                if layer == 0:
                    value = value + halo(0, 0, row)
                    v0[p, layer, rows] = value
                if layer == slab - 1:
                    value = value + halo(1, 0, row)
                    v0[p, layer, rows] = value
                put(start, layer + 2, row, value + wide[p, 1 + layer // 2, rows])
            near = halo(0, 1, row) + edges[p, 0, rows].astype(F32) + wide[p, 0, rows]
            put(start, 1, row, in_left * near)
            put(start, 0, row, in_left * (halo(0, 2, row) + wide[p, 0, rows]))
            near = halo(1, 1, row) + edges[p, 1, rows].astype(F32) + wide[p, 3, rows]
            put(start, slab + 2, row, in_right * near)
            put(start, slab + 3, row, in_right * (halo(1, 2, row) + wide[p, 3, rows]))

        def sweep(ref, at, row):
            total = stencil(ref, at, row, band[...])
            return W * (total + read(ref, at - 1, row) + read(ref, at + 1, row))

        for row in range(0, rows_y, STEP):
            put(swept, 0, row, in_left * sweep(start, 1, row))
            for layer in range(slab):
                put(swept, layer + 1, row, sweep(start, layer + 2, row))
            put(swept, slab + 1, row, in_right * sweep(start, slab + 2, row))
        for row in range(0, rows_y, STEP):
            rows = slice(row, row + STEP)
            for layer in range(slab):
                kept[p, layer, rows] = (sweep(swept, layer + 1, row) + v0[p, layer, rows]).astype(BF16)
        output(p).start()
        half = lanes // 2
        for layer in range(slab):
            value = dot(identity[...], kept[p, layer], ((1,), (1,))).astype(BF16)
            column = 2 * layer * rows_y
            turned[p, :, column : column + rows_y] = value[:half]
            turned[p, :, column + rows_y : column + 2 * rows_y] = value[half:]
        return carry

    lax.fori_loop(0, pairs, one_pair, 0)
    ids_copy.wait()
    for copy in late:
        copy.wait()
    half = lanes // 2
    fields = turned[...].reshape(pairs * half, 2 * slab * rows_y)
    count = groups * pairs
    first_row = lax.axis_index("pair") * pairs
    left = lax.broadcasted_iota(jnp.int32, (rows_y, lanes), 1) < half
    diagonal = lax.broadcasted_iota(jnp.int32, (half, 2 * lanes), 0) == lax.rem(
        lax.broadcasted_iota(jnp.int32, (half, 2 * lanes), 1), half
    )

    def density16(p, layer):
        turn, k = p // pairs, lax.rem(p, pairs)
        i, a = late_ids[turn, 0, k], late_ids[turn, 1, k]
        return (occ[i, layer].astype(F32) * vir[a, layer].astype(F32)).astype(BF16)

    def four_rows(turn, carry):
        p = 4 * turn
        pieces = []
        for layer in range(slab):
            upper_row, lower_row = [], []
            for j in (0, 2):
                one, two = density16(p + j, layer), density16(p + j + 1, layer)
                upper_row.append(jnp.where(left, one, pltpu.roll(two, half, 1)))
                lower_row.append(jnp.where(left, pltpu.roll(one, half, 1), two))
            pieces += [jnp.concatenate(upper_row, axis=1), jnp.concatenate(lower_row, axis=1)]
        product = dot(fields, jnp.concatenate(pieces, axis=0))
        row = first_row + p
        row = jnp.where(row >= count, row - count, row) // 2
        for q in range(pairs):
            block = jnp.where(diagonal, product[q * half : (q + 1) * half], 0.0)
            block = jnp.sum(block, axis=0, keepdims=True)
            sums[row, q : q + 1] = block[:, :lanes]
            sums[row + 1, q : q + 1] = block[:, lanes:]
        return carry

    lax.fori_loop(0, count // 4, four_rows, 0)
    scale = 1.0 / float(slab * rows_y * lanes * lax.axis_size("dom"))
    total = scale * sums[...]
    left = lax.broadcasted_iota(jnp.int32, total.shape, 2) < half
    panel[0] = jnp.sum(jnp.where(left, total, 0.0), axis=2)
    panel[1] = jnp.sum(jnp.where(left, 0.0, total), axis=2)
    for p in range(pairs):
        output(p).wait()


def sine_table(length):
    steps = np.arange(length, dtype=np.float64) + 1.0
    return math.sqrt(2.0 / (length + 1)) * np.sin(np.pi * steps[:, None] * steps[None, :] / (length + 1))


def eigenvalues(length):
    return 2.0 - 2.0 * np.cos(np.pi * (np.arange(length, dtype=np.float64) + 1.0) / (length + 1))


def coarse_tables(size_x, size_y, size_z):
    sine_x, sine_z = sine_table(size_x), sine_table(size_z)
    modes = np.einsum("dk,zl->dzkl", sine_x, np.repeat(sine_z, 2, axis=0))
    modes = np.repeat(modes[:, None], 2, axis=1).reshape(size_x * 4 * size_z, size_x * size_z)
    high = modes.astype(BF16)
    low = (modes - high.astype(np.float64)).astype(BF16)
    total = eigenvalues(size_y)[:, None, None] + eigenvalues(size_x)[None, :, None] + eigenvalues(size_z)[None, None, :]
    inverse = (0.5 / total).reshape(size_y, size_x * size_z)
    return jnp.asarray(np.stack([high, low])), jnp.asarray(sine_table(size_y), F32), jnp.asarray(inverse, F32)


def shards(occupied, virtual, pair_ids):
    orbitals, slab, rows_y, lanes = occupied.shape
    pairs = pair_ids.shape[0]
    slabs = lax.axis_size("dom")
    parts = slabs // pairs
    half_y = rows_y // 2
    part_rows = half_y // parts
    padded_y = rows_y + 2 * PAD
    ids = pair_ids.T

    hbm, vmem = pl.BlockSpec(memory_space=pltpu.HBM), pl.BlockSpec(memory_space=pltpu.VMEM)
    anywhere = pl.BlockSpec(memory_space=pl.ANY)
    in_hbm = lambda x: pltpu.with_memory_space_constraint(x, pltpu.HBM)
    halo = (pairs, 3, rows_y, lanes)
    own = (pairs, slab, rows_y, lanes)
    share = (pairs, parts, 3, part_rows, lanes)
    tile = (16, lanes)
    shares, first, second, v0, ids_tile = pl.pallas_call(
        source_kernel,
        in_specs=[hbm, hbm, hbm],
        out_specs=[hbm] * 5,
        out_shape=[
            pltpu.HBM(share, BF16),
            pltpu.HBM(halo, BF16),
            pltpu.HBM(halo, BF16),
            pltpu.HBM(own, F32),
            pltpu.HBM(tile, BF16),
        ],
        scratch_shapes=[
            pltpu.SMEM(ids.shape, jnp.int32),
            pltpu.VMEM(own, BF16),
            pltpu.VMEM(own, BF16),
            pltpu.VMEM((2 * lanes, lanes), BF16),
            pltpu.VMEM((2 * lanes, lanes), BF16),
            pltpu.VMEM((slab, padded_y, lanes), F32),
            pltpu.VMEM((slab + 2, padded_y, lanes), F32),
            pltpu.VMEM(own, F32),
            pltpu.VMEM((slab // 2 + 2, rows_y, lanes), F32),
            pltpu.VMEM((pairs, 2, 3, rows_y, lanes), BF16),
            pltpu.VMEM(share, BF16),
            pltpu.VMEM(tile, BF16),
            pltpu.SemaphoreType.DMA((2,)),
            pltpu.SemaphoreType.DMA((2, pairs)),
            pltpu.SemaphoreType.DMA((4, pairs)),
        ],
        compiler_params=pltpu.CompilerParams(vmem_limit_bytes=32 * MIB),
        name="source",
    )(in_hbm(ids), in_hbm(occupied), in_hbm(virtual))

    inside = [(i, i ^ 1) for i in range(slabs)]
    outside = [(i, i + 1) for i in range(1, slabs - 1, 2)]
    outside = outside + [(j, i) for i, j in outside]
    first_halo = lax.ppermute(first, "dom", inside)
    second_halo = lax.ppermute(second, "dom", outside)
    groups = lax.axis_size("pair")
    perm = [(d * groups + (g + d) % groups, d * groups + g) for d in range(slabs) for g in range(groups)]
    ids_tile = lax.ppermute(ids_tile, ("dom", "pair"), perm)

    received = lax.all_to_all(shares.reshape(slabs, 3, part_rows, lanes), "dom", 0, 0)
    views = [received]
    for turn in range(1, parts):
        perm = [(g * parts + (h + turn) % parts, g * parts + h) for g in range(slabs // parts) for h in range(parts)]
        views.append(lax.ppermute(received, "dom", perm))
    tables = coarse_tables(slabs, half_y // 2, lanes // 4)
    padded = pltpu.VMEM((slabs, half_y + 2 * PAD, lanes), F32)
    plain = pltpu.VMEM((slabs, half_y, lanes), F32)
    smoothed = pl.pallas_call(
        middle_kernel,
        in_specs=[vmem] * (parts + 4),
        out_specs=vmem,
        out_shape=jax.ShapeDtypeStruct((slabs, 3 * part_rows + 16, lanes), BF16),
        scratch_shapes=[padded, padded, padded, plain, plain],
        compiler_params=pltpu.CompilerParams(vmem_limit_bytes=32 * MIB),
        name="middle",
    )(*views, *tables, ids_tile)
    returned = lax.all_to_all(smoothed, "dom", 0, 0)

    count = groups * pairs
    potentials, panel = pl.pallas_call(
        final_kernel,
        in_specs=[hbm] * 5 + [vmem] * 3,
        out_specs=[hbm, vmem],
        out_shape=[pltpu.HBM(own, BF16), jax.ShapeDtypeStruct((2, count // 2, pairs), F32)],
        scratch_shapes=[
            pltpu.VMEM(own, F32),
            pltpu.VMEM((pairs, 2, rows_y, lanes), BF16),
            pltpu.VMEM((2 * lanes, lanes), BF16),
            pltpu.VMEM((lanes, 2 * lanes), BF16),
            pltpu.VMEM((lanes, lanes), BF16),
            pltpu.VMEM((pairs, 4, rows_y, lanes), F32),
            pltpu.VMEM((slab + 4, padded_y, lanes), F32),
            pltpu.VMEM((slab + 2, padded_y, lanes), F32),
            pltpu.VMEM(own, BF16),
            pltpu.VMEM(occupied.shape, BF16),
            pltpu.VMEM(virtual.shape, BF16),
            pltpu.VMEM((groups,) + tile, jnp.int32),
            pltpu.SMEM((groups,) + tile, jnp.int32),
            pltpu.VMEM((pairs, lanes // 2, 2 * slab * rows_y), BF16),
            pltpu.VMEM((count // 2, pairs, lanes), F32),
            pltpu.SemaphoreType.DMA,
            pltpu.SemaphoreType.DMA((3, pairs)),
            pltpu.SemaphoreType.DMA((pairs,)),
            pltpu.SemaphoreType.DMA((2,)),
        ],
        compiler_params=pltpu.CompilerParams(vmem_limit_bytes=24 * MIB),
        name="final",
    )(*[in_hbm(x) for x in (occupied, virtual, v0, first, second)], returned, first_halo, second_halo)
    panel = jnp.swapaxes(panel, 0, 1).reshape(slabs, count // slabs, pairs)
    return potentials, jnp.sum(lax.all_to_all(panel, "dom", 0, 0), axis=0)


def solution(mesh):
    placed = (P(None, "dom", None, None), P(None, "dom", None, None), P("pair", None))
    return jax.shard_map(
        shards,
        mesh=mesh,
        in_specs=placed,
        out_specs=(P("pair", "dom", None, None), P("dom", "pair")),
        check_vma=False,
    )
```

```python
import math

import jax
import jax.numpy as jnp
import numpy as np
from jax import lax
from jax.experimental import pallas as pl
from jax.experimental.pallas import tpu as pltpu
from jax.sharding import PartitionSpec as P

W = 0.8 / 6.0
CENTRE = 1.5
PAD = 8
STEP = 64
F32 = jnp.float32
BF16 = jnp.bfloat16
MIB = 1024 * 1024
HIGHEST = lax.Precision.HIGHEST


def dot(a, b, contract=((1,), (0,)), precision=None):
    return lax.dot_general(a, b, (contract, ((), ())), precision=precision, preferred_element_type=F32)


def high_low(x):
    high = x.astype(BF16)
    return high, (x - high.astype(F32)).astype(BF16)


def dot_split(a, table, contract=((1,), (0,))):
    high, low = high_low(a)
    return dot(high, table[0], contract) + (dot(low, table[0], contract) + dot(high, table[1], contract))


def zero_rims(ref):
    zeros = jnp.zeros((ref.shape[0], PAD, ref.shape[2]), F32)
    ref[:, :PAD] = zeros
    ref[:, ref.shape[1] - PAD :] = zeros


def read(ref, layer, row, rows=STEP):
    return ref[layer, PAD + row : PAD + row + rows, :]


def put(ref, layer, row, value):
    ref[layer, PAD + row : PAD + row + value.shape[0]] = value


def across(centre, blocks=1):
    lane = lax.broadcasted_iota(jnp.int32, centre.shape, 1)
    width = centre.shape[1] // blocks
    first = lane % width == 0 if blocks > 1 else lane == 0
    last = lane % width == width - 1 if blocks > 1 else lane == width - 1
    lower = jnp.where(first, 0.0, pltpu.roll(centre, 1, 1))
    upper = jnp.where(last, 0.0, pltpu.roll(centre, centre.shape[1] - 1, 1))
    return CENTRE * centre + lower + upper


def across_by_matrix(centre, band):
    high, low = high_low(centre)
    return dot(jnp.concatenate([high, low], axis=1), band)


def beside(ref, layer, row, rows=STEP):
    return read(ref, layer, row - 1, rows) + read(ref, layer, row + 1, rows)


def stencil(ref, layer, row, band):
    centre = read(ref, layer, row)
    along_z = across(centre) if layer % 2 else across_by_matrix(centre, band)
    return along_z + beside(ref, layer, row)


def fill_band(ref):
    lanes = ref.shape[1]
    line = lax.rem(lax.broadcasted_iota(jnp.int32, ref.shape, 0), lanes)
    apart = jnp.abs(line - lax.broadcasted_iota(jnp.int32, ref.shape, 1))
    ref[...] = jnp.where(apart == 0, CENTRE, jnp.where(apart == 1, 1.0, 0.0)).astype(BF16)


def fill_children(ref, value, axis):
    child = lax.broadcasted_iota(jnp.int32, ref.shape, axis)
    parent = lax.broadcasted_iota(jnp.int32, ref.shape, 1 - axis)
    ref[...] = jnp.where(child // 2 == parent, value, 0.0).astype(BF16)


def sides(axis="dom"):
    me, count = lax.axis_index(axis), lax.axis_size(axis)
    below = jnp.where(me == 0, 0.0, 1.0).astype(F32)
    above = jnp.where(me == count - 1, 0.0, 1.0).astype(F32)
    return below, above, lax.rem(me, 2) == 0


def source_kernel(
    ids_hbm, occ, vir, shares, first, second, v0_out, ids_out,
    ids, occ_rows, vir_rows, band, fold, own, once, beyond, v0s, sums, packed, share, ids_tile, ids_sems, in_sems, out_sems,
):
    pairs, slab, rows_y, lanes = occ_rows.shape
    parts, part_rows = share.shape[1], share.shape[3]
    in_left, in_right, even = sides()
    upper = jnp.where(even, 1, 0)

    copy = pltpu.make_async_copy(ids_hbm, ids, ids_sems.at[0])
    copy.start()
    zero_rims(own)
    zero_rims(once)
    fill_band(band)
    copy.wait()

    def inputs(p):
        return (
            pltpu.make_async_copy(occ.at[ids[0, p]], occ_rows.at[p], in_sems.at[0, p]),
            pltpu.make_async_copy(vir.at[ids[1, p]], vir_rows.at[p], in_sems.at[1, p]),
        )

    def last_output(p):
        return pltpu.make_async_copy(share.at[p], shares.at[p], out_sems.at[0, p])

    def outputs(p):
        return (
            pltpu.make_async_copy(packed.at[p, upper], first.at[p], out_sems.at[1, p]),
            pltpu.make_async_copy(packed.at[p, 1 - upper], second.at[p], out_sems.at[2, p]),
            pltpu.make_async_copy(v0s.at[p], v0_out.at[p], out_sems.at[3, p]),
        )

    for p in range(pairs):
        for copy in inputs(p):
            copy.start()
    line = lax.broadcasted_iota(jnp.int32, ids_tile.shape, 0)
    lane = lax.broadcasted_iota(jnp.int32, ids_tile.shape, 1)
    tile = jnp.zeros(ids_tile.shape, F32)
    for p in range(pairs):
        for j in range(2):
            tile = jnp.where((line == j) & (lane == p), ids[j, p].astype(F32), tile)
    ids_tile[...] = tile.astype(BF16)
    ids_copy = pltpu.make_async_copy(ids_tile, ids_out, ids_sems.at[1])
    ids_copy.start()
    fill_children(fold, 0.5, 0)

    def one_pair(p, carry):
        for copy in inputs(p):
            copy.wait()
        for layer in range(slab):
            own[layer, PAD : PAD + rows_y] = occ_rows[p, layer].astype(F32) * vir_rows[p, layer].astype(F32)

        for row in range(0, rows_y, STEP):
            rows = slice(row, row + STEP)
            for layer in range(slab):
                centre = read(own, layer, row)
                total = stencil(own, layer, row, band[...])
                if layer == 0:
                    beyond[0, rows] = (W * in_left) * total
                if layer == slab - 1:
                    beyond[1, rows] = (W * in_right) * total
                if layer > 0:
                    total = total + read(own, layer - 1, row)
                if layer < slab - 1:
                    total = total + read(own, layer + 1, row)
                value = W * total
                put(once, layer + 1, row, value)
                v0 = W * (centre + value)
                v0s[p, layer, rows] = v0
                if layer == 0:
                    put(once, 0, row, (W * in_left) * centre)
                    packed[p, 0, 0, rows] = (W * W * centre).astype(BF16)
                    packed[p, 0, 1, rows] = v0.astype(BF16)
                if layer == 1:
                    packed[p, 0, 2, rows] = v0.astype(BF16)
                if layer == slab - 2:
                    packed[p, 1, 2, rows] = v0.astype(BF16)
                if layer == slab - 1:
                    put(once, slab + 1, row, (W * in_right) * centre)
                    packed[p, 1, 0, rows] = (W * W * centre).astype(BF16)
                    packed[p, 1, 1, rows] = v0.astype(BF16)

        for copy in outputs(p):
            copy.start()

        def twice(layer, row):
            if layer == -2:
                return read(once, 0, row)
            if layer == slab + 1:
                return read(once, slab + 1, row)
            if layer == -1:
                return beyond[0, row : row + STEP] + read(once, 1, row)
            if layer == slab:
                return beyond[1, row : row + STEP] + read(once, slab, row)
            at = layer + 1
            return stencil(once, at, row, band[...]) + read(once, at - 1, row) + read(once, at + 1, row)

        for row in range(0, rows_y, STEP):
            for coarse in range(slab // 2 + 2):
                pair_sum = twice(2 * coarse - 2, row) + twice(2 * coarse - 1, row)
                sums[coarse, row : row + STEP] = W * pair_sum

        half = rows_y // 2

        def folded(coarse):
            return sums[coarse, pl.ds(0, half, stride=2), :] + sums[coarse, pl.ds(1, half, stride=2), :]

        def together(left, right):
            both = jnp.concatenate([folded(left), folded(right)], axis=1)
            high, low = high_low(both)
            return dot(high, fold[...]) + dot(low, fold[...])

        outer = together(3, 0)
        edge = outer.astype(BF16)
        lane = lax.broadcasted_iota(jnp.int32, outer.shape, 1)
        rest = pltpu.roll(outer - edge.astype(F32), lanes // 2, 1) * jnp.where(lane < lanes // 2, in_left, in_right)
        own_high, own_low = high_low(together(1, 2) + rest)
        for part in range(parts):
            rows = slice(part * part_rows, (part + 1) * part_rows)
            share[p, part, 0] = own_high[rows]
            share[p, part, 1] = own_low[rows]
            share[p, part, 2] = edge[rows]
        last_output(p).start()
        return carry

    lax.fori_loop(0, pairs, one_pair, 0)
    ids_copy.wait()
    for p in range(pairs):
        for copy in (*outputs(p), last_output(p)):
            copy.wait()


def middle_kernel(*refs):
    parts = len(refs) - 10
    received = refs[:parts]
    modes, table_y, inverse, ids_tile, out = refs[parts : parts + 5]
    source, field_a, field_b, smooth, edge = refs[parts + 5 :]
    slabs, _, part_rows, lanes = received[0].shape
    rows_y = parts * part_rows
    own_part = lax.rem(lax.axis_index("dom"), parts)
    left = lax.broadcasted_iota(jnp.int32, (part_rows, lanes), 1) < lanes // 2
    for ref in (source, field_a, field_b):
        zero_rims(ref)
    for turn in range(parts):
        at = own_part + turn
        at = jnp.where(at >= parts, at - parts, at) * part_rows
        at = pl.multiple_of(at, part_rows)
        ref = received[turn]
        for d in range(slabs):
            value = ref[d, 0].astype(F32) + ref[d, 1].astype(F32)
            before = ref[d - 1, 2].astype(F32) if d > 0 else jnp.zeros_like(value)
            after = ref[d + 1, 2].astype(F32) if d < slabs - 1 else jnp.zeros_like(value)
            source[d, pl.ds(PAD + at, part_rows)] = value + jnp.where(left, before, after)

    half = lanes // 2
    left = lax.broadcasted_iota(jnp.int32, (rows_y, lanes), 1) < half

    def swapped(ref, d):
        return pltpu.roll(read(ref, d, 0, rows_y), half, 1)

    def apply(ref, each):
        zeros = jnp.zeros((rows_y, lanes), F32)
        before, here = zeros, swapped(ref, 0)
        for d in range(slabs):
            after = swapped(ref, d + 1) if d < slabs - 1 else zeros
            total = across(read(ref, d, 0, rows_y), 2) + beside(ref, d, 0, rows_y)
            each(d, total + here + jnp.where(left, before, after))
            before, here = here, after

    apply(source, lambda d, total: put(field_a, d, 0, W * total))

    def to_coarse(d, total):
        smooth[d] = W * (read(source, d, 0, rows_y) + read(field_a, d, 0, rows_y))
        put(field_b, d, 0, W * total)

    apply(field_a, to_coarse)
    pieces = []
    for d in range(slabs):
        even_rows = field_b[d, pl.ds(PAD, rows_y // 2, stride=2), :]
        odd_rows = field_b[d, pl.ds(PAD + 1, rows_y // 2, stride=2), :]
        pieces.append(even_rows + odd_rows)
    spectral = dot_split(jnp.concatenate(pieces, axis=1), modes)
    spectral = dot(table_y[...], spectral, precision=HIGHEST) * inverse[...]
    spread = dot_split(dot(table_y[...], spectral, precision=HIGHEST), modes, ((1,), (1,)))
    for d in range(slabs):
        value = spread[:, d * lanes : (d + 1) * lanes]
        field_b[d, pl.ds(PAD, rows_y // 2, stride=2), :] = value
        field_b[d, pl.ds(PAD + 1, rows_y // 2, stride=2), :] = value
    for d in range(slabs):
        put(field_a, d, 0, smooth[d] + read(field_b, d, 0, rows_y))

    apply(field_a, lambda d, total: put(field_b, d, 0, W * total))
    apply(field_b, lambda d, total: put(field_a, d, 0, W * total + smooth[d]))
    zeros = jnp.zeros((rows_y, lanes), F32)
    before, here = zeros, swapped(field_a, 0)
    for d in range(slabs):
        after = swapped(field_a, d + 1) if d < slabs - 1 else zeros
        edge[d] = jnp.where(left, before, after) - read(field_a, d, 0, rows_y)
        before, here = here, after
    at = pl.multiple_of(own_part * part_rows, part_rows)
    for d in range(slabs):
        high, low = high_low(field_a[d, pl.ds(PAD + at, part_rows)])
        out[d, :part_rows] = high
        out[d, part_rows : 2 * part_rows] = low
        out[d, 2 * part_rows : 3 * part_rows] = edge[d, pl.ds(at, part_rows)].astype(BF16)
        out[d, 3 * part_rows :] = ids_tile[...]


def final_kernel(
    all_occ, all_vir, v0_hbm, first_sent, second_sent, coarse, first, second, out, panel,
    v0, edges, band, spread, identity, wide, start, swept, kept,
    occ, vir, late_vector, late_ids, turned, sums, ids_sem, in_sems, out_sems, late_sems,
):
    pairs, slab, rows_y, lanes = kept.shape
    groups = late_vector.shape[0]
    parts, part_rows = coarse.shape[0] // pairs, (coarse.shape[1] - 16) // 3
    in_left, in_right, even = sides()
    upper = jnp.where(even, 1, 0)

    def inputs(p):
        return (
            pltpu.make_async_copy(v0_hbm.at[p], v0.at[p], in_sems.at[0, p]),
            pltpu.make_async_copy(first_sent.at[p, 0], edges.at[p, upper], in_sems.at[1, p]),
            pltpu.make_async_copy(second_sent.at[p, 0], edges.at[p, 1 - upper], in_sems.at[2, p]),
        )

    def output(p):
        return pltpu.make_async_copy(kept.at[p], out.at[p], out_sems.at[p])

    for p in range(pairs):
        for copy in inputs(p):
            copy.start()
    late = [pltpu.make_async_copy(all_occ, occ, late_sems.at[0]), pltpu.make_async_copy(all_vir, vir, late_sems.at[1])]
    for turn in range(groups):
        late_vector[turn] = coarse[turn, 3 * part_rows :].astype(F32).astype(jnp.int32)
    ids_copy = pltpu.make_async_copy(late_vector, late_ids, ids_sem)
    ids_copy.start()
    fill_band(band)
    fill_children(spread, 1.0, 1)
    line = lax.broadcasted_iota(jnp.int32, identity.shape, 0)
    identity[...] = jnp.where(line == lax.broadcasted_iota(jnp.int32, identity.shape, 1), 1.0, 0.0).astype(BF16)
    zero_rims(start)
    zero_rims(swept)

    def spread_out(p, carry):
        for part in range(parts):
            table = spread[...]
            at = p * parts + part
            own = dot(coarse[at, :part_rows], table) + dot(coarse[at, part_rows : 2 * part_rows], table)
            beyond = own + dot(coarse[at, 2 * part_rows : 3 * part_rows], table)
            for at, value in enumerate((beyond[:, :lanes], own[:, :lanes], own[:, lanes:], beyond[:, lanes:])):
                rows = 2 * part * part_rows
                wide[p, at, pl.ds(rows, part_rows, stride=2), :] = value
                wide[p, at, pl.ds(rows + 1, part_rows, stride=2), :] = value
        return carry

    lax.fori_loop(0, pairs, spread_out, 0)

    def one_pair(p, carry):
        for copy in inputs(p):
            copy.wait()

        @pl.when(p == 0)
        def _():
            for copy in late:
                copy.start()

        def halo(edge, index, row):
            rows = slice(row, row + STEP)
            one, two = first[p, index, rows].astype(F32), second[p, index, rows].astype(F32)
            return jnp.where(even == (edge == 1), one, two)

        for row in range(0, rows_y, STEP):
            rows = slice(row, row + STEP)
            for layer in range(slab):
                value = v0[p, layer, rows]
                if layer == 0:
                    value = value + halo(0, 0, row)
                    v0[p, layer, rows] = value
                if layer == slab - 1:
                    value = value + halo(1, 0, row)
                    v0[p, layer, rows] = value
                put(start, layer + 2, row, value + wide[p, 1 + layer // 2, rows])
            near = halo(0, 1, row) + edges[p, 0, rows].astype(F32) + wide[p, 0, rows]
            put(start, 1, row, in_left * near)
            put(start, 0, row, in_left * (halo(0, 2, row) + wide[p, 0, rows]))
            near = halo(1, 1, row) + edges[p, 1, rows].astype(F32) + wide[p, 3, rows]
            put(start, slab + 2, row, in_right * near)
            put(start, slab + 3, row, in_right * (halo(1, 2, row) + wide[p, 3, rows]))

        def sweep(ref, at, row):
            total = stencil(ref, at, row, band[...])
            return W * (total + read(ref, at - 1, row) + read(ref, at + 1, row))

        for row in range(0, rows_y, STEP):
            put(swept, 0, row, in_left * sweep(start, 1, row))
            for layer in range(slab):
                put(swept, layer + 1, row, sweep(start, layer + 2, row))
            put(swept, slab + 1, row, in_right * sweep(start, slab + 2, row))
        for row in range(0, rows_y, STEP):
            rows = slice(row, row + STEP)
            for layer in range(slab):
                kept[p, layer, rows] = (sweep(swept, layer + 1, row) + v0[p, layer, rows]).astype(BF16)
        output(p).start()
        half = lanes // 2
        for layer in range(slab):
            value = dot(identity[...], kept[p, layer], ((1,), (1,))).astype(BF16)
            column = 2 * layer * rows_y
            turned[p, :, column : column + rows_y] = value[:half]
            turned[p, :, column + rows_y : column + 2 * rows_y] = value[half:]
        return carry

    lax.fori_loop(0, pairs, one_pair, 0)
    ids_copy.wait()
    for copy in late:
        copy.wait()
    half = lanes // 2
    fields = turned[...].reshape(pairs * half, 2 * slab * rows_y)
    count = groups * pairs
    first_row = lax.axis_index("pair") * pairs
    left = lax.broadcasted_iota(jnp.int32, (rows_y, lanes), 1) < half
    diagonal = lax.broadcasted_iota(jnp.int32, (half, 2 * lanes), 0) == lax.rem(
        lax.broadcasted_iota(jnp.int32, (half, 2 * lanes), 1), half
    )

    def density16(p, layer):
        turn, k = p // pairs, lax.rem(p, pairs)
        i, a = late_ids[turn, 0, k], late_ids[turn, 1, k]
        return (occ[i, layer].astype(F32) * vir[a, layer].astype(F32)).astype(BF16)

    def four_rows(turn, carry):
        p = 4 * turn
        pieces = []
        for layer in range(slab):
            upper_row, lower_row = [], []
            for j in (0, 2):
                one, two = density16(p + j, layer), density16(p + j + 1, layer)
                upper_row.append(jnp.where(left, one, pltpu.roll(two, half, 1)))
                lower_row.append(jnp.where(left, pltpu.roll(one, half, 1), two))
            pieces += [jnp.concatenate(upper_row, axis=1), jnp.concatenate(lower_row, axis=1)]
        product = dot(fields, jnp.concatenate(pieces, axis=0))
        row = first_row + p
        row = jnp.where(row >= count, row - count, row) // 2
        for q in range(pairs):
            block = jnp.where(diagonal, product[q * half : (q + 1) * half], 0.0)
            block = jnp.sum(block, axis=0, keepdims=True)
            sums[row, q : q + 1] = block[:, :lanes]
            sums[row + 1, q : q + 1] = block[:, lanes:]
        return carry

    lax.fori_loop(0, count // 4, four_rows, 0)
    scale = 1.0 / float(slab * rows_y * lanes * lax.axis_size("dom"))
    total = scale * sums[...]
    left = lax.broadcasted_iota(jnp.int32, total.shape, 2) < half
    panel[0] = jnp.sum(jnp.where(left, total, 0.0), axis=2)
    panel[1] = jnp.sum(jnp.where(left, 0.0, total), axis=2)
    for p in range(pairs):
        output(p).wait()


def sine_table(length):
    steps = np.arange(length, dtype=np.float64) + 1.0
    return math.sqrt(2.0 / (length + 1)) * np.sin(np.pi * steps[:, None] * steps[None, :] / (length + 1))


def eigenvalues(length):
    return 2.0 - 2.0 * np.cos(np.pi * (np.arange(length, dtype=np.float64) + 1.0) / (length + 1))


def coarse_tables(size_x, size_y, size_z):
    sine_x, sine_z = sine_table(size_x), sine_table(size_z)
    modes = np.einsum("dk,zl->dzkl", sine_x, np.repeat(sine_z, 2, axis=0))
    modes = np.repeat(modes[:, None], 2, axis=1).reshape(size_x * 4 * size_z, size_x * size_z)
    high = modes.astype(BF16)
    low = (modes - high.astype(np.float64)).astype(BF16)
    total = eigenvalues(size_y)[:, None, None] + eigenvalues(size_x)[None, :, None] + eigenvalues(size_z)[None, None, :]
    inverse = (0.5 / total).reshape(size_y, size_x * size_z)
    return jnp.asarray(np.stack([high, low])), jnp.asarray(sine_table(size_y), F32), jnp.asarray(inverse, F32)


def shards(occupied, virtual, pair_ids):
    orbitals, slab, rows_y, lanes = occupied.shape
    pairs = pair_ids.shape[0]
    slabs = lax.axis_size("dom")
    parts = slabs // pairs
    half_y = rows_y // 2
    part_rows = half_y // parts
    padded_y = rows_y + 2 * PAD
    ids = pair_ids.T

    hbm, vmem = pl.BlockSpec(memory_space=pltpu.HBM), pl.BlockSpec(memory_space=pltpu.VMEM)
    anywhere = pl.BlockSpec(memory_space=pl.ANY)
    in_hbm = lambda x: pltpu.with_memory_space_constraint(x, pltpu.HBM)
    halo = (pairs, 3, rows_y, lanes)
    own = (pairs, slab, rows_y, lanes)
    share = (pairs, parts, 3, part_rows, lanes)
    tile = (16, lanes)
    shares, first, second, v0, ids_tile = pl.pallas_call(
        source_kernel,
        in_specs=[hbm, hbm, hbm],
        out_specs=[hbm] * 5,
        out_shape=[
            pltpu.HBM(share, BF16),
            pltpu.HBM(halo, BF16),
            pltpu.HBM(halo, BF16),
            pltpu.HBM(own, F32),
            pltpu.HBM(tile, BF16),
        ],
        scratch_shapes=[
            pltpu.SMEM(ids.shape, jnp.int32),
            pltpu.VMEM(own, BF16),
            pltpu.VMEM(own, BF16),
            pltpu.VMEM((2 * lanes, lanes), BF16),
            pltpu.VMEM((2 * lanes, lanes), BF16),
            pltpu.VMEM((slab, padded_y, lanes), F32),
            pltpu.VMEM((slab + 2, padded_y, lanes), F32),
            pltpu.VMEM((2, rows_y, lanes), F32),
            pltpu.VMEM(own, F32),
            pltpu.VMEM((slab // 2 + 2, rows_y, lanes), F32),
            pltpu.VMEM((pairs, 2, 3, rows_y, lanes), BF16),
            pltpu.VMEM(share, BF16),
            pltpu.VMEM(tile, BF16),
            pltpu.SemaphoreType.DMA((2,)),
            pltpu.SemaphoreType.DMA((2, pairs)),
            pltpu.SemaphoreType.DMA((4, pairs)),
        ],
        compiler_params=pltpu.CompilerParams(vmem_limit_bytes=32 * MIB),
        name="source",
    )(in_hbm(ids), in_hbm(occupied), in_hbm(virtual))

    inside = [(i, i ^ 1) for i in range(slabs)]
    outside = [(i, i + 1) for i in range(1, slabs - 1, 2)]
    outside = outside + [(j, i) for i, j in outside]
    first_halo = lax.ppermute(first, "dom", inside)
    second_halo = lax.ppermute(second, "dom", outside)
    groups = lax.axis_size("pair")
    perm = [(d * groups + (g + d) % groups, d * groups + g) for d in range(slabs) for g in range(groups)]
    ids_tile = lax.ppermute(ids_tile, ("dom", "pair"), perm)

    received = lax.all_to_all(shares.reshape(slabs, 3, part_rows, lanes), "dom", 0, 0)
    views = [received]
    for turn in range(1, parts):
        perm = [(g * parts + (h + turn) % parts, g * parts + h) for g in range(slabs // parts) for h in range(parts)]
        views.append(lax.ppermute(received, "dom", perm))
    tables = coarse_tables(slabs, half_y // 2, lanes // 4)
    padded = pltpu.VMEM((slabs, half_y + 2 * PAD, lanes), F32)
    plain = pltpu.VMEM((slabs, half_y, lanes), F32)
    smoothed = pl.pallas_call(
        middle_kernel,
        in_specs=[vmem] * (parts + 4),
        out_specs=vmem,
        out_shape=jax.ShapeDtypeStruct((slabs, 3 * part_rows + 16, lanes), BF16),
        scratch_shapes=[padded, padded, padded, plain, plain],
        compiler_params=pltpu.CompilerParams(vmem_limit_bytes=32 * MIB),
        name="middle",
    )(*views, *tables, ids_tile)
    returned = lax.all_to_all(smoothed, "dom", 0, 0)

    count = groups * pairs
    potentials, panel = pl.pallas_call(
        final_kernel,
        in_specs=[hbm] * 5 + [vmem] * 3,
        out_specs=[hbm, vmem],
        out_shape=[pltpu.HBM(own, BF16), jax.ShapeDtypeStruct((2, count // 2, pairs), F32)],
        scratch_shapes=[
            pltpu.VMEM(own, F32),
            pltpu.VMEM((pairs, 2, rows_y, lanes), BF16),
            pltpu.VMEM((2 * lanes, lanes), BF16),
            pltpu.VMEM((lanes, 2 * lanes), BF16),
            pltpu.VMEM((lanes, lanes), BF16),
            pltpu.VMEM((pairs, 4, rows_y, lanes), F32),
            pltpu.VMEM((slab + 4, padded_y, lanes), F32),
            pltpu.VMEM((slab + 2, padded_y, lanes), F32),
            pltpu.VMEM(own, BF16),
            pltpu.VMEM(occupied.shape, BF16),
            pltpu.VMEM(virtual.shape, BF16),
            pltpu.VMEM((groups,) + tile, jnp.int32),
            pltpu.SMEM((groups,) + tile, jnp.int32),
            pltpu.VMEM((pairs, lanes // 2, 2 * slab * rows_y), BF16),
            pltpu.VMEM((count // 2, pairs, lanes), F32),
            pltpu.SemaphoreType.DMA,
            pltpu.SemaphoreType.DMA((3, pairs)),
            pltpu.SemaphoreType.DMA((pairs,)),
            pltpu.SemaphoreType.DMA((2,)),
        ],
        compiler_params=pltpu.CompilerParams(vmem_limit_bytes=24 * MIB),
        name="final",
    )(*[in_hbm(x) for x in (occupied, virtual, v0, first, second)], returned, first_halo, second_halo)
    panel = jnp.swapaxes(panel, 0, 1).reshape(slabs, count // slabs, pairs)
    return potentials, jnp.sum(lax.all_to_all(panel, "dom", 0, 0), axis=0)


def solution(mesh):
    placed = (P(None, "dom", None, None), P(None, "dom", None, None), P("pair", None))
    return jax.shard_map(
        shards,
        mesh=mesh,
        in_specs=placed,
        out_specs=(P("pair", "dom", None, None), P("dom", "pair")),
        check_vma=False,
    )
```

```python
import math

import jax
import jax.numpy as jnp
import numpy as np
from jax import lax
from jax.experimental import pallas as pl
from jax.experimental.pallas import tpu as pltpu
from jax.sharding import PartitionSpec as P

W = 0.8 / 6.0
CENTRE = 1.5
PAD = 8
STEP = 64
F32 = jnp.float32
BF16 = jnp.bfloat16
MIB = 1024 * 1024
HIGHEST = lax.Precision.HIGHEST


def dot(a, b, contract=((1,), (0,)), precision=None):
    return lax.dot_general(a, b, (contract, ((), ())), precision=precision, preferred_element_type=F32)


def high_low(x):
    high = x.astype(BF16)
    return high, (x - high.astype(F32)).astype(BF16)


def dot_split(a, table, contract=((1,), (0,))):
    high, low = high_low(a)
    return dot(high, table[0], contract) + (dot(low, table[0], contract) + dot(high, table[1], contract))


def zero_rims(ref):
    zeros = jnp.zeros((ref.shape[0], PAD, ref.shape[2]), F32)
    ref[:, :PAD] = zeros
    ref[:, ref.shape[1] - PAD :] = zeros


def read(ref, layer, row, rows=STEP):
    return ref[layer, PAD + row : PAD + row + rows, :]


def put(ref, layer, row, value):
    ref[layer, PAD + row : PAD + row + value.shape[0]] = value


def across(centre, blocks=1):
    lane = lax.broadcasted_iota(jnp.int32, centre.shape, 1)
    width = centre.shape[1] // blocks
    first = lane % width == 0 if blocks > 1 else lane == 0
    last = lane % width == width - 1 if blocks > 1 else lane == width - 1
    lower = jnp.where(first, 0.0, pltpu.roll(centre, 1, 1))
    upper = jnp.where(last, 0.0, pltpu.roll(centre, centre.shape[1] - 1, 1))
    return CENTRE * centre + lower + upper


def across_by_matrix(centre, band):
    high, low = high_low(centre)
    return dot(jnp.concatenate([high, low], axis=1), band)


def beside(ref, layer, row, rows=STEP):
    return read(ref, layer, row - 1, rows) + read(ref, layer, row + 1, rows)


def stencil(ref, layer, row, band):
    centre = read(ref, layer, row)
    along_z = across(centre) if layer % 2 else across_by_matrix(centre, band)
    return along_z + beside(ref, layer, row)


def fill_band(ref):
    lanes = ref.shape[1]
    line = lax.rem(lax.broadcasted_iota(jnp.int32, ref.shape, 0), lanes)
    apart = jnp.abs(line - lax.broadcasted_iota(jnp.int32, ref.shape, 1))
    ref[...] = jnp.where(apart == 0, CENTRE, jnp.where(apart == 1, 1.0, 0.0)).astype(BF16)


def fill_children(ref, value, axis):
    child = lax.broadcasted_iota(jnp.int32, ref.shape, axis)
    parent = lax.broadcasted_iota(jnp.int32, ref.shape, 1 - axis)
    ref[...] = jnp.where(child // 2 == parent, value, 0.0).astype(BF16)


def sides(axis="dom"):
    me, count = lax.axis_index(axis), lax.axis_size(axis)
    below = jnp.where(me == 0, 0.0, 1.0).astype(F32)
    above = jnp.where(me == count - 1, 0.0, 1.0).astype(F32)
    return below, above, lax.rem(me, 2) == 0


def source_kernel(
    ids_hbm, occ, vir, shares, first, second, v0_out,
    ids, occ_rows, vir_rows, band, fold, own, once, beyond, v0s, sums, packed, share, ids_sem, in_sems, out_sems,
):
    pairs, slab, rows_y, lanes = occ_rows.shape
    parts, part_rows = share.shape[1], share.shape[3]
    in_left, in_right, even = sides()
    upper = jnp.where(even, 1, 0)

    copy = pltpu.make_async_copy(ids_hbm, ids, ids_sem)
    copy.start()
    zero_rims(own)
    zero_rims(once)
    fill_band(band)
    copy.wait()

    def inputs(p):
        return (
            pltpu.make_async_copy(occ.at[ids[0, p]], occ_rows.at[p], in_sems.at[0, p]),
            pltpu.make_async_copy(vir.at[ids[1, p]], vir_rows.at[p], in_sems.at[1, p]),
        )

    def last_output(p):
        return pltpu.make_async_copy(share.at[p], shares.at[p], out_sems.at[0, p])

    def outputs(p):
        return (
            pltpu.make_async_copy(packed.at[p, upper], first.at[p], out_sems.at[1, p]),
            pltpu.make_async_copy(packed.at[p, 1 - upper], second.at[p], out_sems.at[2, p]),
            pltpu.make_async_copy(v0s.at[p], v0_out.at[p], out_sems.at[3, p]),
        )

    for p in range(pairs):
        for copy in inputs(p):
            copy.start()
    fill_children(fold, 0.5, 0)

    def one_pair(p, carry):
        for copy in inputs(p):
            copy.wait()
        for layer in range(slab):
            own[layer, PAD : PAD + rows_y] = occ_rows[p, layer].astype(F32) * vir_rows[p, layer].astype(F32)

        for row in range(0, rows_y, STEP):
            rows = slice(row, row + STEP)
            for layer in range(slab):
                centre = read(own, layer, row)
                total = stencil(own, layer, row, band[...])
                if layer == 0:
                    beyond[0, rows] = (W * in_left) * total
                if layer == slab - 1:
                    beyond[1, rows] = (W * in_right) * total
                if layer > 0:
                    total = total + read(own, layer - 1, row)
                if layer < slab - 1:
                    total = total + read(own, layer + 1, row)
                value = W * total
                put(once, layer + 1, row, value)
                v0 = W * (centre + value)
                v0s[p, layer, rows] = v0
                if layer == 0:
                    put(once, 0, row, (W * in_left) * centre)
                    packed[p, 0, 0, rows] = (W * W * centre).astype(BF16)
                    packed[p, 0, 1, rows] = v0.astype(BF16)
                if layer == 1:
                    packed[p, 0, 2, rows] = v0.astype(BF16)
                if layer == slab - 2:
                    packed[p, 1, 2, rows] = v0.astype(BF16)
                if layer == slab - 1:
                    put(once, slab + 1, row, (W * in_right) * centre)
                    packed[p, 1, 0, rows] = (W * W * centre).astype(BF16)
                    packed[p, 1, 1, rows] = v0.astype(BF16)

        for copy in outputs(p):
            copy.start()

        def twice(layer, row):
            if layer == -2:
                return read(once, 0, row)
            if layer == slab + 1:
                return read(once, slab + 1, row)
            if layer == -1:
                return beyond[0, row : row + STEP] + read(once, 1, row)
            if layer == slab:
                return beyond[1, row : row + STEP] + read(once, slab, row)
            at = layer + 1
            return stencil(once, at, row, band[...]) + read(once, at - 1, row) + read(once, at + 1, row)

        for row in range(0, rows_y, STEP):
            for coarse in range(slab // 2 + 2):
                pair_sum = twice(2 * coarse - 2, row) + twice(2 * coarse - 1, row)
                sums[coarse, row : row + STEP] = W * pair_sum

        half = rows_y // 2

        def folded(coarse):
            return sums[coarse, pl.ds(0, half, stride=2), :] + sums[coarse, pl.ds(1, half, stride=2), :]

        def together(left, right):
            both = jnp.concatenate([folded(left), folded(right)], axis=1)
            high, low = high_low(both)
            return dot(high, fold[...]) + dot(low, fold[...])

        outer = together(3, 0)
        edge = outer.astype(BF16)
        lane = lax.broadcasted_iota(jnp.int32, outer.shape, 1)
        rest = pltpu.roll(outer - edge.astype(F32), lanes // 2, 1) * jnp.where(lane < lanes // 2, in_left, in_right)
        own_high, own_low = high_low(together(1, 2) + rest)
        for part in range(parts):
            rows = slice(part * part_rows, (part + 1) * part_rows)
            share[p, part, 0] = own_high[rows]
            share[p, part, 1] = own_low[rows]
            share[p, part, 2] = edge[rows]
        last_output(p).start()
        return carry

    lax.fori_loop(0, pairs, one_pair, 0)
    for p in range(pairs):
        for copy in (*outputs(p), last_output(p)):
            copy.wait()


def middle_kernel(*refs):
    parts = len(refs) - 9
    received = refs[:parts]
    modes, table_y, inverse, out = refs[parts : parts + 4]
    source, field_a, field_b, smooth, edge = refs[parts + 4 :]
    slabs, _, part_rows, lanes = received[0].shape
    rows_y = parts * part_rows
    own_part = lax.rem(lax.axis_index("dom"), parts)
    left = lax.broadcasted_iota(jnp.int32, (part_rows, lanes), 1) < lanes // 2
    for ref in (source, field_a, field_b):
        zero_rims(ref)
    for turn in range(parts):
        at = own_part + turn
        at = jnp.where(at >= parts, at - parts, at) * part_rows
        at = pl.multiple_of(at, part_rows)
        ref = received[turn]
        for d in range(slabs):
            value = ref[d, 0].astype(F32) + ref[d, 1].astype(F32)
            before = ref[d - 1, 2].astype(F32) if d > 0 else jnp.zeros_like(value)
            after = ref[d + 1, 2].astype(F32) if d < slabs - 1 else jnp.zeros_like(value)
            source[d, pl.ds(PAD + at, part_rows)] = value + jnp.where(left, before, after)

    half = lanes // 2
    left = lax.broadcasted_iota(jnp.int32, (rows_y, lanes), 1) < half

    def swapped(ref, d):
        return pltpu.roll(read(ref, d, 0, rows_y), half, 1)

    def apply(ref, each):
        zeros = jnp.zeros((rows_y, lanes), F32)
        before, here = zeros, swapped(ref, 0)
        for d in range(slabs):
            after = swapped(ref, d + 1) if d < slabs - 1 else zeros
            total = across(read(ref, d, 0, rows_y), 2) + beside(ref, d, 0, rows_y)
            each(d, total + here + jnp.where(left, before, after))
            before, here = here, after

    apply(source, lambda d, total: put(field_a, d, 0, W * total))

    def to_coarse(d, total):
        smooth[d] = W * (read(source, d, 0, rows_y) + read(field_a, d, 0, rows_y))
        put(field_b, d, 0, W * total)

    apply(field_a, to_coarse)
    pieces = []
    for d in range(slabs):
        even_rows = field_b[d, pl.ds(PAD, rows_y // 2, stride=2), :]
        odd_rows = field_b[d, pl.ds(PAD + 1, rows_y // 2, stride=2), :]
        pieces.append(even_rows + odd_rows)
    spectral = dot_split(jnp.concatenate(pieces, axis=1), modes)
    spectral = dot(table_y[...], spectral, precision=HIGHEST) * inverse[...]
    spread = dot_split(dot(table_y[...], spectral, precision=HIGHEST), modes, ((1,), (1,)))
    for d in range(slabs):
        value = spread[:, d * lanes : (d + 1) * lanes]
        field_b[d, pl.ds(PAD, rows_y // 2, stride=2), :] = value
        field_b[d, pl.ds(PAD + 1, rows_y // 2, stride=2), :] = value
    for d in range(slabs):
        put(field_a, d, 0, smooth[d] + read(field_b, d, 0, rows_y))

    apply(field_a, lambda d, total: put(field_b, d, 0, W * total))
    apply(field_b, lambda d, total: put(field_a, d, 0, W * total + smooth[d]))
    zeros = jnp.zeros((rows_y, lanes), F32)
    before, here = zeros, swapped(field_a, 0)
    for d in range(slabs):
        after = swapped(field_a, d + 1) if d < slabs - 1 else zeros
        edge[d] = jnp.where(left, before, after) - read(field_a, d, 0, rows_y)
        before, here = here, after
    at = pl.multiple_of(own_part * part_rows, part_rows)
    for d in range(slabs):
        high, low = high_low(field_a[d, pl.ds(PAD + at, part_rows)])
        out[d, :part_rows] = high
        out[d, part_rows : 2 * part_rows] = low
        out[d, 2 * part_rows :] = edge[d, pl.ds(at, part_rows)].astype(BF16)


def final_kernel(
    all_ids, all_occ, all_vir, v0_hbm, first_sent, second_sent, coarse, first, second, out, panel,
    v0, edges, band, spread, identity, wide, start, swept, kept,
    occ, vir, ids, turned, sums, in_sems, out_sems, late_sems,
):
    pairs, slab, rows_y, lanes = kept.shape
    parts, part_rows = coarse.shape[0] // pairs, coarse.shape[1] // 3
    in_left, in_right, even = sides()
    upper = jnp.where(even, 1, 0)

    def inputs(p):
        return (
            pltpu.make_async_copy(v0_hbm.at[p], v0.at[p], in_sems.at[0, p]),
            pltpu.make_async_copy(first_sent.at[p, 0], edges.at[p, upper], in_sems.at[1, p]),
            pltpu.make_async_copy(second_sent.at[p, 0], edges.at[p, 1 - upper], in_sems.at[2, p]),
        )

    def output(p):
        return pltpu.make_async_copy(kept.at[p], out.at[p], out_sems.at[p])

    for p in range(pairs):
        for copy in inputs(p):
            copy.start()
    late = [
        pltpu.make_async_copy(all_ids, ids, late_sems.at[0]),
        pltpu.make_async_copy(all_occ, occ, late_sems.at[1]),
        pltpu.make_async_copy(all_vir, vir, late_sems.at[2]),
    ]
    fill_band(band)
    fill_children(spread, 1.0, 1)
    line = lax.broadcasted_iota(jnp.int32, identity.shape, 0)
    identity[...] = jnp.where(line == lax.broadcasted_iota(jnp.int32, identity.shape, 1), 1.0, 0.0).astype(BF16)
    zero_rims(start)
    zero_rims(swept)

    def spread_out(p, carry):
        for part in range(parts):
            table = spread[...]
            at = p * parts + part
            own = dot(coarse[at, :part_rows], table) + dot(coarse[at, part_rows : 2 * part_rows], table)
            beyond = own + dot(coarse[at, 2 * part_rows :], table)
            for at, value in enumerate((beyond[:, :lanes], own[:, :lanes], own[:, lanes:], beyond[:, lanes:])):
                rows = 2 * part * part_rows
                wide[p, at, pl.ds(rows, part_rows, stride=2), :] = value
                wide[p, at, pl.ds(rows + 1, part_rows, stride=2), :] = value
        return carry

    lax.fori_loop(0, pairs, spread_out, 0)

    def one_pair(p, carry):
        for copy in inputs(p):
            copy.wait()

        @pl.when(p == 0)
        def _():
            for copy in late:
                copy.start()

        def halo(edge, index, row):
            rows = slice(row, row + STEP)
            one, two = first[p, index, rows].astype(F32), second[p, index, rows].astype(F32)
            return jnp.where(even == (edge == 1), one, two)

        for row in range(0, rows_y, STEP):
            rows = slice(row, row + STEP)
            for layer in range(slab):
                value = v0[p, layer, rows]
                if layer == 0:
                    value = value + halo(0, 0, row)
                    v0[p, layer, rows] = value
                if layer == slab - 1:
                    value = value + halo(1, 0, row)
                    v0[p, layer, rows] = value
                put(start, layer + 2, row, value + wide[p, 1 + layer // 2, rows])
            near = halo(0, 1, row) + edges[p, 0, rows].astype(F32) + wide[p, 0, rows]
            put(start, 1, row, in_left * near)
            put(start, 0, row, in_left * (halo(0, 2, row) + wide[p, 0, rows]))
            near = halo(1, 1, row) + edges[p, 1, rows].astype(F32) + wide[p, 3, rows]
            put(start, slab + 2, row, in_right * near)
            put(start, slab + 3, row, in_right * (halo(1, 2, row) + wide[p, 3, rows]))

        def sweep(ref, at, row):
            total = stencil(ref, at, row, band[...])
            return W * (total + read(ref, at - 1, row) + read(ref, at + 1, row))

        for row in range(0, rows_y, STEP):
            put(swept, 0, row, in_left * sweep(start, 1, row))
            for layer in range(slab):
                put(swept, layer + 1, row, sweep(start, layer + 2, row))
            put(swept, slab + 1, row, in_right * sweep(start, slab + 2, row))
        for row in range(0, rows_y, STEP):
            rows = slice(row, row + STEP)
            for layer in range(slab):
                kept[p, layer, rows] = (sweep(swept, layer + 1, row) + v0[p, layer, rows]).astype(BF16)
        output(p).start()
        half = lanes // 2
        for layer in range(slab):
            value = dot(identity[...], kept[p, layer], ((1,), (1,))).astype(BF16)
            column = 2 * layer * rows_y
            turned[p, :, column : column + rows_y] = value[:half]
            turned[p, :, column + rows_y : column + 2 * rows_y] = value[half:]
        return carry

    lax.fori_loop(0, pairs, one_pair, 0)
    for copy in late:
        copy.wait()
    half = lanes // 2
    fields = turned[...].reshape(pairs * half, 2 * slab * rows_y)
    count = ids.shape[0] // 2 * pairs
    first_row = lax.axis_index("pair") * pairs
    left = lax.broadcasted_iota(jnp.int32, (rows_y, lanes), 1) < half
    diagonal = lax.broadcasted_iota(jnp.int32, (half, 2 * lanes), 0) == lax.rem(
        lax.broadcasted_iota(jnp.int32, (half, 2 * lanes), 1), half
    )

    def density16(p, layer):
        turn, k = p // pairs, lax.rem(p, pairs)
        i, a = ids[2 * turn, k], ids[2 * turn + 1, k]
        return (occ[i, layer].astype(F32) * vir[a, layer].astype(F32)).astype(BF16)

    def four_rows(turn, carry):
        p = 4 * turn
        pieces = []
        for layer in range(slab):
            upper_row, lower_row = [], []
            for j in (0, 2):
                one, two = density16(p + j, layer), density16(p + j + 1, layer)
                upper_row.append(jnp.where(left, one, pltpu.roll(two, half, 1)))
                lower_row.append(jnp.where(left, pltpu.roll(one, half, 1), two))
            pieces += [jnp.concatenate(upper_row, axis=1), jnp.concatenate(lower_row, axis=1)]
        product = dot(fields, jnp.concatenate(pieces, axis=0))
        row = first_row + p
        row = jnp.where(row >= count, row - count, row) // 2
        for q in range(pairs):
            block = jnp.where(diagonal, product[q * half : (q + 1) * half], 0.0)
            block = jnp.sum(block, axis=0, keepdims=True)
            sums[row, q : q + 1] = block[:, :lanes]
            sums[row + 1, q : q + 1] = block[:, lanes:]
        return carry

    lax.fori_loop(0, count // 4, four_rows, 0)
    scale = 1.0 / float(slab * rows_y * lanes * lax.axis_size("dom"))
    total = scale * sums[...]
    left = lax.broadcasted_iota(jnp.int32, total.shape, 2) < half
    panel[0] = jnp.sum(jnp.where(left, total, 0.0), axis=2)
    panel[1] = jnp.sum(jnp.where(left, 0.0, total), axis=2)
    for p in range(pairs):
        output(p).wait()


def sine_table(length):
    steps = np.arange(length, dtype=np.float64) + 1.0
    return math.sqrt(2.0 / (length + 1)) * np.sin(np.pi * steps[:, None] * steps[None, :] / (length + 1))


def eigenvalues(length):
    return 2.0 - 2.0 * np.cos(np.pi * (np.arange(length, dtype=np.float64) + 1.0) / (length + 1))


def coarse_tables(size_x, size_y, size_z):
    sine_x, sine_z = sine_table(size_x), sine_table(size_z)
    modes = np.einsum("dk,zl->dzkl", sine_x, np.repeat(sine_z, 2, axis=0))
    modes = np.repeat(modes[:, None], 2, axis=1).reshape(size_x * 4 * size_z, size_x * size_z)
    high = modes.astype(BF16)
    low = (modes - high.astype(np.float64)).astype(BF16)
    total = eigenvalues(size_y)[:, None, None] + eigenvalues(size_x)[None, :, None] + eigenvalues(size_z)[None, None, :]
    inverse = (0.5 / total).reshape(size_y, size_x * size_z)
    return jnp.asarray(np.stack([high, low])), jnp.asarray(sine_table(size_y), F32), jnp.asarray(inverse, F32)


def shards(occupied, virtual, pair_ids):
    orbitals, slab, rows_y, lanes = occupied.shape
    pairs = pair_ids.shape[0]
    slabs = lax.axis_size("dom")
    parts = slabs // pairs
    half_y = rows_y // 2
    part_rows = half_y // parts
    padded_y = rows_y + 2 * PAD
    ids = pair_ids.T

    hbm, vmem = pl.BlockSpec(memory_space=pltpu.HBM), pl.BlockSpec(memory_space=pltpu.VMEM)
    anywhere = pl.BlockSpec(memory_space=pl.ANY)
    in_hbm = lambda x: pltpu.with_memory_space_constraint(x, pltpu.HBM)
    halo = (pairs, 3, rows_y, lanes)
    own = (pairs, slab, rows_y, lanes)
    share = (pairs, parts, 3, part_rows, lanes)
    shares, first, second, v0 = pl.pallas_call(
        source_kernel,
        in_specs=[hbm, hbm, hbm],
        out_specs=[hbm] * 4,
        out_shape=[
            pltpu.HBM(share, BF16),
            pltpu.HBM(halo, BF16),
            pltpu.HBM(halo, BF16),
            pltpu.HBM(own, F32),
        ],
        scratch_shapes=[
            pltpu.SMEM(ids.shape, jnp.int32),
            pltpu.VMEM(own, BF16),
            pltpu.VMEM(own, BF16),
            pltpu.VMEM((2 * lanes, lanes), BF16),
            pltpu.VMEM((2 * lanes, lanes), BF16),
            pltpu.VMEM((slab, padded_y, lanes), F32),
            pltpu.VMEM((slab + 2, padded_y, lanes), F32),
            pltpu.VMEM((2, rows_y, lanes), F32),
            pltpu.VMEM(own, F32),
            pltpu.VMEM((slab // 2 + 2, rows_y, lanes), F32),
            pltpu.VMEM((pairs, 2, 3, rows_y, lanes), BF16),
            pltpu.VMEM(share, BF16),
            pltpu.SemaphoreType.DMA,
            pltpu.SemaphoreType.DMA((2, pairs)),
            pltpu.SemaphoreType.DMA((4, pairs)),
        ],
        compiler_params=pltpu.CompilerParams(vmem_limit_bytes=32 * MIB),
        name="source",
    )(in_hbm(ids), in_hbm(occupied), in_hbm(virtual))

    inside = [(i, i ^ 1) for i in range(slabs)]
    outside = [(i, i + 1) for i in range(1, slabs - 1, 2)]
    outside = outside + [(j, i) for i, j in outside]
    first_halo = lax.ppermute(first, "dom", inside)
    second_halo = lax.ppermute(second, "dom", outside)
    received = lax.all_to_all(shares.reshape(slabs, 3, part_rows, lanes), "dom", 0, 0)
    views = [received]
    for turn in range(1, parts):
        perm = [(g * parts + (h + turn) % parts, g * parts + h) for g in range(slabs // parts) for h in range(parts)]
        views.append(lax.ppermute(received, "dom", perm))
    tables = coarse_tables(slabs, half_y // 2, lanes // 4)
    padded = pltpu.VMEM((slabs, half_y + 2 * PAD, lanes), F32)
    plain = pltpu.VMEM((slabs, half_y, lanes), F32)
    smoothed = pl.pallas_call(
        middle_kernel,
        in_specs=[vmem] * (parts + 3),
        out_specs=vmem,
        out_shape=jax.ShapeDtypeStruct((slabs, 3 * part_rows, lanes), BF16),
        scratch_shapes=[padded, padded, padded, plain, plain],
        compiler_params=pltpu.CompilerParams(vmem_limit_bytes=32 * MIB),
        name="middle",
    )(*views, *tables)
    groups = lax.axis_size("pair")
    late_ids, smoothed = lax.optimization_barrier((ids, smoothed))
    turns = [[((g + turn) % groups, g) for g in range(groups)] for turn in range(1, groups)]
    all_ids = jnp.concatenate([ids] + [lax.ppermute(late_ids, "pair", perm) for perm in turns], axis=0)
    returned = lax.all_to_all(smoothed, "dom", 0, 0)

    count = groups * pairs
    potentials, panel = pl.pallas_call(
        final_kernel,
        in_specs=[anywhere] + [hbm] * 5 + [vmem] * 3,
        out_specs=[hbm, vmem],
        out_shape=[pltpu.HBM(own, BF16), jax.ShapeDtypeStruct((2, count // 2, pairs), F32)],
        scratch_shapes=[
            pltpu.VMEM(own, F32),
            pltpu.VMEM((pairs, 2, rows_y, lanes), BF16),
            pltpu.VMEM((2 * lanes, lanes), BF16),
            pltpu.VMEM((lanes, 2 * lanes), BF16),
            pltpu.VMEM((lanes, lanes), BF16),
            pltpu.VMEM((pairs, 4, rows_y, lanes), F32),
            pltpu.VMEM((slab + 4, padded_y, lanes), F32),
            pltpu.VMEM((slab + 2, padded_y, lanes), F32),
            pltpu.VMEM(own, BF16),
            pltpu.VMEM(occupied.shape, BF16),
            pltpu.VMEM(virtual.shape, BF16),
            pltpu.SMEM(all_ids.shape, jnp.int32),
            pltpu.VMEM((pairs, lanes // 2, 2 * slab * rows_y), BF16),
            pltpu.VMEM((count // 2, pairs, lanes), F32),
            pltpu.SemaphoreType.DMA((3, pairs)),
            pltpu.SemaphoreType.DMA((pairs,)),
            pltpu.SemaphoreType.DMA((3,)),
        ],
        compiler_params=pltpu.CompilerParams(vmem_limit_bytes=24 * MIB),
        name="final",
    )(all_ids, *[in_hbm(x) for x in (occupied, virtual, v0, first, second)], returned, first_halo, second_halo)
    panel = jnp.swapaxes(panel, 0, 1).reshape(slabs, count // slabs, pairs)
    return potentials, jnp.sum(lax.all_to_all(panel, "dom", 0, 0), axis=0)


def solution(mesh):
    placed = (P(None, "dom", None, None), P(None, "dom", None, None), P("pair", None))
    return jax.shard_map(
        shards,
        mesh=mesh,
        in_specs=placed,
        out_specs=(P("pair", "dom", None, None), P("dom", "pair")),
        check_vma=False,
    )
```

```python
import math

import jax
import jax.numpy as jnp
import numpy as np
from jax import lax
from jax.experimental import pallas as pl
from jax.experimental.pallas import tpu as pltpu
from jax.sharding import PartitionSpec as P

W = 0.8 / 6.0
CENTRE = 1.5
PAD = 8
STEP = 64
F32 = jnp.float32
BF16 = jnp.bfloat16
MIB = 1024 * 1024
HIGHEST = lax.Precision.HIGHEST


def dot(a, b, contract=((1,), (0,)), precision=None):
    return lax.dot_general(a, b, (contract, ((), ())), precision=precision, preferred_element_type=F32)


def high_low(x):
    high = x.astype(BF16)
    return high, (x - high.astype(F32)).astype(BF16)


def dot_split(a, table, contract=((1,), (0,))):
    high, low = high_low(a)
    return dot(high, table[0], contract) + (dot(low, table[0], contract) + dot(high, table[1], contract))


def zero_rims(ref):
    zeros = jnp.zeros((ref.shape[0], PAD, ref.shape[2]), F32)
    ref[:, :PAD] = zeros
    ref[:, ref.shape[1] - PAD :] = zeros


def read(ref, layer, row, rows=STEP):
    return ref[layer, PAD + row : PAD + row + rows, :]


def put(ref, layer, row, value):
    ref[layer, PAD + row : PAD + row + value.shape[0]] = value


def across(centre, blocks=1):
    lane = lax.broadcasted_iota(jnp.int32, centre.shape, 1)
    width = centre.shape[1] // blocks
    first = lane % width == 0 if blocks > 1 else lane == 0
    last = lane % width == width - 1 if blocks > 1 else lane == width - 1
    lower = jnp.where(first, 0.0, pltpu.roll(centre, 1, 1))
    upper = jnp.where(last, 0.0, pltpu.roll(centre, centre.shape[1] - 1, 1))
    return CENTRE * centre + lower + upper


def across_by_matrix(centre, band):
    high, low = high_low(centre)
    return dot(jnp.concatenate([high, low], axis=1), band)


def beside(ref, layer, row, rows=STEP):
    return read(ref, layer, row - 1, rows) + read(ref, layer, row + 1, rows)


def stencil(ref, layer, row, band):
    centre = read(ref, layer, row)
    along_z = across(centre) if layer % 2 else across_by_matrix(centre, band)
    return along_z + beside(ref, layer, row)


def fill_band(ref):
    lanes = ref.shape[1]
    line = lax.rem(lax.broadcasted_iota(jnp.int32, ref.shape, 0), lanes)
    apart = jnp.abs(line - lax.broadcasted_iota(jnp.int32, ref.shape, 1))
    ref[...] = jnp.where(apart == 0, CENTRE, jnp.where(apart == 1, 1.0, 0.0)).astype(BF16)


def fill_children(ref, value, axis):
    child = lax.broadcasted_iota(jnp.int32, ref.shape, axis)
    parent = lax.broadcasted_iota(jnp.int32, ref.shape, 1 - axis)
    ref[...] = jnp.where(child // 2 == parent, value, 0.0).astype(BF16)


def sides(axis="dom"):
    me, count = lax.axis_index(axis), lax.axis_size(axis)
    below = jnp.where(me == 0, 0.0, 1.0).astype(F32)
    above = jnp.where(me == count - 1, 0.0, 1.0).astype(F32)
    return below, above, lax.rem(me, 2) == 0


def source_kernel(
    ids_hbm, occ, vir, shares, first, second, v0_out,
    ids, occ_rows, vir_rows, band, fold, own, once, beyond, v0s, sums, packed, share, ids_sem, in_sems, out_sems,
):
    pairs, slab, rows_y, lanes = occ_rows.shape
    parts, part_rows = share.shape[1], share.shape[3]
    in_left, in_right, even = sides()
    upper = jnp.where(even, 1, 0)

    copy = pltpu.make_async_copy(ids_hbm, ids, ids_sem)
    copy.start()
    zero_rims(own)
    zero_rims(once)
    fill_band(band)
    copy.wait()

    def inputs(p):
        return (
            pltpu.make_async_copy(occ.at[ids[0, p]], occ_rows.at[p], in_sems.at[0, p]),
            pltpu.make_async_copy(vir.at[ids[1, p]], vir_rows.at[p], in_sems.at[1, p]),
        )

    def last_output(p):
        return pltpu.make_async_copy(share.at[p], shares.at[p], out_sems.at[0, p])

    def outputs(p):
        return (
            pltpu.make_async_copy(packed.at[p, upper], first.at[p], out_sems.at[1, p]),
            pltpu.make_async_copy(packed.at[p, 1 - upper], second.at[p], out_sems.at[2, p]),
            pltpu.make_async_copy(v0s.at[p], v0_out.at[p], out_sems.at[3, p]),
        )

    for p in range(pairs):
        for copy in inputs(p):
            copy.start()
    fill_children(fold, 0.5, 0)

    def one_pair(p, carry):
        for copy in inputs(p):
            copy.wait()
        for layer in range(slab):
            own[layer, PAD : PAD + rows_y] = occ_rows[p, layer].astype(F32) * vir_rows[p, layer].astype(F32)

        for row in range(0, rows_y, STEP):
            rows = slice(row, row + STEP)
            for layer in range(slab):
                centre = read(own, layer, row)
                total = stencil(own, layer, row, band[...])
                if layer == 0:
                    beyond[0, rows] = (W * in_left) * total
                if layer == slab - 1:
                    beyond[1, rows] = (W * in_right) * total
                if layer > 0:
                    total = total + read(own, layer - 1, row)
                if layer < slab - 1:
                    total = total + read(own, layer + 1, row)
                value = W * total
                put(once, layer + 1, row, value)
                v0 = W * (centre + value)
                v0s[p, layer, rows] = v0
                if layer == 0:
                    put(once, 0, row, (W * in_left) * centre)
                    packed[p, 0, 0, rows] = (W * W * centre).astype(BF16)
                    packed[p, 0, 1, rows] = v0.astype(BF16)
                if layer == 1:
                    packed[p, 0, 2, rows] = v0.astype(BF16)
                if layer == slab - 2:
                    packed[p, 1, 2, rows] = v0.astype(BF16)
                if layer == slab - 1:
                    put(once, slab + 1, row, (W * in_right) * centre)
                    packed[p, 1, 0, rows] = (W * W * centre).astype(BF16)
                    packed[p, 1, 1, rows] = v0.astype(BF16)

        for copy in outputs(p):
            copy.start()

        def twice(layer, row):
            if layer == -2:
                return read(once, 0, row)
            if layer == slab + 1:
                return read(once, slab + 1, row)
            if layer == -1:
                return beyond[0, row : row + STEP] + read(once, 1, row)
            if layer == slab:
                return beyond[1, row : row + STEP] + read(once, slab, row)
            at = layer + 1
            return stencil(once, at, row, band[...]) + read(once, at - 1, row) + read(once, at + 1, row)

        for row in range(0, rows_y, STEP):
            for coarse in range(slab // 2 + 2):
                pair_sum = twice(2 * coarse - 2, row) + twice(2 * coarse - 1, row)
                sums[coarse, row : row + STEP] = W * pair_sum

        half = rows_y // 2

        def folded(coarse):
            return sums[coarse, pl.ds(0, half, stride=2), :] + sums[coarse, pl.ds(1, half, stride=2), :]

        def together(left, right):
            both = jnp.concatenate([folded(left), folded(right)], axis=1)
            high, low = high_low(both)
            return dot(high, fold[...]) + dot(low, fold[...])

        outer = together(3, 0)
        edge = outer.astype(BF16)
        lane = lax.broadcasted_iota(jnp.int32, outer.shape, 1)
        rest = pltpu.roll(outer - edge.astype(F32), lanes // 2, 1) * jnp.where(lane < lanes // 2, in_left, in_right)
        own_high, own_low = high_low(together(1, 2) + rest)
        for part in range(parts):
            rows = slice(part * part_rows, (part + 1) * part_rows)
            share[p, part, 0] = own_high[rows]
            share[p, part, 1] = own_low[rows]
            share[p, part, 2] = edge[rows]
        last_output(p).start()
        return carry

    lax.fori_loop(0, pairs, one_pair, 0)
    for p in range(pairs):
        for copy in (*outputs(p), last_output(p)):
            copy.wait()


def middle_kernel(*refs):
    parts = len(refs) - 9
    received = refs[:parts]
    modes, table_y, inverse, out = refs[parts : parts + 4]
    source, field_a, field_b, smooth, edge = refs[parts + 4 :]
    slabs, _, part_rows, lanes = received[0].shape
    rows_y = parts * part_rows
    own_part = lax.rem(lax.axis_index("dom"), parts)
    left = lax.broadcasted_iota(jnp.int32, (part_rows, lanes), 1) < lanes // 2
    for ref in (source, field_a, field_b):
        zero_rims(ref)
    for turn in range(parts):
        at = own_part + turn
        at = jnp.where(at >= parts, at - parts, at) * part_rows
        at = pl.multiple_of(at, part_rows)
        ref = received[turn]
        for d in range(slabs):
            value = ref[d, 0].astype(F32) + ref[d, 1].astype(F32)
            before = ref[d - 1, 2].astype(F32) if d > 0 else jnp.zeros_like(value)
            after = ref[d + 1, 2].astype(F32) if d < slabs - 1 else jnp.zeros_like(value)
            source[d, pl.ds(PAD + at, part_rows)] = value + jnp.where(left, before, after)

    half = lanes // 2
    left = lax.broadcasted_iota(jnp.int32, (rows_y, lanes), 1) < half

    def swapped(ref, d):
        return pltpu.roll(read(ref, d, 0, rows_y), half, 1)

    def apply(ref, each):
        zeros = jnp.zeros((rows_y, lanes), F32)
        before, here = zeros, swapped(ref, 0)
        for d in range(slabs):
            after = swapped(ref, d + 1) if d < slabs - 1 else zeros
            total = across(read(ref, d, 0, rows_y), 2) + beside(ref, d, 0, rows_y)
            each(d, total + here + jnp.where(left, before, after))
            before, here = here, after

    apply(source, lambda d, total: put(field_a, d, 0, W * total))

    def to_coarse(d, total):
        smooth[d] = W * (read(source, d, 0, rows_y) + read(field_a, d, 0, rows_y))
        put(field_b, d, 0, W * total)

    apply(field_a, to_coarse)
    pieces = []
    for d in range(slabs):
        even_rows = field_b[d, pl.ds(PAD, rows_y // 2, stride=2), :]
        odd_rows = field_b[d, pl.ds(PAD + 1, rows_y // 2, stride=2), :]
        pieces.append(even_rows + odd_rows)
    spectral = dot_split(jnp.concatenate(pieces, axis=1), modes)
    spectral = dot(table_y[...], spectral, precision=HIGHEST) * inverse[...]
    spread = dot_split(dot(table_y[...], spectral, precision=HIGHEST), modes, ((1,), (1,)))
    for d in range(slabs):
        value = spread[:, d * lanes : (d + 1) * lanes]
        field_b[d, pl.ds(PAD, rows_y // 2, stride=2), :] = value
        field_b[d, pl.ds(PAD + 1, rows_y // 2, stride=2), :] = value
    for d in range(slabs):
        put(field_a, d, 0, smooth[d] + read(field_b, d, 0, rows_y))

    apply(field_a, lambda d, total: put(field_b, d, 0, W * total))
    apply(field_b, lambda d, total: put(field_a, d, 0, W * total + smooth[d]))
    zeros = jnp.zeros((rows_y, lanes), F32)
    before, here = zeros, swapped(field_a, 0)
    for d in range(slabs):
        after = swapped(field_a, d + 1) if d < slabs - 1 else zeros
        edge[d] = jnp.where(left, before, after) - read(field_a, d, 0, rows_y)
        before, here = here, after
    at = pl.multiple_of(own_part * part_rows, part_rows)
    for d in range(slabs):
        high, low = high_low(field_a[d, pl.ds(PAD + at, part_rows)])
        out[d, :part_rows] = high
        out[d, part_rows : 2 * part_rows] = low
        out[d, 2 * part_rows :] = edge[d, pl.ds(at, part_rows)].astype(BF16)


def final_kernel(
    all_ids, all_occ, all_vir, v0_hbm, first_sent, second_sent, coarse, first, second, out, panel,
    v0, edges, band, spread, identity, wide, start, swept, kept,
    occ, vir, ids, turned, sums, in_sems, out_sems, late_sems,
):
    pairs, slab, rows_y, lanes = kept.shape
    parts, part_rows = coarse.shape[0] // pairs, coarse.shape[1] // 3
    in_left, in_right, even = sides()
    upper = jnp.where(even, 1, 0)

    def inputs(p):
        return (
            pltpu.make_async_copy(v0_hbm.at[p], v0.at[p], in_sems.at[0, p]),
            pltpu.make_async_copy(first_sent.at[p, 0], edges.at[p, upper], in_sems.at[1, p]),
            pltpu.make_async_copy(second_sent.at[p, 0], edges.at[p, 1 - upper], in_sems.at[2, p]),
        )

    def output(p):
        return pltpu.make_async_copy(kept.at[p], out.at[p], out_sems.at[p])

    for p in range(pairs):
        for copy in inputs(p):
            copy.start()
    late = [
        pltpu.make_async_copy(all_ids, ids, late_sems.at[0]),
        pltpu.make_async_copy(all_occ, occ, late_sems.at[1]),
        pltpu.make_async_copy(all_vir, vir, late_sems.at[2]),
    ]
    fill_band(band)
    fill_children(spread, 1.0, 1)
    line = lax.broadcasted_iota(jnp.int32, identity.shape, 0)
    identity[...] = jnp.where(line == lax.broadcasted_iota(jnp.int32, identity.shape, 1), 1.0, 0.0).astype(BF16)
    zero_rims(start)
    zero_rims(swept)

    def spread_out(p, carry):
        for part in range(parts):
            table = spread[...]
            at = p * parts + part
            own = dot(coarse[at, :part_rows], table) + dot(coarse[at, part_rows : 2 * part_rows], table)
            beyond = own + dot(coarse[at, 2 * part_rows :], table)
            for at, value in enumerate((beyond[:, :lanes], own[:, :lanes], own[:, lanes:], beyond[:, lanes:])):
                rows = 2 * part * part_rows
                wide[p, at, pl.ds(rows, part_rows, stride=2), :] = value
                wide[p, at, pl.ds(rows + 1, part_rows, stride=2), :] = value
        return carry

    lax.fori_loop(0, pairs, spread_out, 0)

    def one_pair(p, carry):
        for copy in inputs(p):
            copy.wait()

        @pl.when(p == 0)
        def _():
            for copy in late:
                copy.start()

        def halo(edge, index, row):
            rows = slice(row, row + STEP)
            one, two = first[p, index, rows].astype(F32), second[p, index, rows].astype(F32)
            return jnp.where(even == (edge == 1), one, two)

        for row in range(0, rows_y, STEP):
            rows = slice(row, row + STEP)
            for layer in range(slab):
                value = v0[p, layer, rows]
                if layer == 0:
                    value = value + halo(0, 0, row)
                    v0[p, layer, rows] = value
                if layer == slab - 1:
                    value = value + halo(1, 0, row)
                    v0[p, layer, rows] = value
                put(start, layer + 2, row, value + wide[p, 1 + layer // 2, rows])
            near = halo(0, 1, row) + edges[p, 0, rows].astype(F32) + wide[p, 0, rows]
            put(start, 1, row, in_left * near)
            put(start, 0, row, in_left * (halo(0, 2, row) + wide[p, 0, rows]))
            near = halo(1, 1, row) + edges[p, 1, rows].astype(F32) + wide[p, 3, rows]
            put(start, slab + 2, row, in_right * near)
            put(start, slab + 3, row, in_right * (halo(1, 2, row) + wide[p, 3, rows]))

        def sweep(ref, at, row):
            total = stencil(ref, at, row, band[...])
            return W * (total + read(ref, at - 1, row) + read(ref, at + 1, row))

        for row in range(0, rows_y, STEP):
            put(swept, 0, row, in_left * sweep(start, 1, row))
            for layer in range(slab):
                put(swept, layer + 1, row, sweep(start, layer + 2, row))
            put(swept, slab + 1, row, in_right * sweep(start, slab + 2, row))
        for row in range(0, rows_y, STEP):
            rows = slice(row, row + STEP)
            for layer in range(slab):
                kept[p, layer, rows] = (sweep(swept, layer + 1, row) + v0[p, layer, rows]).astype(BF16)
        output(p).start()
        half = lanes // 2
        for layer in range(slab):
            value = dot(identity[...], kept[p, layer], ((1,), (1,))).astype(BF16)
            column = 2 * layer * rows_y
            turned[p, :, column : column + rows_y] = value[:half]
            turned[p, :, column + rows_y : column + 2 * rows_y] = value[half:]
        return carry

    lax.fori_loop(0, pairs, one_pair, 0, unroll=2)
    for copy in late:
        copy.wait()
    half = lanes // 2
    fields = turned[...].reshape(pairs * half, 2 * slab * rows_y)
    count = ids.shape[0] // 2 * pairs
    first_row = lax.axis_index("pair") * pairs
    left = lax.broadcasted_iota(jnp.int32, (rows_y, lanes), 1) < half
    diagonal = lax.broadcasted_iota(jnp.int32, (half, 2 * lanes), 0) == lax.rem(
        lax.broadcasted_iota(jnp.int32, (half, 2 * lanes), 1), half
    )

    def density16(p, layer):
        turn, k = p // pairs, lax.rem(p, pairs)
        i, a = ids[2 * turn, k], ids[2 * turn + 1, k]
        return (occ[i, layer].astype(F32) * vir[a, layer].astype(F32)).astype(BF16)

    def four_rows(turn, carry):
        p = 4 * turn
        pieces = []
        for layer in range(slab):
            upper_row, lower_row = [], []
            for j in (0, 2):
                one, two = density16(p + j, layer), density16(p + j + 1, layer)
                upper_row.append(jnp.where(left, one, pltpu.roll(two, half, 1)))
                lower_row.append(jnp.where(left, pltpu.roll(one, half, 1), two))
            pieces += [jnp.concatenate(upper_row, axis=1), jnp.concatenate(lower_row, axis=1)]
        product = dot(fields, jnp.concatenate(pieces, axis=0))
        row = first_row + p
        row = jnp.where(row >= count, row - count, row) // 2
        for q in range(pairs):
            block = jnp.where(diagonal, product[q * half : (q + 1) * half], 0.0)
            block = jnp.sum(block, axis=0, keepdims=True)
            sums[row, q : q + 1] = block[:, :lanes]
            sums[row + 1, q : q + 1] = block[:, lanes:]
        return carry

    lax.fori_loop(0, count // 4, four_rows, 0, unroll=4)
    scale = 1.0 / float(slab * rows_y * lanes * lax.axis_size("dom"))
    total = scale * sums[...]
    left = lax.broadcasted_iota(jnp.int32, total.shape, 2) < half
    panel[0] = jnp.sum(jnp.where(left, total, 0.0), axis=2)
    panel[1] = jnp.sum(jnp.where(left, 0.0, total), axis=2)
    for p in range(pairs):
        output(p).wait()


def sine_table(length):
    steps = np.arange(length, dtype=np.float64) + 1.0
    return math.sqrt(2.0 / (length + 1)) * np.sin(np.pi * steps[:, None] * steps[None, :] / (length + 1))


def eigenvalues(length):
    return 2.0 - 2.0 * np.cos(np.pi * (np.arange(length, dtype=np.float64) + 1.0) / (length + 1))


def coarse_tables(size_x, size_y, size_z):
    sine_x, sine_z = sine_table(size_x), sine_table(size_z)
    modes = np.einsum("dk,zl->dzkl", sine_x, np.repeat(sine_z, 2, axis=0))
    modes = np.repeat(modes[:, None], 2, axis=1).reshape(size_x * 4 * size_z, size_x * size_z)
    high = modes.astype(BF16)
    low = (modes - high.astype(np.float64)).astype(BF16)
    total = eigenvalues(size_y)[:, None, None] + eigenvalues(size_x)[None, :, None] + eigenvalues(size_z)[None, None, :]
    inverse = (0.5 / total).reshape(size_y, size_x * size_z)
    return jnp.asarray(np.stack([high, low])), jnp.asarray(sine_table(size_y), F32), jnp.asarray(inverse, F32)


def shards(occupied, virtual, pair_ids):
    orbitals, slab, rows_y, lanes = occupied.shape
    pairs = pair_ids.shape[0]
    slabs = lax.axis_size("dom")
    parts = slabs // pairs
    half_y = rows_y // 2
    part_rows = half_y // parts
    padded_y = rows_y + 2 * PAD
    ids = pair_ids.T

    hbm, vmem = pl.BlockSpec(memory_space=pltpu.HBM), pl.BlockSpec(memory_space=pltpu.VMEM)
    anywhere = pl.BlockSpec(memory_space=pl.ANY)
    in_hbm = lambda x: pltpu.with_memory_space_constraint(x, pltpu.HBM)
    halo = (pairs, 3, rows_y, lanes)
    own = (pairs, slab, rows_y, lanes)
    share = (pairs, parts, 3, part_rows, lanes)
    shares, first, second, v0 = pl.pallas_call(
        source_kernel,
        in_specs=[hbm, hbm, hbm],
        out_specs=[hbm] * 4,
        out_shape=[
            pltpu.HBM(share, BF16),
            pltpu.HBM(halo, BF16),
            pltpu.HBM(halo, BF16),
            pltpu.HBM(own, F32),
        ],
        scratch_shapes=[
            pltpu.SMEM(ids.shape, jnp.int32),
            pltpu.VMEM(own, BF16),
            pltpu.VMEM(own, BF16),
            pltpu.VMEM((2 * lanes, lanes), BF16),
            pltpu.VMEM((2 * lanes, lanes), BF16),
            pltpu.VMEM((slab, padded_y, lanes), F32),
            pltpu.VMEM((slab + 2, padded_y, lanes), F32),
            pltpu.VMEM((2, rows_y, lanes), F32),
            pltpu.VMEM(own, F32),
            pltpu.VMEM((slab // 2 + 2, rows_y, lanes), F32),
            pltpu.VMEM((pairs, 2, 3, rows_y, lanes), BF16),
            pltpu.VMEM(share, BF16),
            pltpu.SemaphoreType.DMA,
            pltpu.SemaphoreType.DMA((2, pairs)),
            pltpu.SemaphoreType.DMA((4, pairs)),
        ],
        compiler_params=pltpu.CompilerParams(vmem_limit_bytes=32 * MIB),
        name="source",
    )(in_hbm(ids), in_hbm(occupied), in_hbm(virtual))

    inside = [(i, i ^ 1) for i in range(slabs)]
    outside = [(i, i + 1) for i in range(1, slabs - 1, 2)]
    outside = outside + [(j, i) for i, j in outside]
    first_halo = lax.ppermute(first, "dom", inside)
    second_halo = lax.ppermute(second, "dom", outside)
    received = lax.all_to_all(shares.reshape(slabs, 3, part_rows, lanes), "dom", 0, 0)
    views = [received]
    for turn in range(1, parts):
        perm = [(g * parts + (h + turn) % parts, g * parts + h) for g in range(slabs // parts) for h in range(parts)]
        views.append(lax.ppermute(received, "dom", perm))
    tables = coarse_tables(slabs, half_y // 2, lanes // 4)
    padded = pltpu.VMEM((slabs, half_y + 2 * PAD, lanes), F32)
    plain = pltpu.VMEM((slabs, half_y, lanes), F32)
    smoothed = pl.pallas_call(
        middle_kernel,
        in_specs=[vmem] * (parts + 3),
        out_specs=vmem,
        out_shape=jax.ShapeDtypeStruct((slabs, 3 * part_rows, lanes), BF16),
        scratch_shapes=[padded, padded, padded, plain, plain],
        compiler_params=pltpu.CompilerParams(vmem_limit_bytes=32 * MIB),
        name="middle",
    )(*views, *tables)
    groups = lax.axis_size("pair")
    late_ids, smoothed = lax.optimization_barrier((ids, smoothed))
    turns = [[((g + turn) % groups, g) for g in range(groups)] for turn in range(1, groups)]
    all_ids = jnp.concatenate([ids] + [lax.ppermute(late_ids, "pair", perm) for perm in turns], axis=0)
    returned = lax.all_to_all(smoothed, "dom", 0, 0)

    count = groups * pairs
    potentials, panel = pl.pallas_call(
        final_kernel,
        in_specs=[anywhere] + [hbm] * 5 + [vmem] * 3,
        out_specs=[hbm, vmem],
        out_shape=[pltpu.HBM(own, BF16), jax.ShapeDtypeStruct((2, count // 2, pairs), F32)],
        scratch_shapes=[
            pltpu.VMEM(own, F32),
            pltpu.VMEM((pairs, 2, rows_y, lanes), BF16),
            pltpu.VMEM((2 * lanes, lanes), BF16),
            pltpu.VMEM((lanes, 2 * lanes), BF16),
            pltpu.VMEM((lanes, lanes), BF16),
            pltpu.VMEM((pairs, 4, rows_y, lanes), F32),
            pltpu.VMEM((slab + 4, padded_y, lanes), F32),
            pltpu.VMEM((slab + 2, padded_y, lanes), F32),
            pltpu.VMEM(own, BF16),
            pltpu.VMEM(occupied.shape, BF16),
            pltpu.VMEM(virtual.shape, BF16),
            pltpu.SMEM(all_ids.shape, jnp.int32),
            pltpu.VMEM((pairs, lanes // 2, 2 * slab * rows_y), BF16),
            pltpu.VMEM((count // 2, pairs, lanes), F32),
            pltpu.SemaphoreType.DMA((3, pairs)),
            pltpu.SemaphoreType.DMA((pairs,)),
            pltpu.SemaphoreType.DMA((3,)),
        ],
        compiler_params=pltpu.CompilerParams(vmem_limit_bytes=24 * MIB),
        name="final",
    )(all_ids, *[in_hbm(x) for x in (occupied, virtual, v0, first, second)], returned, first_halo, second_halo)
    panel = jnp.swapaxes(panel, 0, 1).reshape(slabs, count // slabs, pairs)
    return potentials, jnp.sum(lax.all_to_all(panel, "dom", 0, 0), axis=0)


def solution(mesh):
    placed = (P(None, "dom", None, None), P(None, "dom", None, None), P("pair", None))
    return jax.shard_map(
        shards,
        mesh=mesh,
        in_specs=placed,
        out_specs=(P("pair", "dom", None, None), P("dom", "pair")),
        check_vma=False,
    )
```

```python
import math

import jax
import jax.numpy as jnp
import numpy as np
from jax import lax
from jax.experimental import pallas as pl
from jax.experimental.pallas import tpu as pltpu
from jax.sharding import PartitionSpec as P

W = 0.8 / 6.0
CENTRE = 1.5
PAD = 8
STEP = 64
F32 = jnp.float32
BF16 = jnp.bfloat16
MIB = 1024 * 1024
HIGHEST = lax.Precision.HIGHEST


def dot(a, b, contract=((1,), (0,)), precision=None):
    return lax.dot_general(a, b, (contract, ((), ())), precision=precision, preferred_element_type=F32)


def high_low(x):
    high = x.astype(BF16)
    return high, (x - high.astype(F32)).astype(BF16)


def dot_split(a, table, contract=((1,), (0,))):
    high, low = high_low(a)
    return dot(high, table[0], contract) + (dot(low, table[0], contract) + dot(high, table[1], contract))


def zero_rims(ref):
    zeros = jnp.zeros((ref.shape[0], PAD, ref.shape[2]), F32)
    ref[:, :PAD] = zeros
    ref[:, ref.shape[1] - PAD :] = zeros


def read(ref, layer, row, rows=STEP):
    return ref[layer, PAD + row : PAD + row + rows, :]


def put(ref, layer, row, value):
    ref[layer, PAD + row : PAD + row + value.shape[0]] = value


def across(centre, blocks=1):
    lane = lax.broadcasted_iota(jnp.int32, centre.shape, 1)
    width = centre.shape[1] // blocks
    first = lane % width == 0 if blocks > 1 else lane == 0
    last = lane % width == width - 1 if blocks > 1 else lane == width - 1
    lower = jnp.where(first, 0.0, pltpu.roll(centre, 1, 1))
    upper = jnp.where(last, 0.0, pltpu.roll(centre, centre.shape[1] - 1, 1))
    return CENTRE * centre + lower + upper


def across_by_matrix(centre, band):
    high, low = high_low(centre)
    return dot(jnp.concatenate([high, low], axis=1), band)


def beside(ref, layer, row, rows=STEP):
    return read(ref, layer, row - 1, rows) + read(ref, layer, row + 1, rows)


def stencil(ref, layer, row, band):
    centre = read(ref, layer, row)
    along_z = across(centre) if layer % 2 else across_by_matrix(centre, band)
    return along_z + beside(ref, layer, row)


def fill_band(ref):
    lanes = ref.shape[1]
    line = lax.rem(lax.broadcasted_iota(jnp.int32, ref.shape, 0), lanes)
    apart = jnp.abs(line - lax.broadcasted_iota(jnp.int32, ref.shape, 1))
    ref[...] = jnp.where(apart == 0, CENTRE, jnp.where(apart == 1, 1.0, 0.0)).astype(BF16)


def fill_children(ref, value, axis):
    child = lax.broadcasted_iota(jnp.int32, ref.shape, axis)
    parent = lax.broadcasted_iota(jnp.int32, ref.shape, 1 - axis)
    ref[...] = jnp.where(child // 2 == parent, value, 0.0).astype(BF16)


def sides(axis="dom"):
    me, count = lax.axis_index(axis), lax.axis_size(axis)
    below = jnp.where(me == 0, 0.0, 1.0).astype(F32)
    above = jnp.where(me == count - 1, 0.0, 1.0).astype(F32)
    return below, above, lax.rem(me, 2) == 0


def source_kernel(
    ids_hbm, occ, vir, shares, first, second, v0_out,
    ids, occ_rows, vir_rows, band, fold, own, once, beyond, v0s, sums, packed, share, ids_sem, in_sems, out_sems,
):
    pairs, slab, rows_y, lanes = occ_rows.shape
    parts, part_rows = share.shape[1], share.shape[3]
    in_left, in_right, even = sides()
    upper = jnp.where(even, 1, 0)

    copy = pltpu.make_async_copy(ids_hbm, ids, ids_sem)
    copy.start()
    zero_rims(own)
    zero_rims(once)
    fill_band(band)
    copy.wait()

    def inputs(p):
        return (
            pltpu.make_async_copy(occ.at[ids[0, p]], occ_rows.at[p], in_sems.at[0, p]),
            pltpu.make_async_copy(vir.at[ids[1, p]], vir_rows.at[p], in_sems.at[1, p]),
        )

    def last_output(p):
        return pltpu.make_async_copy(share.at[p], shares.at[p], out_sems.at[0, p])

    def outputs(p):
        return (
            pltpu.make_async_copy(packed.at[p, upper], first.at[p], out_sems.at[1, p]),
            pltpu.make_async_copy(packed.at[p, 1 - upper], second.at[p], out_sems.at[2, p]),
            pltpu.make_async_copy(v0s.at[p], v0_out.at[p], out_sems.at[3, p]),
        )

    for p in range(pairs):
        for copy in inputs(p):
            copy.start()
    fill_children(fold, 0.5, 0)

    def one_pair(p, carry):
        for copy in inputs(p):
            copy.wait()
        for layer in range(slab):
            own[layer, PAD : PAD + rows_y] = occ_rows[p, layer].astype(F32) * vir_rows[p, layer].astype(F32)

        for row in range(0, rows_y, STEP):
            rows = slice(row, row + STEP)
            for layer in range(slab):
                centre = read(own, layer, row)
                total = stencil(own, layer, row, band[...])
                if layer == 0:
                    beyond[0, rows] = (W * in_left) * total
                if layer == slab - 1:
                    beyond[1, rows] = (W * in_right) * total
                if layer > 0:
                    total = total + read(own, layer - 1, row)
                if layer < slab - 1:
                    total = total + read(own, layer + 1, row)
                value = W * total
                put(once, layer + 1, row, value)
                v0 = W * (centre + value)
                v0s[p, layer, rows] = v0
                if layer == 0:
                    put(once, 0, row, (W * in_left) * centre)
                    packed[p, 0, 0, rows] = (W * W * centre).astype(BF16)
                    packed[p, 0, 1, rows] = v0.astype(BF16)
                if layer == 1:
                    packed[p, 0, 2, rows] = v0.astype(BF16)
                if layer == slab - 2:
                    packed[p, 1, 2, rows] = v0.astype(BF16)
                if layer == slab - 1:
                    put(once, slab + 1, row, (W * in_right) * centre)
                    packed[p, 1, 0, rows] = (W * W * centre).astype(BF16)
                    packed[p, 1, 1, rows] = v0.astype(BF16)

        for copy in outputs(p):
            copy.start()

        def twice(layer, row):
            if layer == -2:
                return read(once, 0, row)
            if layer == slab + 1:
                return read(once, slab + 1, row)
            if layer == -1:
                return beyond[0, row : row + STEP] + read(once, 1, row)
            if layer == slab:
                return beyond[1, row : row + STEP] + read(once, slab, row)
            at = layer + 1
            return stencil(once, at, row, band[...]) + read(once, at - 1, row) + read(once, at + 1, row)

        for row in range(0, rows_y, STEP):
            for coarse in range(slab // 2 + 2):
                pair_sum = twice(2 * coarse - 2, row) + twice(2 * coarse - 1, row)
                sums[coarse, row : row + STEP] = W * pair_sum

        half = rows_y // 2

        def folded(coarse):
            return sums[coarse, pl.ds(0, half, stride=2), :] + sums[coarse, pl.ds(1, half, stride=2), :]

        def together(left, right):
            both = jnp.concatenate([folded(left), folded(right)], axis=1)
            high, low = high_low(both)
            return dot(high, fold[...]) + dot(low, fold[...])

        outer = together(3, 0)
        edge = outer.astype(BF16)
        lane = lax.broadcasted_iota(jnp.int32, outer.shape, 1)
        rest = pltpu.roll(outer - edge.astype(F32), lanes // 2, 1) * jnp.where(lane < lanes // 2, in_left, in_right)
        own_high, own_low = high_low(together(1, 2) + rest)
        for part in range(parts):
            rows = slice(part * part_rows, (part + 1) * part_rows)
            share[p, part, 0] = own_high[rows]
            share[p, part, 1] = own_low[rows]
            share[p, part, 2] = edge[rows]
        last_output(p).start()
        return carry

    lax.fori_loop(0, pairs, one_pair, 0)
    for p in range(pairs):
        for copy in (*outputs(p), last_output(p)):
            copy.wait()


def middle_kernel(*refs):
    parts = len(refs) - 9
    received = refs[:parts]
    modes, table_y, inverse, out = refs[parts : parts + 4]
    source, field_a, field_b, smooth, edge = refs[parts + 4 :]
    slabs, _, part_rows, lanes = received[0].shape
    rows_y = parts * part_rows
    own_part = lax.rem(lax.axis_index("dom"), parts)
    left = lax.broadcasted_iota(jnp.int32, (part_rows, lanes), 1) < lanes // 2
    for ref in (source, field_a, field_b):
        zero_rims(ref)
    for turn in range(parts):
        at = own_part + turn
        at = jnp.where(at >= parts, at - parts, at) * part_rows
        at = pl.multiple_of(at, part_rows)
        ref = received[turn]
        for d in range(slabs):
            value = ref[d, 0].astype(F32) + ref[d, 1].astype(F32)
            before = ref[d - 1, 2].astype(F32) if d > 0 else jnp.zeros_like(value)
            after = ref[d + 1, 2].astype(F32) if d < slabs - 1 else jnp.zeros_like(value)
            source[d, pl.ds(PAD + at, part_rows)] = value + jnp.where(left, before, after)

    half = lanes // 2
    left = lax.broadcasted_iota(jnp.int32, (rows_y, lanes), 1) < half

    def swapped(ref, d):
        return pltpu.roll(read(ref, d, 0, rows_y), half, 1)

    def apply(ref, each):
        zeros = jnp.zeros((rows_y, lanes), F32)
        before, here = zeros, swapped(ref, 0)
        for d in range(slabs):
            after = swapped(ref, d + 1) if d < slabs - 1 else zeros
            total = across(read(ref, d, 0, rows_y), 2) + beside(ref, d, 0, rows_y)
            each(d, total + here + jnp.where(left, before, after))
            before, here = here, after

    apply(source, lambda d, total: put(field_a, d, 0, W * total))

    def to_coarse(d, total):
        smooth[d] = W * (read(source, d, 0, rows_y) + read(field_a, d, 0, rows_y))
        put(field_b, d, 0, W * total)

    apply(field_a, to_coarse)
    pieces = []
    for d in range(slabs):
        even_rows = field_b[d, pl.ds(PAD, rows_y // 2, stride=2), :]
        odd_rows = field_b[d, pl.ds(PAD + 1, rows_y // 2, stride=2), :]
        pieces.append(even_rows + odd_rows)
    spectral = dot_split(jnp.concatenate(pieces, axis=1), modes)
    spectral = dot(table_y[...], spectral, precision=HIGHEST) * inverse[...]
    spread = dot_split(dot(table_y[...], spectral, precision=HIGHEST), modes, ((1,), (1,)))
    for d in range(slabs):
        value = spread[:, d * lanes : (d + 1) * lanes]
        field_b[d, pl.ds(PAD, rows_y // 2, stride=2), :] = value
        field_b[d, pl.ds(PAD + 1, rows_y // 2, stride=2), :] = value
    for d in range(slabs):
        put(field_a, d, 0, smooth[d] + read(field_b, d, 0, rows_y))

    apply(field_a, lambda d, total: put(field_b, d, 0, W * total))
    apply(field_b, lambda d, total: put(field_a, d, 0, W * total + smooth[d]))
    zeros = jnp.zeros((rows_y, lanes), F32)
    before, here = zeros, swapped(field_a, 0)
    for d in range(slabs):
        after = swapped(field_a, d + 1) if d < slabs - 1 else zeros
        edge[d] = jnp.where(left, before, after) - read(field_a, d, 0, rows_y)
        before, here = here, after
    at = pl.multiple_of(own_part * part_rows, part_rows)
    for d in range(slabs):
        high, low = high_low(field_a[d, pl.ds(PAD + at, part_rows)])
        out[d, :part_rows] = high
        out[d, part_rows : 2 * part_rows] = low
        out[d, 2 * part_rows :] = edge[d, pl.ds(at, part_rows)].astype(BF16)


def final_kernel(
    all_ids, all_occ, all_vir, v0_hbm, first_sent, second_sent, coarse, first, second, out, panel,
    v0, edges, band, spread, identity, wide, start, swept, kept,
    occ, vir, ids, turned, sums, in_sems, out_sems, late_sems,
):
    pairs, slab, rows_y, lanes = kept.shape
    parts, part_rows = coarse.shape[0] // pairs, coarse.shape[1] // 3
    in_left, in_right, even = sides()
    upper = jnp.where(even, 1, 0)

    def inputs(p):
        return (
            pltpu.make_async_copy(v0_hbm.at[p], v0.at[p], in_sems.at[0, p]),
            pltpu.make_async_copy(first_sent.at[p, 0], edges.at[p, upper], in_sems.at[1, p]),
            pltpu.make_async_copy(second_sent.at[p, 0], edges.at[p, 1 - upper], in_sems.at[2, p]),
        )

    def output(p):
        return pltpu.make_async_copy(kept.at[p], out.at[p], out_sems.at[p])

    for p in range(pairs):
        for copy in inputs(p):
            copy.start()
    late = [
        pltpu.make_async_copy(all_ids, ids, late_sems.at[0]),
        pltpu.make_async_copy(all_occ, occ, late_sems.at[1]),
        pltpu.make_async_copy(all_vir, vir, late_sems.at[2]),
    ]
    fill_band(band)
    fill_children(spread, 1.0, 1)
    line = lax.broadcasted_iota(jnp.int32, identity.shape, 0)
    identity[...] = jnp.where(line == lax.broadcasted_iota(jnp.int32, identity.shape, 1), 1.0, 0.0).astype(BF16)
    zero_rims(start)
    zero_rims(swept)

    def spread_out(p, carry):
        for part in range(parts):
            table = spread[...]
            at = p * parts + part
            own = dot(coarse[at, :part_rows], table) + dot(coarse[at, part_rows : 2 * part_rows], table)
            beyond = own + dot(coarse[at, 2 * part_rows :], table)
            for at, value in enumerate((beyond[:, :lanes], own[:, :lanes], own[:, lanes:], beyond[:, lanes:])):
                rows = 2 * part * part_rows
                wide[p, at, pl.ds(rows, part_rows, stride=2), :] = value
                wide[p, at, pl.ds(rows + 1, part_rows, stride=2), :] = value
        return carry

    lax.fori_loop(0, pairs, spread_out, 0)

    def one_pair(p, carry):
        for copy in inputs(p):
            copy.wait()

        @pl.when(p == 0)
        def _():
            for copy in late:
                copy.start()

        def halo(edge, index, row):
            rows = slice(row, row + STEP)
            one, two = first[p, index, rows].astype(F32), second[p, index, rows].astype(F32)
            return jnp.where(even == (edge == 1), one, two)

        for row in range(0, rows_y, STEP):
            rows = slice(row, row + STEP)
            for layer in range(slab):
                value = v0[p, layer, rows]
                if layer == 0:
                    value = value + halo(0, 0, row)
                    v0[p, layer, rows] = value
                if layer == slab - 1:
                    value = value + halo(1, 0, row)
                    v0[p, layer, rows] = value
                put(start, layer + 2, row, value + wide[p, 1 + layer // 2, rows])
            near = halo(0, 1, row) + edges[p, 0, rows].astype(F32) + wide[p, 0, rows]
            put(start, 1, row, in_left * near)
            put(start, 0, row, in_left * (halo(0, 2, row) + wide[p, 0, rows]))
            near = halo(1, 1, row) + edges[p, 1, rows].astype(F32) + wide[p, 3, rows]
            put(start, slab + 2, row, in_right * near)
            put(start, slab + 3, row, in_right * (halo(1, 2, row) + wide[p, 3, rows]))

        def sweep(ref, at, row):
            total = stencil(ref, at, row, band[...])
            return W * (total + read(ref, at - 1, row) + read(ref, at + 1, row))

        for row in range(0, rows_y, STEP):
            put(swept, 0, row, in_left * sweep(start, 1, row))
            for layer in range(slab):
                put(swept, layer + 1, row, sweep(start, layer + 2, row))
            put(swept, slab + 1, row, in_right * sweep(start, slab + 2, row))
        for row in range(0, rows_y, STEP):
            rows = slice(row, row + STEP)
            for layer in range(slab):
                kept[p, layer, rows] = (sweep(swept, layer + 1, row) + v0[p, layer, rows]).astype(BF16)
        output(p).start()
        half = lanes // 2
        for layer in range(slab):
            value = dot(identity[...], kept[p, layer], ((1,), (1,))).astype(BF16)
            column = 2 * layer * rows_y
            turned[p, :, column : column + rows_y] = value[:half]
            turned[p, :, column + rows_y : column + 2 * rows_y] = value[half:]
        return carry

    lax.fori_loop(0, pairs, one_pair, 0, unroll=2)
    for copy in late:
        copy.wait()
    half = lanes // 2
    fields = turned[...].reshape(pairs * half, 2 * slab * rows_y)
    count = ids.shape[0] // 2 * pairs
    first_row = lax.axis_index("pair") * pairs
    left = lax.broadcasted_iota(jnp.int32, (rows_y, lanes), 1) < half
    diagonal = lax.broadcasted_iota(jnp.int32, (half, 2 * lanes), 0) == lax.rem(
        lax.broadcasted_iota(jnp.int32, (half, 2 * lanes), 1), half
    )

    def density16(p, layer):
        turn, k = p // pairs, lax.rem(p, pairs)
        i, a = ids[2 * turn, k], ids[2 * turn + 1, k]
        return (occ[i, layer].astype(F32) * vir[a, layer].astype(F32)).astype(BF16)

    def four_rows(turn, carry):
        p = 4 * turn
        pieces = []
        for layer in range(slab):
            upper_row, lower_row = [], []
            for j in (0, 2):
                one, two = density16(p + j, layer), density16(p + j + 1, layer)
                upper_row.append(jnp.where(left, one, pltpu.roll(two, half, 1)))
                lower_row.append(jnp.where(left, pltpu.roll(one, half, 1), two))
            pieces += [jnp.concatenate(upper_row, axis=1), jnp.concatenate(lower_row, axis=1)]
        product = dot(fields, jnp.concatenate(pieces, axis=0))
        row = first_row + p
        row = jnp.where(row >= count, row - count, row) // 2
        for q in range(pairs):
            block = jnp.where(diagonal, product[q * half : (q + 1) * half], 0.0)
            block = jnp.sum(block, axis=0, keepdims=True)
            sums[row, q : q + 1] = block[:, :lanes]
            sums[row + 1, q : q + 1] = block[:, lanes:]
        return carry

    lax.fori_loop(0, count // 4, four_rows, 0, unroll=4)
    scale = 1.0 / float(slab * rows_y * lanes * lax.axis_size("dom"))
    total = scale * sums[...]
    left = lax.broadcasted_iota(jnp.int32, total.shape, 2) < half
    panel[0] = jnp.sum(jnp.where(left, total, 0.0), axis=2)
    panel[1] = jnp.sum(jnp.where(left, 0.0, total), axis=2)
    for p in range(pairs):
        output(p).wait()


def sine_table(length):
    steps = np.arange(length, dtype=np.float64) + 1.0
    return math.sqrt(2.0 / (length + 1)) * np.sin(np.pi * steps[:, None] * steps[None, :] / (length + 1))


def eigenvalues(length):
    return 2.0 - 2.0 * np.cos(np.pi * (np.arange(length, dtype=np.float64) + 1.0) / (length + 1))


def coarse_tables(size_x, size_y, size_z):
    sine_x, sine_z = sine_table(size_x), sine_table(size_z)
    modes = np.einsum("dk,zl->dzkl", sine_x, np.repeat(sine_z, 2, axis=0))
    modes = np.repeat(modes[:, None], 2, axis=1).reshape(size_x * 4 * size_z, size_x * size_z)
    high = modes.astype(BF16)
    low = (modes - high.astype(np.float64)).astype(BF16)
    total = eigenvalues(size_y)[:, None, None] + eigenvalues(size_x)[None, :, None] + eigenvalues(size_z)[None, None, :]
    inverse = (0.5 / total).reshape(size_y, size_x * size_z)
    return jnp.asarray(np.stack([high, low])), jnp.asarray(sine_table(size_y), F32), jnp.asarray(inverse, F32)


def shards(occupied, virtual, pair_ids):
    orbitals, slab, rows_y, lanes = occupied.shape
    pairs = pair_ids.shape[0]
    slabs = lax.axis_size("dom")
    parts = slabs // pairs
    half_y = rows_y // 2
    part_rows = half_y // parts
    padded_y = rows_y + 2 * PAD
    ids = pair_ids.T

    hbm, vmem = pl.BlockSpec(memory_space=pltpu.HBM), pl.BlockSpec(memory_space=pltpu.VMEM)
    anywhere = pl.BlockSpec(memory_space=pl.ANY)
    in_hbm = lambda x: pltpu.with_memory_space_constraint(x, pltpu.HBM)
    halo = (pairs, 3, rows_y, lanes)
    own = (pairs, slab, rows_y, lanes)
    share = (pairs, parts, 3, part_rows, lanes)
    shares, first, second, v0 = pl.pallas_call(
        source_kernel,
        in_specs=[hbm, hbm, hbm],
        out_specs=[hbm] * 4,
        out_shape=[
            pltpu.HBM(share, BF16),
            pltpu.HBM(halo, BF16),
            pltpu.HBM(halo, BF16),
            pltpu.HBM(own, F32),
        ],
        scratch_shapes=[
            pltpu.SMEM(ids.shape, jnp.int32),
            pltpu.VMEM(own, BF16),
            pltpu.VMEM(own, BF16),
            pltpu.VMEM((2 * lanes, lanes), BF16),
            pltpu.VMEM((2 * lanes, lanes), BF16),
            pltpu.VMEM((slab, padded_y, lanes), F32),
            pltpu.VMEM((slab + 2, padded_y, lanes), F32),
            pltpu.VMEM((2, rows_y, lanes), F32),
            pltpu.VMEM(own, F32),
            pltpu.VMEM((slab // 2 + 2, rows_y + PAD, lanes), F32),
            pltpu.VMEM((pairs, 2, 3, rows_y, lanes), BF16),
            pltpu.VMEM(share, BF16),
            pltpu.SemaphoreType.DMA,
            pltpu.SemaphoreType.DMA((2, pairs)),
            pltpu.SemaphoreType.DMA((4, pairs)),
        ],
        compiler_params=pltpu.CompilerParams(vmem_limit_bytes=32 * MIB),
        name="source",
    )(in_hbm(ids), in_hbm(occupied), in_hbm(virtual))

    inside = [(i, i ^ 1) for i in range(slabs)]
    outside = [(i, i + 1) for i in range(1, slabs - 1, 2)]
    outside = outside + [(j, i) for i, j in outside]
    first_halo = lax.ppermute(first, "dom", inside)
    second_halo = lax.ppermute(second, "dom", outside)
    received = lax.all_to_all(shares.reshape(slabs, 3, part_rows, lanes), "dom", 0, 0)
    views = [received]
    for turn in range(1, parts):
        perm = [(g * parts + (h + turn) % parts, g * parts + h) for g in range(slabs // parts) for h in range(parts)]
        views.append(lax.ppermute(received, "dom", perm))
    tables = coarse_tables(slabs, half_y // 2, lanes // 4)
    padded = pltpu.VMEM((slabs, half_y + 2 * PAD, lanes), F32)
    plain = pltpu.VMEM((slabs, half_y, lanes), F32)
    smoothed = pl.pallas_call(
        middle_kernel,
        in_specs=[vmem] * (parts + 3),
        out_specs=vmem,
        out_shape=jax.ShapeDtypeStruct((slabs, 3 * part_rows, lanes), BF16),
        scratch_shapes=[padded, padded, padded, plain, plain],
        compiler_params=pltpu.CompilerParams(vmem_limit_bytes=32 * MIB),
        name="middle",
    )(*views, *tables)
    groups = lax.axis_size("pair")
    late_ids, smoothed = lax.optimization_barrier((ids, smoothed))
    turns = [[((g + turn) % groups, g) for g in range(groups)] for turn in range(1, groups)]
    all_ids = jnp.concatenate([ids] + [lax.ppermute(late_ids, "pair", perm) for perm in turns], axis=0)
    returned = lax.all_to_all(smoothed, "dom", 0, 0)

    count = groups * pairs
    potentials, panel = pl.pallas_call(
        final_kernel,
        in_specs=[anywhere] + [hbm] * 5 + [vmem] * 3,
        out_specs=[hbm, vmem],
        out_shape=[pltpu.HBM(own, BF16), jax.ShapeDtypeStruct((2, count // 2, pairs), F32)],
        scratch_shapes=[
            pltpu.VMEM(own, F32),
            pltpu.VMEM((pairs, 2, rows_y, lanes), BF16),
            pltpu.VMEM((2 * lanes, lanes), BF16),
            pltpu.VMEM((lanes, 2 * lanes), BF16),
            pltpu.VMEM((lanes, lanes), BF16),
            pltpu.VMEM((pairs, 4, rows_y + PAD, lanes), F32),
            pltpu.VMEM((slab + 4, padded_y, lanes), F32),
            pltpu.VMEM((slab + 2, padded_y, lanes), F32),
            pltpu.VMEM(own, BF16),
            pltpu.VMEM(occupied.shape, BF16),
            pltpu.VMEM(virtual.shape, BF16),
            pltpu.SMEM(all_ids.shape, jnp.int32),
            pltpu.VMEM((pairs, lanes // 2, 2 * slab * rows_y), BF16),
            pltpu.VMEM((count // 2, pairs, lanes), F32),
            pltpu.SemaphoreType.DMA((3, pairs)),
            pltpu.SemaphoreType.DMA((pairs,)),
            pltpu.SemaphoreType.DMA((3,)),
        ],
        compiler_params=pltpu.CompilerParams(vmem_limit_bytes=24 * MIB),
        name="final",
    )(all_ids, *[in_hbm(x) for x in (occupied, virtual, v0, first, second)], returned, first_halo, second_halo)
    panel = jnp.swapaxes(panel, 0, 1).reshape(slabs, count // slabs, pairs)
    return potentials, jnp.sum(lax.all_to_all(panel, "dom", 0, 0), axis=0)


def solution(mesh):
    placed = (P(None, "dom", None, None), P(None, "dom", None, None), P("pair", None))
    return jax.shard_map(
        shards,
        mesh=mesh,
        in_specs=placed,
        out_specs=(P("pair", "dom", None, None), P("dom", "pair")),
        check_vma=False,
    )
```

```python
import math

import jax
import jax.numpy as jnp
import numpy as np
from jax import lax
from jax.experimental import pallas as pl
from jax.experimental.pallas import tpu as pltpu
from jax.sharding import PartitionSpec as P

W = 0.8 / 6.0
CENTRE = 1.5
PAD = 8
STEP = 64
F32 = jnp.float32
BF16 = jnp.bfloat16
MIB = 1024 * 1024
HIGHEST = lax.Precision.HIGHEST


def dot(a, b, contract=((1,), (0,)), precision=None):
    return lax.dot_general(a, b, (contract, ((), ())), precision=precision, preferred_element_type=F32)


def high_low(x):
    high = x.astype(BF16)
    return high, (x - high.astype(F32)).astype(BF16)


def dot_split(a, table, contract=((1,), (0,))):
    high, low = high_low(a)
    return dot(high, table[0], contract) + (dot(low, table[0], contract) + dot(high, table[1], contract))


def zero_rims(ref):
    zeros = jnp.zeros((ref.shape[0], PAD, ref.shape[2]), F32)
    ref[:, :PAD] = zeros
    ref[:, ref.shape[1] - PAD :] = zeros


def read(ref, layer, row, rows=STEP):
    return ref[layer, PAD + row : PAD + row + rows, :]


def put(ref, layer, row, value):
    ref[layer, PAD + row : PAD + row + value.shape[0]] = value


def across(centre, blocks=1):
    lane = lax.broadcasted_iota(jnp.int32, centre.shape, 1)
    width = centre.shape[1] // blocks
    first = lane % width == 0 if blocks > 1 else lane == 0
    last = lane % width == width - 1 if blocks > 1 else lane == width - 1
    lower = jnp.where(first, 0.0, pltpu.roll(centre, 1, 1))
    upper = jnp.where(last, 0.0, pltpu.roll(centre, centre.shape[1] - 1, 1))
    return CENTRE * centre + lower + upper


def across_by_matrix(centre, band):
    high, low = high_low(centre)
    return dot(jnp.concatenate([high, low], axis=1), band)


def beside(ref, layer, row, rows=STEP):
    return read(ref, layer, row - 1, rows) + read(ref, layer, row + 1, rows)


def stencil(ref, layer, row, band):
    centre = read(ref, layer, row)
    along_z = across(centre) if layer % 2 else across_by_matrix(centre, band)
    return along_z + beside(ref, layer, row)


def fill_band(ref):
    lanes = ref.shape[1]
    line = lax.rem(lax.broadcasted_iota(jnp.int32, ref.shape, 0), lanes)
    apart = jnp.abs(line - lax.broadcasted_iota(jnp.int32, ref.shape, 1))
    ref[...] = jnp.where(apart == 0, CENTRE, jnp.where(apart == 1, 1.0, 0.0)).astype(BF16)


def fill_children(ref, value, axis):
    child = lax.broadcasted_iota(jnp.int32, ref.shape, axis)
    parent = lax.broadcasted_iota(jnp.int32, ref.shape, 1 - axis)
    ref[...] = jnp.where(child // 2 == parent, value, 0.0).astype(BF16)


def sides(axis="dom"):
    me, count = lax.axis_index(axis), lax.axis_size(axis)
    below = jnp.where(me == 0, 0.0, 1.0).astype(F32)
    above = jnp.where(me == count - 1, 0.0, 1.0).astype(F32)
    return below, above, lax.rem(me, 2) == 0


def source_kernel(
    ids_hbm, occ, vir, shares, first, second, v0_out,
    ids, occ_rows, vir_rows, band, fold, own, once, beyond, v0s, sums, packed, share, ids_sem, in_sems, out_sems,
):
    pairs, slab, rows_y, lanes = occ_rows.shape
    parts, part_rows = share.shape[1], share.shape[3]
    in_left, in_right, even = sides()
    upper = jnp.where(even, 1, 0)

    copy = pltpu.make_async_copy(ids_hbm, ids, ids_sem)
    copy.start()
    zero_rims(own)
    zero_rims(once)
    fill_band(band)
    copy.wait()

    def inputs(p):
        return (
            pltpu.make_async_copy(occ.at[ids[0, p]], occ_rows.at[p], in_sems.at[0, p]),
            pltpu.make_async_copy(vir.at[ids[1, p]], vir_rows.at[p], in_sems.at[1, p]),
        )

    def last_output(p):
        return pltpu.make_async_copy(share.at[p], shares.at[p], out_sems.at[0, p])

    def outputs(p):
        return (
            pltpu.make_async_copy(packed.at[p, upper], first.at[p], out_sems.at[1, p]),
            pltpu.make_async_copy(packed.at[p, 1 - upper], second.at[p], out_sems.at[2, p]),
            pltpu.make_async_copy(v0s.at[p], v0_out.at[p], out_sems.at[3, p]),
        )

    for p in range(pairs):
        for copy in inputs(p):
            copy.start()
    fill_children(fold, 0.5, 0)

    def one_pair(p, carry):
        for copy in inputs(p):
            copy.wait()
        for layer in range(slab):
            own[layer, PAD : PAD + rows_y] = occ_rows[p, layer].astype(F32) * vir_rows[p, layer].astype(F32)

        for row in range(0, rows_y, STEP):
            rows = slice(row, row + STEP)
            for layer in range(slab):
                centre = read(own, layer, row)
                total = stencil(own, layer, row, band[...])
                if layer == 0:
                    beyond[0, rows] = (W * in_left) * total
                if layer == slab - 1:
                    beyond[1, rows] = (W * in_right) * total
                if layer > 0:
                    total = total + read(own, layer - 1, row)
                if layer < slab - 1:
                    total = total + read(own, layer + 1, row)
                value = W * total
                put(once, layer + 1, row, value)
                v0 = W * (centre + value)
                v0s[p, layer, rows] = v0
                if layer == 0:
                    put(once, 0, row, (W * in_left) * centre)
                    packed[p, 0, 0, rows] = (W * W * centre).astype(BF16)
                    packed[p, 0, 1, rows] = v0.astype(BF16)
                if layer == 1:
                    packed[p, 0, 2, rows] = v0.astype(BF16)
                if layer == slab - 2:
                    packed[p, 1, 2, rows] = v0.astype(BF16)
                if layer == slab - 1:
                    put(once, slab + 1, row, (W * in_right) * centre)
                    packed[p, 1, 0, rows] = (W * W * centre).astype(BF16)
                    packed[p, 1, 1, rows] = v0.astype(BF16)

        for copy in outputs(p):
            copy.start()

        def twice(layer, row):
            if layer == -2:
                return read(once, 0, row)
            if layer == slab + 1:
                return read(once, slab + 1, row)
            if layer == -1:
                return beyond[0, row : row + STEP] + read(once, 1, row)
            if layer == slab:
                return beyond[1, row : row + STEP] + read(once, slab, row)
            at = layer + 1
            return stencil(once, at, row, band[...]) + read(once, at - 1, row) + read(once, at + 1, row)

        for row in range(0, rows_y, STEP):
            for coarse in range(slab // 2 + 2):
                pair_sum = twice(2 * coarse - 2, row) + twice(2 * coarse - 1, row)
                sums[coarse, row : row + STEP] = W * pair_sum

        half = rows_y // 2

        def folded(coarse):
            return sums[coarse, pl.ds(0, half, stride=2), :] + sums[coarse, pl.ds(1, half, stride=2), :]

        def together(left, right):
            both = jnp.concatenate([folded(left), folded(right)], axis=1)
            high, low = high_low(both)
            return dot(high, fold[...]) + dot(low, fold[...])

        outer = together(3, 0)
        edge = outer.astype(BF16)
        lane = lax.broadcasted_iota(jnp.int32, outer.shape, 1)
        rest = pltpu.roll(outer - edge.astype(F32), lanes // 2, 1) * jnp.where(lane < lanes // 2, in_left, in_right)
        own_high, own_low = high_low(together(1, 2) + rest)
        for part in range(parts):
            rows = slice(part * part_rows, (part + 1) * part_rows)
            share[p, part, 0] = own_high[rows]
            share[p, part, 1] = own_low[rows]
            share[p, part, 2] = edge[rows]
        last_output(p).start()
        return carry

    lax.fori_loop(0, pairs, one_pair, 0, unroll=2)
    for p in range(pairs):
        for copy in (*outputs(p), last_output(p)):
            copy.wait()


def middle_kernel(*refs):
    parts = len(refs) - 9
    received = refs[:parts]
    modes, table_y, inverse, out = refs[parts : parts + 4]
    source, field_a, field_b, smooth, edge = refs[parts + 4 :]
    slabs, _, part_rows, lanes = received[0].shape
    rows_y = parts * part_rows
    own_part = lax.rem(lax.axis_index("dom"), parts)
    left = lax.broadcasted_iota(jnp.int32, (part_rows, lanes), 1) < lanes // 2
    for ref in (source, field_a, field_b):
        zero_rims(ref)
    for turn in range(parts):
        at = own_part + turn
        at = jnp.where(at >= parts, at - parts, at) * part_rows
        at = pl.multiple_of(at, part_rows)
        ref = received[turn]
        for d in range(slabs):
            value = ref[d, 0].astype(F32) + ref[d, 1].astype(F32)
            before = ref[d - 1, 2].astype(F32) if d > 0 else jnp.zeros_like(value)
            after = ref[d + 1, 2].astype(F32) if d < slabs - 1 else jnp.zeros_like(value)
            source[d, pl.ds(PAD + at, part_rows)] = value + jnp.where(left, before, after)

    half = lanes // 2
    left = lax.broadcasted_iota(jnp.int32, (rows_y, lanes), 1) < half

    def swapped(ref, d):
        return pltpu.roll(read(ref, d, 0, rows_y), half, 1)

    def apply(ref, each):
        zeros = jnp.zeros((rows_y, lanes), F32)
        before, here = zeros, swapped(ref, 0)
        for d in range(slabs):
            after = swapped(ref, d + 1) if d < slabs - 1 else zeros
            total = across(read(ref, d, 0, rows_y), 2) + beside(ref, d, 0, rows_y)
            each(d, total + here + jnp.where(left, before, after))
            before, here = here, after

    apply(source, lambda d, total: put(field_a, d, 0, W * total))

    def to_coarse(d, total):
        smooth[d] = W * (read(source, d, 0, rows_y) + read(field_a, d, 0, rows_y))
        put(field_b, d, 0, W * total)

    apply(field_a, to_coarse)
    pieces = []
    for d in range(slabs):
        even_rows = field_b[d, pl.ds(PAD, rows_y // 2, stride=2), :]
        odd_rows = field_b[d, pl.ds(PAD + 1, rows_y // 2, stride=2), :]
        pieces.append(even_rows + odd_rows)
    spectral = dot_split(jnp.concatenate(pieces, axis=1), modes)
    spectral = dot(table_y[...], spectral, precision=HIGHEST) * inverse[...]
    spread = dot_split(dot(table_y[...], spectral, precision=HIGHEST), modes, ((1,), (1,)))
    for d in range(slabs):
        value = spread[:, d * lanes : (d + 1) * lanes]
        field_b[d, pl.ds(PAD, rows_y // 2, stride=2), :] = value
        field_b[d, pl.ds(PAD + 1, rows_y // 2, stride=2), :] = value
    for d in range(slabs):
        put(field_a, d, 0, smooth[d] + read(field_b, d, 0, rows_y))

    apply(field_a, lambda d, total: put(field_b, d, 0, W * total))
    apply(field_b, lambda d, total: put(field_a, d, 0, W * total + smooth[d]))
    zeros = jnp.zeros((rows_y, lanes), F32)
    before, here = zeros, swapped(field_a, 0)
    for d in range(slabs):
        after = swapped(field_a, d + 1) if d < slabs - 1 else zeros
        edge[d] = jnp.where(left, before, after) - read(field_a, d, 0, rows_y)
        before, here = here, after
    at = pl.multiple_of(own_part * part_rows, part_rows)
    for d in range(slabs):
        high, low = high_low(field_a[d, pl.ds(PAD + at, part_rows)])
        out[d, :part_rows] = high
        out[d, part_rows : 2 * part_rows] = low
        out[d, 2 * part_rows :] = edge[d, pl.ds(at, part_rows)].astype(BF16)


def final_kernel(
    all_ids, all_occ, all_vir, v0_hbm, first_sent, second_sent, coarse, first, second, out, panel,
    v0, edges, band, spread, identity, wide, start, swept, kept,
    occ, vir, ids, turned, sums, in_sems, out_sems, late_sems,
):
    pairs, slab, rows_y, lanes = kept.shape
    parts, part_rows = coarse.shape[0] // pairs, coarse.shape[1] // 3
    in_left, in_right, even = sides()
    upper = jnp.where(even, 1, 0)

    def inputs(p):
        return (
            pltpu.make_async_copy(v0_hbm.at[p], v0.at[p], in_sems.at[0, p]),
            pltpu.make_async_copy(first_sent.at[p, 0], edges.at[p, upper], in_sems.at[1, p]),
            pltpu.make_async_copy(second_sent.at[p, 0], edges.at[p, 1 - upper], in_sems.at[2, p]),
        )

    def output(p):
        return pltpu.make_async_copy(kept.at[p], out.at[p], out_sems.at[p])

    for p in range(pairs):
        for copy in inputs(p):
            copy.start()
    late = [
        pltpu.make_async_copy(all_ids, ids, late_sems.at[0]),
        pltpu.make_async_copy(all_occ, occ, late_sems.at[1]),
        pltpu.make_async_copy(all_vir, vir, late_sems.at[2]),
    ]
    fill_band(band)
    fill_children(spread, 1.0, 1)
    line = lax.broadcasted_iota(jnp.int32, identity.shape, 0)
    identity[...] = jnp.where(line == lax.broadcasted_iota(jnp.int32, identity.shape, 1), 1.0, 0.0).astype(BF16)
    zero_rims(start)
    zero_rims(swept)

    def spread_out(p, carry):
        for part in range(parts):
            table = spread[...]
            at = p * parts + part
            own = dot(coarse[at, :part_rows], table) + dot(coarse[at, part_rows : 2 * part_rows], table)
            beyond = own + dot(coarse[at, 2 * part_rows :], table)
            for at, value in enumerate((beyond[:, :lanes], own[:, :lanes], own[:, lanes:], beyond[:, lanes:])):
                rows = 2 * part * part_rows
                wide[p, at, pl.ds(rows, part_rows, stride=2), :] = value
                wide[p, at, pl.ds(rows + 1, part_rows, stride=2), :] = value
        return carry

    lax.fori_loop(0, pairs, spread_out, 0)

    def one_pair(p, carry):
        for copy in inputs(p):
            copy.wait()

        @pl.when(p == 0)
        def _():
            for copy in late:
                copy.start()

        def halo(edge, index, row):
            rows = slice(row, row + STEP)
            one, two = first[p, index, rows].astype(F32), second[p, index, rows].astype(F32)
            return jnp.where(even == (edge == 1), one, two)

        for row in range(0, rows_y, STEP):
            rows = slice(row, row + STEP)
            for layer in range(slab):
                value = v0[p, layer, rows]
                if layer == 0:
                    value = value + halo(0, 0, row)
                    v0[p, layer, rows] = value
                if layer == slab - 1:
                    value = value + halo(1, 0, row)
                    v0[p, layer, rows] = value
                put(start, layer + 2, row, value + wide[p, 1 + layer // 2, rows])
            near = halo(0, 1, row) + edges[p, 0, rows].astype(F32) + wide[p, 0, rows]
            put(start, 1, row, in_left * near)
            put(start, 0, row, in_left * (halo(0, 2, row) + wide[p, 0, rows]))
            near = halo(1, 1, row) + edges[p, 1, rows].astype(F32) + wide[p, 3, rows]
            put(start, slab + 2, row, in_right * near)
            put(start, slab + 3, row, in_right * (halo(1, 2, row) + wide[p, 3, rows]))

        def sweep(ref, at, row):
            total = stencil(ref, at, row, band[...])
            return W * (total + read(ref, at - 1, row) + read(ref, at + 1, row))

        for row in range(0, rows_y, STEP):
            put(swept, 0, row, in_left * sweep(start, 1, row))
            for layer in range(slab):
                put(swept, layer + 1, row, sweep(start, layer + 2, row))
            put(swept, slab + 1, row, in_right * sweep(start, slab + 2, row))
        for row in range(0, rows_y, STEP):
            rows = slice(row, row + STEP)
            for layer in range(slab):
                kept[p, layer, rows] = (sweep(swept, layer + 1, row) + v0[p, layer, rows]).astype(BF16)
        output(p).start()
        half = lanes // 2
        for layer in range(slab):
            value = dot(identity[...], kept[p, layer], ((1,), (1,))).astype(BF16)
            column = 2 * layer * rows_y
            turned[p, :, column : column + rows_y] = value[:half]
            turned[p, :, column + rows_y : column + 2 * rows_y] = value[half:]
        return carry

    lax.fori_loop(0, pairs, one_pair, 0, unroll=2)
    for copy in late:
        copy.wait()
    half = lanes // 2
    fields = turned[...].reshape(pairs * half, 2 * slab * rows_y)
    count = ids.shape[0] // 2 * pairs
    first_row = lax.axis_index("pair") * pairs
    left = lax.broadcasted_iota(jnp.int32, (rows_y, lanes), 1) < half
    diagonal = lax.broadcasted_iota(jnp.int32, (half, 2 * lanes), 0) == lax.rem(
        lax.broadcasted_iota(jnp.int32, (half, 2 * lanes), 1), half
    )

    def density16(p, layer):
        turn, k = p // pairs, lax.rem(p, pairs)
        i, a = ids[2 * turn, k], ids[2 * turn + 1, k]
        return (occ[i, layer].astype(F32) * vir[a, layer].astype(F32)).astype(BF16)

    def four_rows(turn, carry):
        p = 4 * turn
        pieces = []
        for layer in range(slab):
            upper_row, lower_row = [], []
            for j in (0, 2):
                one, two = density16(p + j, layer), density16(p + j + 1, layer)
                upper_row.append(jnp.where(left, one, pltpu.roll(two, half, 1)))
                lower_row.append(jnp.where(left, pltpu.roll(one, half, 1), two))
            pieces += [jnp.concatenate(upper_row, axis=1), jnp.concatenate(lower_row, axis=1)]
        product = dot(fields, jnp.concatenate(pieces, axis=0))
        row = first_row + p
        row = jnp.where(row >= count, row - count, row) // 2
        for q in range(pairs):
            block = jnp.where(diagonal, product[q * half : (q + 1) * half], 0.0)
            block = jnp.sum(block, axis=0, keepdims=True)
            sums[row, q : q + 1] = block[:, :lanes]
            sums[row + 1, q : q + 1] = block[:, lanes:]
        return carry

    lax.fori_loop(0, count // 4, four_rows, 0, unroll=4)
    scale = 1.0 / float(slab * rows_y * lanes * lax.axis_size("dom"))
    total = scale * sums[...]
    left = lax.broadcasted_iota(jnp.int32, total.shape, 2) < half
    panel[0] = jnp.sum(jnp.where(left, total, 0.0), axis=2)
    panel[1] = jnp.sum(jnp.where(left, 0.0, total), axis=2)
    for p in range(pairs):
        output(p).wait()


def sine_table(length):
    steps = np.arange(length, dtype=np.float64) + 1.0
    return math.sqrt(2.0 / (length + 1)) * np.sin(np.pi * steps[:, None] * steps[None, :] / (length + 1))


def eigenvalues(length):
    return 2.0 - 2.0 * np.cos(np.pi * (np.arange(length, dtype=np.float64) + 1.0) / (length + 1))


def coarse_tables(size_x, size_y, size_z):
    sine_x, sine_z = sine_table(size_x), sine_table(size_z)
    modes = np.einsum("dk,zl->dzkl", sine_x, np.repeat(sine_z, 2, axis=0))
    modes = np.repeat(modes[:, None], 2, axis=1).reshape(size_x * 4 * size_z, size_x * size_z)
    high = modes.astype(BF16)
    low = (modes - high.astype(np.float64)).astype(BF16)
    total = eigenvalues(size_y)[:, None, None] + eigenvalues(size_x)[None, :, None] + eigenvalues(size_z)[None, None, :]
    inverse = (0.5 / total).reshape(size_y, size_x * size_z)
    return jnp.asarray(np.stack([high, low])), jnp.asarray(sine_table(size_y), F32), jnp.asarray(inverse, F32)


def shards(occupied, virtual, pair_ids):
    orbitals, slab, rows_y, lanes = occupied.shape
    pairs = pair_ids.shape[0]
    slabs = lax.axis_size("dom")
    parts = slabs // pairs
    half_y = rows_y // 2
    part_rows = half_y // parts
    padded_y = rows_y + 2 * PAD
    ids = pair_ids.T

    hbm, vmem = pl.BlockSpec(memory_space=pltpu.HBM), pl.BlockSpec(memory_space=pltpu.VMEM)
    anywhere = pl.BlockSpec(memory_space=pl.ANY)
    in_hbm = lambda x: pltpu.with_memory_space_constraint(x, pltpu.HBM)
    halo = (pairs, 3, rows_y, lanes)
    own = (pairs, slab, rows_y, lanes)
    share = (pairs, parts, 3, part_rows, lanes)
    shares, first, second, v0 = pl.pallas_call(
        source_kernel,
        in_specs=[hbm, hbm, hbm],
        out_specs=[hbm] * 4,
        out_shape=[
            pltpu.HBM(share, BF16),
            pltpu.HBM(halo, BF16),
            pltpu.HBM(halo, BF16),
            pltpu.HBM(own, F32),
        ],
        scratch_shapes=[
            pltpu.SMEM(ids.shape, jnp.int32),
            pltpu.VMEM(own, BF16),
            pltpu.VMEM(own, BF16),
            pltpu.VMEM((2 * lanes, lanes), BF16),
            pltpu.VMEM((2 * lanes, lanes), BF16),
            pltpu.VMEM((slab, padded_y, lanes), F32),
            pltpu.VMEM((slab + 2, padded_y, lanes), F32),
            pltpu.VMEM((2, rows_y, lanes), F32),
            pltpu.VMEM(own, F32),
            pltpu.VMEM((slab // 2 + 2, rows_y + PAD, lanes), F32),
            pltpu.VMEM((pairs, 2, 3, rows_y, lanes), BF16),
            pltpu.VMEM(share, BF16),
            pltpu.SemaphoreType.DMA,
            pltpu.SemaphoreType.DMA((2, pairs)),
            pltpu.SemaphoreType.DMA((4, pairs)),
        ],
        compiler_params=pltpu.CompilerParams(vmem_limit_bytes=32 * MIB),
        name="source",
    )(in_hbm(ids), in_hbm(occupied), in_hbm(virtual))

    inside = [(i, i ^ 1) for i in range(slabs)]
    outside = [(i, i + 1) for i in range(1, slabs - 1, 2)]
    outside = outside + [(j, i) for i, j in outside]
    first_halo = lax.ppermute(first, "dom", inside)
    second_halo = lax.ppermute(second, "dom", outside)
    received = lax.all_to_all(shares.reshape(slabs, 3, part_rows, lanes), "dom", 0, 0)
    views = [received]
    for turn in range(1, parts):
        perm = [(g * parts + (h + turn) % parts, g * parts + h) for g in range(slabs // parts) for h in range(parts)]
        views.append(lax.ppermute(received, "dom", perm))
    tables = coarse_tables(slabs, half_y // 2, lanes // 4)
    padded = pltpu.VMEM((slabs, half_y + 2 * PAD, lanes), F32)
    plain = pltpu.VMEM((slabs, half_y, lanes), F32)
    smoothed = pl.pallas_call(
        middle_kernel,
        in_specs=[vmem] * (parts + 3),
        out_specs=vmem,
        out_shape=jax.ShapeDtypeStruct((slabs, 3 * part_rows, lanes), BF16),
        scratch_shapes=[padded, padded, padded, plain, plain],
        compiler_params=pltpu.CompilerParams(vmem_limit_bytes=32 * MIB),
        name="middle",
    )(*views, *tables)
    groups = lax.axis_size("pair")
    late_ids, smoothed = lax.optimization_barrier((ids, smoothed))
    turns = [[((g + turn) % groups, g) for g in range(groups)] for turn in range(1, groups)]
    all_ids = jnp.concatenate([ids] + [lax.ppermute(late_ids, "pair", perm) for perm in turns], axis=0)
    returned = lax.all_to_all(smoothed, "dom", 0, 0)

    count = groups * pairs
    potentials, panel = pl.pallas_call(
        final_kernel,
        in_specs=[anywhere] + [hbm] * 5 + [vmem] * 3,
        out_specs=[hbm, vmem],
        out_shape=[pltpu.HBM(own, BF16), jax.ShapeDtypeStruct((2, count // 2, pairs), F32)],
        scratch_shapes=[
            pltpu.VMEM(own, F32),
            pltpu.VMEM((pairs, 2, rows_y, lanes), BF16),
            pltpu.VMEM((2 * lanes, lanes), BF16),
            pltpu.VMEM((lanes, 2 * lanes), BF16),
            pltpu.VMEM((lanes, lanes), BF16),
            pltpu.VMEM((pairs, 4, rows_y + PAD, lanes), F32),
            pltpu.VMEM((slab + 4, padded_y, lanes), F32),
            pltpu.VMEM((slab + 2, padded_y, lanes), F32),
            pltpu.VMEM(own, BF16),
            pltpu.VMEM(occupied.shape, BF16),
            pltpu.VMEM(virtual.shape, BF16),
            pltpu.SMEM(all_ids.shape, jnp.int32),
            pltpu.VMEM((pairs, lanes // 2, 2 * slab * rows_y), BF16),
            pltpu.VMEM((count // 2, pairs, lanes), F32),
            pltpu.SemaphoreType.DMA((3, pairs)),
            pltpu.SemaphoreType.DMA((pairs,)),
            pltpu.SemaphoreType.DMA((3,)),
        ],
        compiler_params=pltpu.CompilerParams(vmem_limit_bytes=24 * MIB),
        name="final",
    )(all_ids, *[in_hbm(x) for x in (occupied, virtual, v0, first, second)], returned, first_halo, second_halo)
    panel = jnp.swapaxes(panel, 0, 1).reshape(slabs, count // slabs, pairs)
    return potentials, jnp.sum(lax.all_to_all(panel, "dom", 0, 0), axis=0)


def solution(mesh):
    placed = (P(None, "dom", None, None), P(None, "dom", None, None), P("pair", None))
    return jax.shard_map(
        shards,
        mesh=mesh,
        in_specs=placed,
        out_specs=(P("pair", "dom", None, None), P("dom", "pair")),
        check_vma=False,
    )
```
